32 devices in a mesh: grp: 2 (over y), qb: 16 (over z, x, core).
Axes of the slice: x: 2, y: 2, z: 4, core: 2. Of those that a mesh axis runs over, the one named last changes fastest.
Arguments:
- query_rows: bfloat16 [49152, 128], P(('grp', 'qb')), parts along dimension 0, may hold values from -6 to 6
- key_rows: bfloat16 [49152, 128], P(('grp', 'qb')), parts along dimension 0, may hold values from -6 to 6
- value_rows: bfloat16 [49152, 128], P(('grp', 'qb')), parts along dimension 0, may hold values from -6 to 6
- output_rows: bfloat16 [49152, 128], P(('grp', 'qb')), parts along dimension 0, may hold values from -4 to 4
- output_grad: bfloat16 [49152, 128], P(('grp', 'qb')), parts along dimension 0, may hold values from -192 to 192
- logsumexp: float32 [49152], P(('grp', 'qb')), parts along dimension 0, may hold values from 6.8 to 7.8
- layout: int32 [384, 3], P('grp'), parts along dimension 0, may hold values from 0 to 191, as said below
Outputs:
- query_grad: bfloat16 [49152, 128], P(('grp', 'qb')), parts along dimension 0
- key_grad: bfloat16 [49152, 128], P(('grp', 'qb')), parts along dimension 0
- value_grad: bfloat16 [49152, 128], P(('grp', 'qb')), parts along dimension 0
The draws below stay inside these ranges and needn't reach their ends.
There are 2 independent parts, one for each index of `grp`. The reference program is written for one: setup_inputs(seed, part) draws one part's arguments, and reference() takes and returns one part's arrays. A program takes and returns all parts, laid end to end along the dimension named above; each array names one. Nothing has to cross between parts.
Inputs may be any that keep to these rules, and one draw needn't show every extreme that they name: `layout`: blocks j * 12 to (j + 1) * 12 - 1 are those of device j. Among the rows of one device's 12 query blocks, at most 4 entries name blocks of any one device, and exactly 4 name blocks of some device.
All inputs are finite; a program needn't handle non-finite values.
Results may differ from the reference program's by a relative error of at most 0.0059.
Values may be sent and summed in bfloat16 or wider, within the bound.
No kernel may reach another device: no remote copies, remote signals or barrier semaphores. Data moves between devices by JAX's collectives and lax.ppermute only.
A program may use at most 192 MiB of HBM per device.

```python
import jax
import jax.numpy as jnp
from jax import lax

QB_DEV = 12
BLK = 128
DH = 128
HEADS = 1
GLOB = 2
RAND = 3
TOKENS = 24576
CAP = 4
N_QB = 16


def draw_layout(key, part):
    key = jax.random.fold_in(key, 11)
    score_key, favor_key, order_key, local_key = jax.random.split(key, 4)
    requests = QB_DEV * RAND
    slot_total = N_QB * CAP
    owner_of = jnp.arange(slot_total, dtype=jnp.int32) // CAP
    scores = jax.random.randint(score_key, (N_QB, slot_total), 0, 2 ** 20, dtype=jnp.int32) * slot_total + jnp.arange(slot_total, dtype=jnp.int32)
    favored = jax.random.randint(favor_key, (N_QB,), 0, N_QB, dtype=jnp.int32)
    scores = scores - (owner_of[None, :] == favored[:, None]).astype(jnp.int32) * 2 ** 30
    picked = jnp.argsort(scores, axis=1)[:, :requests]
    owners = owner_of[picked]
    mixing = jax.random.randint(order_key, (N_QB, requests), 0, 2 ** 20, dtype=jnp.int32) * requests + jnp.arange(requests, dtype=jnp.int32)
    shuffle = jnp.argsort(mixing, axis=1)
    owners = jnp.take_along_axis(owners, shuffle, 1).astype(jnp.int32)
    inside = jax.random.randint(local_key, (N_QB, requests), 0, QB_DEV, dtype=jnp.int32)
    return (owners * QB_DEV + inside).reshape(N_QB * QB_DEV, RAND).astype(jnp.int32)


def steps_of(own_key, dims, pieces, low, largest):
    loudness, own = 1.0, jax.random.fold_in(own_key, 6)
    for axis_at, shards_of in pieces:
        draws = jnp.exp(jax.random.uniform(jax.random.fold_in(own, axis_at), (shards_of,), jnp.float32, low / len(pieces), largest / len(pieces)))
        loudness = loudness * jnp.repeat(draws, dims[axis_at] // shards_of).reshape([-1 if axis == axis_at else 1 for axis in range(len(dims))])
    return loudness


def normal_values(rng, extent, spread, limit, shards=(), kind=jnp.bfloat16):
    entries = spread * jax.random.normal(rng, extent, jnp.float32)
    if shards:
        entries = entries * steps_of(rng, extent, shards, -0.22, 0.18)
    return jnp.clip(entries, -limit, limit).astype(kind)


def setup_inputs(seed: int = 0, part: int = 0) -> dict:
    seeds = jax.random.split(jax.random.key(seed), 8)
    own_keys = jax.random.split(jax.random.fold_in(seeds[7], part), 8)
    query_rows = normal_values(own_keys[0], (TOKENS, HEADS * DH), 1.0, 6.0, ((0, 16),))
    key_rows = normal_values(own_keys[1], (TOKENS, HEADS * DH), 1.0, 6.0, ((0, 16),))
    value_rows = normal_values(own_keys[2], (TOKENS, HEADS * DH), 1.0, 6.0, ((0, 16),))
    output_rows = normal_values(own_keys[3], (TOKENS, HEADS * DH), 0.3, 4.0, ((0, 16),))
    output_grad = normal_values(own_keys[4], (TOKENS, HEADS * DH), 32.0, 192.0, ((0, 16),))
    logsumexp = jnp.clip(6.8 + 1.0 * jax.random.uniform(own_keys[5], (TOKENS,), jnp.float32) ** steps_of(own_keys[5], (TOKENS,), ((0, 16),), -0.2, 0.2), 6.8, 7.8)
    layout = draw_layout(jax.random.fold_in(jax.random.fold_in(seeds[7], part), 71), part)
    return {"query_rows": query_rows, "key_rows": key_rows, "value_rows": value_rows, "output_rows": output_rows, "output_grad": output_grad, "logsumexp": logsumexp, "layout": layout}


def block_grads(query_blk, key_blk, value_blk, grad_blk, lse_blk, delta_blk, masking, scaling):
    scores = jnp.einsum("nqd,nkd->nqk", query_blk.astype(jnp.float32), key_blk.astype(jnp.float32)) * scaling
    probability = jnp.exp(scores - lse_blk[:, :, None]) * masking[:, None, None]
    dweights = jnp.einsum("nqd,nkd->nqk", grad_blk.astype(jnp.float32), value_blk.astype(jnp.float32))
    score_grad = probability * (dweights - delta_blk[:, :, None])
    prob_low = probability.astype(jnp.bfloat16).astype(jnp.float32)
    score_low = score_grad.astype(jnp.bfloat16).astype(jnp.float32)
    query_part = jnp.einsum("nqk,nkd->nqd", score_low, key_blk.astype(jnp.float32)) * scaling
    key_part = jnp.einsum("nqk,nqd->nkd", score_low, query_blk.astype(jnp.float32)) * scaling
    value_part = jnp.einsum("nqk,nqd->nkd", prob_low, grad_blk.astype(jnp.float32))
    return query_part, key_part, value_part


def reference(query_rows, key_rows, value_rows, output_rows, output_grad, logsumexp, layout):
    width = query_rows.shape[1]
    scaling = width ** -0.5
    total = TOKENS // BLK
    query_blocks = query_rows.reshape(total, BLK, width)
    key_blocks = key_rows.reshape(total, BLK, width)
    value_blocks = value_rows.reshape(total, BLK, width)
    grad_blocks = output_grad.reshape(total, BLK, width)
    deltas = jnp.sum(output_grad.astype(jnp.float32) * output_rows.astype(jnp.float32), -1).reshape(total, BLK)
    lse_rows = logsumexp.reshape(total, BLK)
    blocks = jnp.arange(total, dtype=jnp.int32)
    all_ones = jnp.ones((total,), jnp.float32)
    columns = [blocks - 1, blocks, blocks + 1]
    columns = columns + [jnp.full((total,), anchor, jnp.int32) for anchor in range(GLOB)]
    columns = columns + [layout[:, column].astype(jnp.int32) for column in range(RAND)]
    weights = [(blocks > 0).astype(jnp.float32), all_ones, (blocks < total - 1).astype(jnp.float32)]
    weights = weights + [all_ones for column in range(GLOB + RAND)]
    targets = jnp.clip(jnp.stack(columns), 0, total - 1).astype(jnp.int32)
    maskings = jnp.stack(weights)
    flags = jnp.array([0.0] * (3 + GLOB) + [1.0] * RAND, jnp.float32)

    def visit(carry, item):
        query_acc, key_acc, value_acc = carry
        target, masking, flag = item
        query_part, key_part, value_part = block_grads(query_blocks, key_blocks[target], value_blocks[target], grad_blocks, lse_rows, deltas, masking, scaling)
        rounded = query_part.astype(jnp.bfloat16).astype(jnp.float32)
        query_part = jnp.where(flag > 0.5, rounded, query_part)
        return (query_acc + query_part, key_acc.at[target].add(key_part), value_acc.at[target].add(value_part)), None

    zeros = jnp.zeros((total, BLK, width), jnp.float32)
    (query_acc, key_acc, value_acc), unused = lax.scan(visit, (zeros, zeros, zeros), (targets, maskings, flags))
    return (query_acc.reshape(TOKENS, width).astype(jnp.bfloat16), key_acc.reshape(TOKENS, width).astype(jnp.bfloat16), value_acc.reshape(TOKENS, width).astype(jnp.bfloat16))
```

```python
import functools

import jax
import jax.numpy as jnp
from jax import lax
from jax.experimental import pallas as pl
from jax.experimental.pallas import tpu as pltpu
from jax.sharding import PartitionSpec as P

BLK = 128
GLOB = 2
STAT = 16
PAIRS = 2
FAR = 1e30


def pieces(row):
    high = row.astype(jnp.bfloat16)
    rest = row - high.astype(jnp.float32)
    middle = rest.astype(jnp.bfloat16)
    low = (rest - middle.astype(jnp.float32)).astype(jnp.bfloat16)
    return [high.astype(jnp.float32), middle.astype(jnp.float32), low.astype(jnp.float32)]


def pack_kernel(query, grad, output, key, value, lse, unit, keyval):
    count = unit.shape[0]
    width = unit.shape[2]

    def block(b, carry):
        rows = pl.ds(pl.multiple_of(b * BLK, BLK), BLK)
        grads = grad[rows, :]
        unit[b, 0:BLK] = query[rows, :]
        unit[b, BLK : 2 * BLK] = grads
        keyval[b, 0] = key[rows, :]
        keyval[b, 1] = value[rows, :]
        product = grads.astype(jnp.float32) * output[rows, :].astype(jnp.float32)
        delta = jnp.sum(product.T, axis=0, keepdims=True)
        stats = pieces(lse[pl.ds(b, 1), :]) + pieces(delta)
        stats.append(jnp.zeros((STAT - len(stats), width), jnp.float32))
        unit[b, 2 * BLK :] = jnp.concatenate(stats, 0).astype(jnp.bfloat16)
        return carry

    lax.fori_loop(0, count, block, 0)


def pack(query, grad, output, key, value, lse):
    count, width = (query.shape[0] // BLK, query.shape[1])
    return pl.pallas_call(
        pack_kernel,
        out_shape=(
            jax.ShapeDtypeStruct((count, 2 * BLK + STAT, width), jnp.bfloat16),
            jax.ShapeDtypeStruct((count, 2, BLK, width), jnp.bfloat16),
        ),
        name="pack",
    )(query, grad, output, key, value, lse)


def pair_grads(keys, values, queries, grads, lse, delta, scaling, mask=None):
    scores = lax.dot_general(
        keys, queries, (((1,), (1,)), ((), ())), preferred_element_type=jnp.float32
    )
    probability = jnp.exp(scores * scaling - lse)
    if mask is not None:
        probability = jnp.where(mask, probability, 0.0)
    dweights = lax.dot_general(
        values, grads, (((1,), (1,)), ((), ())), preferred_element_type=jnp.float32
    )
    score_low = (probability * (dweights - delta)).astype(jnp.bfloat16)
    prob_low = probability.astype(jnp.bfloat16)
    value_part = jnp.dot(prob_low, grads, preferred_element_type=jnp.float32)
    key_part = jnp.dot(score_low, queries, preferred_element_type=jnp.float32)
    query_part = lax.dot_general(
        score_low, keys, (((0,), (0,)), ((), ())), preferred_element_type=jnp.float32
    )
    return query_part, key_part, value_part


def step_kernel(plan, me_ref, layout_ref, *refs):
    offsets, span, fanout, scaling, first, last = plan
    visits = len(offsets)
    refs = list(refs)
    units = [refs.pop(0) for _ in range(visits)]
    keyvals = [refs.pop(0) for _ in range(span)]
    acc_in = None if first else refs.pop(0)
    dq_out = [refs.pop(0) for _ in range(visits)]
    if last:
        send_out, keep_out = (refs.pop(0), refs.pop(0))
    else:
        acc_out = refs.pop(0)
    unit_s, kv_s, acc_s, dq_s, who, whom, far, sems, acc_sem = refs
    count = unit_s.shape[1]
    width = unit_s.shape[3]
    held = span * count
    me = me_ref[0]
    shards = me_ref[1]
    seat = lax.rem(me, span)
    row = lax.div(me, span)
    low = row * held

    loads = []
    for m in range(span):
        other = jnp.bitwise_xor(seat, m)
        loads.append(
            pltpu.make_async_copy(
                keyvals[m], kv_s.at[pl.ds(other * count, count)], sems.at[visits + m]
            )
        )
    for v in range(visits):
        loads.append(pltpu.make_async_copy(units[v], unit_s.at[v], sems.at[v]))
    for load in loads:
        load.start()
    if not first:
        load = pltpu.make_async_copy(acc_in, acc_s, acc_sem)
        load.start()
        loads.append(load)
    else:

        def clear(b, carry):
            acc_s[b] = jnp.zeros(acc_s.shape[1:], jnp.float32)
            return carry

        lax.fori_loop(0, held, clear, 0)

    def clear_dq(b, carry):
        for v in range(visits):
            dq_s[v, b] = jnp.zeros(dq_s.shape[2:], jnp.float32)
        return carry

    lax.fori_loop(0, count, clear_dq, 0)
    for load in loads:
        load.wait()

    def stats(v, q):
        rows = unit_s[v, q, 2 * BLK :].astype(jnp.float32)
        lse = rows[0:1] + rows[1:2] + rows[2:3]
        delta = rows[3:4] + rows[4:5] + rows[5:6]
        return lse, delta

    def window(v):
        def step(q, carry):
            at = seat * count + q
            start = jnp.clip(at - 1, 0, held - 3)
            keys = kv_s[pl.ds(start, 3), 0].reshape(3 * BLK, width)
            values = kv_s[pl.ds(start, 3), 1].reshape(3 * BLK, width)
            lse, delta = stats(v, q)
            block = lax.broadcasted_iota(jnp.int32, (3 * BLK, BLK), 0) // BLK + start - at
            query_part, key_part, value_part = pair_grads(
                keys,
                values,
                unit_s[v, q, 0:BLK],
                unit_s[v, q, BLK : 2 * BLK],
                lse,
                delta,
                scaling,
                (block >= -1) & (block <= 1),
            )
            dq_s[v, q] += query_part
            acc_s[pl.ds(start, 3), 0] += key_part.reshape(3, BLK, width)
            acc_s[pl.ds(start, 3), 1] += value_part.reshape(3, BLK, width)
            return carry

        lax.fori_loop(0, count, step, 0)

    def anchors(v):
        chunk = 2 if count % 2 == 0 else 1

        def step(c, carry):
            blocks = pl.ds(c * chunk, chunk)
            queries = unit_s[v, blocks, 0:BLK].reshape(chunk * BLK, width)
            grads = unit_s[v, blocks, BLK : 2 * BLK].reshape(chunk * BLK, width)
            lines = [stats(v, c * chunk + k) for k in range(chunk)]
            lse = jnp.concatenate([line[0] for line in lines], 1)
            delta = jnp.concatenate([line[1] for line in lines], 1)
            query_part, key_part, value_part = pair_grads(
                kv_s[0:GLOB, 0].reshape(GLOB * BLK, width),
                kv_s[0:GLOB, 1].reshape(GLOB * BLK, width),
                queries,
                grads,
                lse,
                delta,
                scaling,
            )
            dq_s[v, blocks] += query_part.reshape(chunk, BLK, width)
            acc_s[0:GLOB, 0] += key_part.reshape(GLOB, BLK, width)
            acc_s[0:GLOB, 1] += value_part.reshape(GLOB, BLK, width)
            return carry

        lax.fori_loop(0, count // chunk, step, 0)

    def scattered(v, guest, near):
        def note(at, q, target):
            local = target - low
            hit = (local >= 0) & (local < held)

            @pl.when(hit)
            def _():
                who[at] = q
                whom[at] = local
                far[at] = 0.0

            return at + hit.astype(jnp.int32)

        def gather(q, at):
            block = guest * count + q
            for r in range(fanout):
                at = note(at, q, layout_ref[block * fanout + r])
            if near:
                at = note(at, q, block - 1)
                at = note(at, q, block + 1)
            return at

        found = lax.fori_loop(0, count, gather, 0)
        for k in range(PAIRS - 1):
            who[found + k] = 0
            whom[found + k] = 0
            far[found + k] = FAR

        def step(g, carry):
            places, parts = ([], [])
            for k in range(PAIRS):
                at = g * PAIRS + k
                q, j = (who[at], whom[at])
                lse, delta = stats(v, q)
                places.append((q, j))
                parts.append(
                    pair_grads(
                        kv_s[j, 0],
                        kv_s[j, 1],
                        unit_s[v, q, 0:BLK],
                        unit_s[v, q, BLK : 2 * BLK],
                        lse + far[at],
                        delta,
                        scaling,
                    )
                )
            for (q, j), (query_part, key_part, value_part) in zip(places, parts):
                dq_s[v, q] += query_part
                acc_s[j, 0] += key_part
                acc_s[j, 1] += value_part
            return carry

        lax.fori_loop(0, (found + PAIRS - 1) // PAIRS, step, 0)

    for v, offset in enumerate(offsets):
        guest = me + offset * span
        if offset == 0:
            window(v)

        @pl.when((guest >= 0) & (guest < shards))
        def _(v=v, offset=offset, guest=guest):
            @pl.when(row == 0)
            def _():
                anchors(v)

            scattered(v, guest, abs(offset) == 1)

    def finish_dq(q, carry):
        for v in range(visits):
            dq_out[v][q] = (dq_s[v, q] * scaling).astype(dq_out[v].dtype)
        return carry

    lax.fori_loop(0, count, finish_dq, 0)
    if last:

        def finish(b, carry):
            for k in range(span // 2):
                mine = jnp.bitwise_xor(seat, 2 * k) * count + b
                theirs = jnp.bitwise_xor(seat, 2 * k + 1) * count + b
                keep_out[k, b, 0] = acc_s[mine, 0] * scaling
                keep_out[k, b, 1] = acc_s[mine, 1]
                send_out[k, b, 0] = (acc_s[theirs, 0] * scaling).astype(jnp.bfloat16)
                send_out[k, b, 1] = acc_s[theirs, 1].astype(jnp.bfloat16)
            return carry

        lax.fori_loop(0, count, finish, 0)
    else:
        store = pltpu.make_async_copy(acc_s, acc_out, acc_sem)
        store.start()
        store.wait()


def visit(me, layout, units, offsets, keyvals, acc, last, fanout):
    span = len(keyvals)
    visits = len(units)
    count, _, width = units[0].shape
    first = acc is None
    scaling = width ** (-0.5)
    plan = (offsets, span, fanout, scaling, first, last)
    held = span * count
    smem = pl.BlockSpec(memory_space=pltpu.SMEM)
    hbm = pl.BlockSpec(memory_space=pl.ANY)
    vmem = pl.BlockSpec(memory_space=pltpu.VMEM)
    kinds = [jnp.float32 if offset == 0 else jnp.bfloat16 for offset in offsets]
    outs = [jax.ShapeDtypeStruct((count, BLK, width), kind) for kind in kinds]
    out_specs = [vmem] * visits
    if last:
        outs.append(jax.ShapeDtypeStruct((span // 2, count, 2, BLK, width), jnp.bfloat16))
        outs.append(jax.ShapeDtypeStruct((span // 2, count, 2, BLK, width), jnp.float32))
        out_specs += [vmem, vmem]
    else:
        outs.append(jax.ShapeDtypeStruct((held, 2, BLK, width), jnp.float32))
        out_specs.append(hbm)
    entries = count * (fanout + 2) + PAIRS
    pairs = visits * count * 2 + (3 * count if first else 0)
    return pl.pallas_call(
        functools.partial(step_kernel, plan),
        out_shape=outs,
        in_specs=[smem, smem] + [hbm] * (visits + span + (0 if first else 1)),
        out_specs=out_specs,
        scratch_shapes=[
            pltpu.VMEM((visits,) + units[0].shape, jnp.bfloat16),
            pltpu.VMEM((held, 2, BLK, width), jnp.bfloat16),
            pltpu.VMEM((held, 2, BLK, width), jnp.float32),
            pltpu.VMEM((visits, count, BLK, width), jnp.float32),
            pltpu.SMEM((entries,), jnp.int32),
            pltpu.SMEM((entries,), jnp.int32),
            pltpu.SMEM((entries,), jnp.float32),
            pltpu.SemaphoreType.DMA((visits + span,)),
            pltpu.SemaphoreType.DMA(()),
        ],
        compiler_params=pltpu.CompilerParams(vmem_limit_bytes=40 * 2**20),
        cost_estimate=pl.CostEstimate(
            flops=pairs * 10 * BLK * BLK * width,
            bytes_accessed=16 * 2**20,
            transcendentals=pairs * BLK * BLK,
        ),
        name="visit",
    )(me, layout, *units, *keyvals, *([] if first else [acc]))


def body(query_rows, key_rows, value_rows, output_rows, output_grad, logsumexp, layout):
    shards = lax.axis_size("qb")
    myself = lax.axis_index("qb")
    width = query_rows.shape[1]
    count = query_rows.shape[0] // BLK
    fanout = layout.shape[1]
    span = 4
    while shards // span > 16:
        span = span * 2
    planes = shards // span

    def send(array, pairs):
        return lax.ppermute(array, "qb", pairs)

    def swap(array, bit):
        return send(array, [(i, i ^ bit) for i in range(shards)])

    def shift(array, planes_away, low, high):
        return send(
            array,
            [
                (p * span + e, (p + planes_away) * span + e)
                for p in range(low, high)
                for e in range(span)
            ],
        )

    unit, keyval = pack(
        query_rows, output_grad, output_rows, key_rows, value_rows, logsumexp.reshape(count, BLK)
    )
    keyvals = {0: keyval}
    bit = span // 2
    while bit:
        for m in list(keyvals):
            keyvals[m | bit] = swap(keyvals[m], bit)
        bit = bit // 2
    keyvals = [keyvals[m] for m in range(span)]
    me = jnp.stack([myself, jnp.int32(shards)]).astype(jnp.int32)
    entries = layout.reshape(-1)

    up, down = (unit, unit)
    ups, downs = ([], [])
    for s in range(1, planes):
        up = shift(up, 1, s - 1, planes - 1)
        down = shift(down, -1, 1, planes - s + 1)
        ups.append(up)
        downs.append(down)

    acc = None
    up_parts, down_parts = ([], [])
    for s in range(1, planes):
        guests, offsets = ([ups[s - 1], downs[s - 1]], [-s, s])
        if s == 1:
            guests, offsets = ([unit] + guests, [0] + offsets)
        last = s == planes - 1
        outs = list(visit(me, entries, guests, tuple(offsets), keyvals, acc, last, fanout))
        if s == 1:
            query_acc = outs.pop(0)
        up_parts.append(outs.pop(0))
        down_parts.append(outs.pop(0))
        if last:
            sent, kept = outs
        else:
            acc = outs[0]

    def merge(one, two):
        return (one.astype(jnp.float32) + two.astype(jnp.float32)).astype(jnp.bfloat16)

    far = planes - 1
    query_acc = query_acc + shift(up_parts[-1], -far, far, planes).astype(jnp.float32)
    query_acc = query_acc + shift(down_parts[-1], far, 0, 1).astype(jnp.float32)
    up_back, down_back = (None, None)
    for s in range(planes - 2, 0, -1):
        up_back = up_parts[s - 1] if up_back is None else merge(up_parts[s - 1], up_back)
        down_back = down_parts[s - 1] if down_back is None else merge(down_parts[s - 1], down_back)
        up_back = shift(up_back, -1, s, planes)
        down_back = shift(down_back, 1, 0, planes - s)
    if up_back is not None:
        query_acc = query_acc + up_back.astype(jnp.float32) + down_back.astype(jnp.float32)

    bit = 1
    while True:
        kept = kept + swap(sent, bit).astype(jnp.float32)
        bit = bit * 2
        if bit == span:
            break
        halves = kept.reshape((kept.shape[0] // 2, 2) + kept.shape[1:])
        kept = halves[:, 0]
        sent = halves[:, 1].astype(jnp.bfloat16)
    owned = kept[0]
    query_grad = query_acc.reshape(count * BLK, width).astype(jnp.bfloat16)
    key_grad = owned[:, 0].reshape(count * BLK, width).astype(jnp.bfloat16)
    value_grad = owned[:, 1].reshape(count * BLK, width).astype(jnp.bfloat16)
    return (query_grad, key_grad, value_grad)


def solution(mesh):
    in_specs = (
        P(("grp", "qb"), None),
        P(("grp", "qb"), None),
        P(("grp", "qb"), None),
        P(("grp", "qb"), None),
        P(("grp", "qb"), None),
        P(("grp", "qb")),
        P("grp", None),
    )
    out_specs = (P(("grp", "qb"), None), P(("grp", "qb"), None), P(("grp", "qb"), None))
    return jax.shard_map(body, mesh=mesh, in_specs=in_specs, out_specs=out_specs, check_vma=False)
```

```python
import functools

import jax
import jax.numpy as jnp
from jax import lax
from jax.experimental import pallas as pl
from jax.experimental.pallas import tpu as pltpu
from jax.sharding import PartitionSpec as P

BLK = 128
GLOB = 2
TILE = 16
PAIRS = 3
FAR = 1e30
COST = 0
LIMIT = 24 * 2**20


def pieces(row):
    high = row.astype(jnp.bfloat16)
    rest = row - high.astype(jnp.float32)
    middle = rest.astype(jnp.bfloat16)
    low = (rest - middle.astype(jnp.float32)).astype(jnp.bfloat16)
    return [high.astype(jnp.float32), middle.astype(jnp.float32), low.astype(jnp.float32)]


def stat_rows(count):
    return -(-count // TILE) * TILE


def pack_kernel(query, grad, output, key, value, lse, unit, keyval, delta_s):
    count, width = lse.shape
    rows = stat_rows(count)
    group = 4 if count % 4 == 0 else 1
    ones = jnp.ones((TILE, width), jnp.bfloat16)

    def total(part):
        return lax.dot_general(
            ones, part, (((1,), (1,)), ((), ())), preferred_element_type=jnp.float32
        )

    def step(g, carry):
        highs, lows = ([], [])
        for k in range(group):
            at = pl.ds(pl.multiple_of((g * group + k) * BLK, BLK), BLK)
            after = pl.ds(pl.multiple_of((count + g * group + k) * BLK, BLK), BLK)
            grads = grad[at, :]
            unit[at, :] = query[at, :]
            unit[after, :] = grads
            keyval[at, :] = key[at, :]
            keyval[after, :] = value[at, :]
            product = grads.astype(jnp.float32) * output[at, :].astype(jnp.float32)
            highs.append(product.astype(jnp.bfloat16))
            lows.append((product - highs[-1].astype(jnp.float32)).astype(jnp.bfloat16))
        sums = [total(high) + total(low) for high, low in zip(highs, lows)]
        for k in range(group):
            delta_s[pl.ds(g * group + k, 1), :] = sums[k][0:1]
        return carry

    delta_s[...] = jnp.zeros(delta_s.shape, jnp.float32)
    lax.fori_loop(0, count // group, step, 0)
    lines = lse[...]
    if rows > count:
        lines = jnp.concatenate([lines, jnp.zeros((rows - count, width), jnp.float32)], 0)
    stats = pieces(lines) + pieces(delta_s[...])
    unit[2 * count * BLK :, :] = jnp.concatenate(stats, 0).astype(jnp.bfloat16)


def pack(query, grad, output, key, value, lse):
    count, width = lse.shape
    rows = stat_rows(count)
    return pl.pallas_call(
        pack_kernel,
        out_shape=(
            jax.ShapeDtypeStruct((2 * count * BLK + 6 * rows, width), jnp.bfloat16),
            jax.ShapeDtypeStruct((2 * count * BLK, width), jnp.bfloat16),
        ),
        scratch_shapes=[pltpu.VMEM((rows, width), jnp.float32)],
        name="pack",
    )(query, grad, output, key, value, lse)


def pair_grads(pairs, scaling):
    def outer(one, two):
        return lax.dot_general(
            one, two, (((1,), (1,)), ((), ())), preferred_element_type=jnp.float32
        )

    def inner(one, two):
        return jnp.dot(one, two, preferred_element_type=jnp.float32)

    def flipped(one, two):
        return lax.dot_general(
            one, two, (((0,), (0,)), ((), ())), preferred_element_type=jnp.float32
        )

    scores = [outer(keys, queries) for keys, _, queries, _, _, _, _ in pairs]
    dweights = [outer(values, grads) for _, values, _, grads, _, _, _ in pairs]
    probs = []
    for score, (_, _, _, _, lse, _, mask) in zip(scores, pairs):
        prob = jnp.exp(score * scaling - lse)
        probs.append(prob if mask is None else jnp.where(mask, prob, 0.0))
    prob_lows = [prob.astype(jnp.bfloat16) for prob in probs]
    score_lows = [
        (prob * (dweight - pair[5])).astype(jnp.bfloat16)
        for prob, dweight, pair in zip(probs, dweights, pairs)
    ]
    value_parts = [inner(low, pair[3]) for low, pair in zip(prob_lows, pairs)]
    key_parts = [inner(low, pair[2]) for low, pair in zip(score_lows, pairs)]
    query_parts = [flipped(low, pair[0]) for low, pair in zip(score_lows, pairs)]
    return list(zip(query_parts, key_parts, value_parts))


class Visitor:
    def __init__(self, count, unit, lse, delta, dq, keys, values, acc, layout, lists):
        self.count = count
        self.unit, self.lse, self.delta = (unit, lse, delta)
        self.dq, self.keys, self.values, self.acc = (dq, keys, values, acc)
        self.layout, self.lists = (layout, lists)
        self.width = unit.shape[1]
        self.scaling = self.width ** (-0.5)
        self.held = keys.shape[0] // BLK

    def begin(self):
        count = self.count
        rows = stat_rows(count)
        stats = self.unit[2 * count * BLK :, :].astype(jnp.float32)
        lines = [stats[k * rows : (k + 1) * rows] for k in range(6)]
        self.lse[...] = lines[0] + lines[1] + lines[2]
        self.delta[...] = lines[3] + lines[4] + lines[5]

        def step(q, carry):
            self.dq[q] = jnp.zeros(self.dq.shape[1:], jnp.float32)
            return carry

        lax.fori_loop(0, count, step, 0)

    def rows(self, array, block, blocks=1):
        return array[pl.ds(pl.multiple_of(block * BLK, BLK), blocks * BLK), :]

    def pair(self, q, j, keys=1, shift=0.0, mask=None):
        return (
            self.rows(self.keys, j, keys),
            self.rows(self.values, j, keys),
            self.rows(self.unit, q),
            self.rows(self.unit, self.count + q),
            self.lse[pl.ds(q, 1), :] + shift,
            self.delta[pl.ds(q, 1), :],
            mask,
        )

    def window(self, base):
        count, width = (self.count, self.width)
        chunk = 2 if count % 2 == 0 else 1

        def step(c, carry):
            places, pairs = ([], [])
            for k in range(chunk):
                q = c * chunk + k
                start = jnp.clip(base + q - 1, 0, self.held - 3)
                block = lax.broadcasted_iota(jnp.int32, (3 * BLK, BLK), 0) // BLK
                block = block + start - base - q
                places.append((q, start))
                pairs.append(self.pair(q, start, 3, 0.0, (block >= -1) & (block <= 1)))
            parts = pair_grads(pairs, self.scaling)
            for (q, start), (query_part, key_part, value_part) in zip(places, parts):
                self.dq[q] += query_part
                self.acc[pl.ds(start, 3), 0] += key_part.reshape(3, BLK, width)
                self.acc[pl.ds(start, 3), 1] += value_part.reshape(3, BLK, width)
            return carry

        lax.fori_loop(0, count // chunk, step, 0)

    def anchors(self):
        count, width = (self.count, self.width)
        chunk = 2 if count % 2 == 0 else 1
        turns = 2 if count % (2 * chunk) == 0 else 1

        def step(c, carry):
            places, pairs = ([], [])
            for k in range(turns):
                at = (c * turns + k) * chunk
                places.append(pl.ds(at, chunk))
                pairs.append(
                    (
                        self.keys[0 : GLOB * BLK, :],
                        self.values[0 : GLOB * BLK, :],
                        self.rows(self.unit, at, chunk),
                        self.rows(self.unit, count + at, chunk),
                        jnp.concatenate(
                            [self.lse[pl.ds(at + i, 1), :] for i in range(chunk)], 1
                        ),
                        jnp.concatenate(
                            [self.delta[pl.ds(at + i, 1), :] for i in range(chunk)], 1
                        ),
                        None,
                    )
                )
            parts = pair_grads(pairs, self.scaling)
            for blocks, (query_part, _, _) in zip(places, parts):
                self.dq[blocks] += query_part.reshape(chunk, BLK, width)
            key_part = sum(part[1] for part in parts)
            value_part = sum(part[2] for part in parts)
            self.acc[0:GLOB, 0] += key_part.reshape(GLOB, BLK, width)
            self.acc[0:GLOB, 1] += value_part.reshape(GLOB, BLK, width)
            return carry

        lax.fori_loop(0, count // (chunk * turns), step, 0)

    def scattered(self, guest, low, fanout, near):
        who, whom, far = self.lists
        count = self.count

        def note(at, q, target):
            local = target - low
            hit = (local >= 0) & (local < self.held)
            who[at] = q
            whom[at] = local
            far[at] = 0.0
            return at + hit.astype(jnp.int32)

        def gather(q, at):
            block = guest * count + q
            for r in range(fanout):
                at = note(at, q, self.layout[block * fanout + r])
            return at

        found = lax.fori_loop(0, count, gather, 0)
        if near:
            found = note(found, 0, guest * count - 1)
            found = note(found, count - 1, (guest + 1) * count)
        for k in range(PAIRS - 1):
            who[found + k] = 0
            whom[found + k] = 0
            far[found + k] = FAR

        def step(g, carry):
            places, pairs = ([], [])
            for k in range(PAIRS):
                at = g * PAIRS + k
                places.append((who[at], whom[at]))
                pairs.append(self.pair(who[at], whom[at], 1, far[at]))
            parts = pair_grads(pairs, self.scaling)
            for (q, j), (query_part, key_part, value_part) in zip(places, parts):
                self.dq[q] += query_part
                self.acc[j, 0] += key_part
                self.acc[j, 1] += value_part
            return carry

        lax.fori_loop(0, (found + PAIRS - 1) // PAIRS, step, 0)

    def finish(self, out):
        def step(q, carry):
            out[q] = (self.dq[q] * self.scaling).astype(out.dtype)
            return carry

        lax.fori_loop(0, self.count, step, 0)


def visit_kernel(plan, me_ref, layout, *refs):
    offsets, count, span, fanout, last = plan
    refs = list(refs)
    first = offsets == (0,)
    guests = [refs.pop(0) for _ in offsets]
    me = me_ref[0]
    shards = me_ref[1]
    seat = lax.rem(me, span)
    row = lax.div(me, span)
    low = row * span * count
    if first:
        parts = [refs.pop(0) for _ in range(span)]
        keys, values = (refs.pop(0), refs.pop(0))
    else:
        keys, values = (refs.pop(0), refs.pop(0))
        refs.pop(0)
    acc = refs.pop(0)
    outs = [refs.pop(0) for _ in offsets]
    if last:
        sent, kept = (refs.pop(0), refs.pop(0))
    sums = outs if first else [refs.pop(0) for _ in offsets]
    lse, delta = (refs.pop(0), refs.pop(0))
    lists = refs
    if first:

        def lay(b, carry):
            for m in range(span):
                there = jnp.bitwise_xor(seat, m) * count + b
                acc[there] = jnp.zeros(acc.shape[1:], jnp.float32)
                there = pl.ds(pl.multiple_of(there * BLK, BLK), BLK)
                here = pl.ds(pl.multiple_of(b * BLK, BLK), BLK)
                keys[there, :] = parts[m][here, :]
                here = pl.ds(pl.multiple_of((count + b) * BLK, BLK), BLK)
                values[there, :] = parts[m][here, :]
            return carry

        lax.fori_loop(0, count, lay, 0)

    for v, offset in enumerate(offsets):
        if offset is None:
            guest = jnp.where(row == 0, me + shards - span, me + span - shards)
            present = (row == 0) | (me + span >= shards)
        else:
            guest = me + offset * span
            present = (guest >= 0) & (guest < shards)
        visitor = Visitor(count, guests[v], lse, delta, sums[v], keys, values, acc, layout, lists)
        visitor.begin()
        if offset == 0:
            visitor.window(seat * count)

        @pl.when(present)
        def _(visitor=visitor, near=offset in (-1, 1), guest=guest):
            @pl.when(row == 0)
            def _():
                visitor.anchors()

            visitor.scattered(guest, low, fanout, near)

        visitor.finish(outs[v])

    if last:
        scaling = keys.shape[1] ** (-0.5)

        def finish(b, carry):
            for k in range(span // 2):
                mine = jnp.bitwise_xor(seat, 2 * k) * count + b
                theirs = jnp.bitwise_xor(seat, 2 * k + 1) * count + b
                sent[0, k, b] = (acc[theirs, 0] * scaling).astype(jnp.bfloat16)
                sent[1, k, b] = acc[theirs, 1].astype(jnp.bfloat16)
                kept[0, k, b] = acc[mine, 0] * scaling
                kept[1, k, b] = acc[mine, 1]
            return carry

        lax.fori_loop(0, count, finish, 0)


SMEM = pl.BlockSpec(memory_space=pltpu.SMEM)
VMEM = pl.BlockSpec(memory_space=pltpu.VMEM)


def in_place(array):
    return pltpu.with_memory_space_constraint(array, pltpu.VMEM)


def visit(me, layout, units, offsets, keyvals, acc, last, count, span, fanout):
    first = acc is None
    width = units[0].shape[1]
    held = span * count
    plan = (offsets, count, span, fanout, last)
    operands = units + keyvals
    keys = jax.ShapeDtypeStruct((held * BLK, width), jnp.bfloat16)
    outs = [jax.ShapeDtypeStruct((held, 2, BLK, width), jnp.float32)]
    aliases = {}
    if first:
        outs = [keys, keys] + outs
    else:
        aliases[len(operands) + 2] = 0
        operands = operands + [in_place(acc)]
    kind = jnp.float32 if first else jnp.bfloat16
    outs += [jax.ShapeDtypeStruct((count, BLK, width), kind)] * len(units)
    if last:
        outs.append(jax.ShapeDtypeStruct((2, span // 2, count, BLK, width), jnp.bfloat16))
        outs.append(jax.ShapeDtypeStruct((2, span // 2, count, BLK, width), jnp.float32))
    entries = count * fanout + 2 + PAIRS
    stats = pltpu.VMEM((stat_rows(count), width), jnp.float32)
    return list(
        pl.pallas_call(
            functools.partial(visit_kernel, plan),
            out_shape=outs,
            in_specs=[SMEM, SMEM] + [VMEM] * len(operands),
            out_specs=[VMEM] * len(outs),
            input_output_aliases=aliases,
            scratch_shapes=[pltpu.VMEM((count, BLK, width), jnp.float32)]
            * (0 if first else len(units))
            + [
                stats,
                stats,
                pltpu.SMEM((entries,), jnp.int32),
                pltpu.SMEM((entries,), jnp.int32),
                pltpu.SMEM((entries,), jnp.float32),
            ],
            compiler_params=pltpu.CompilerParams(vmem_limit_bytes=LIMIT),
            cost_estimate=pl.CostEstimate(
                flops=COST * len(offsets) * count * 10 * BLK * BLK * width,
                bytes_accessed=2**20,
                transcendentals=len(offsets) * count * BLK * BLK,
            ),
            name="visit",
        )(me, layout, *operands)
    )


def body(query_rows, key_rows, value_rows, output_rows, output_grad, logsumexp, layout):
    shards = lax.axis_size("qb")
    myself = lax.axis_index("qb")
    width = query_rows.shape[1]
    count = query_rows.shape[0] // BLK
    fanout = layout.shape[1]
    span = 4
    while shards // span > 16:
        span = span * 2
    planes = shards // span

    def send(array, pairs):
        return lax.ppermute(array, "qb", pairs)

    def swap(array, bit):
        return send(array, [(i, i ^ bit) for i in range(shards)])

    def shift(array, planes_away, low, high):
        return send(
            array,
            [
                (p * span + e, (p + planes_away) * span + e)
                for p in range(low, high)
                for e in range(span)
            ],
        )

    me = jnp.stack([myself, jnp.int32(shards)]).astype(jnp.int32)
    entries = layout.reshape(-1)
    unit, keyval = pack(
        query_rows, output_grad, output_rows, key_rows, value_rows, logsumexp.reshape(count, BLK)
    )

    def merge(one, two):
        return (one.astype(jnp.float32) + two.astype(jnp.float32)).astype(jnp.bfloat16)

    def wide(array):
        return array.astype(jnp.float32)

    def tie(*arrays):
        return lax.optimization_barrier(arrays)

    last = planes - 1
    ends = [(last * span + e, e) for e in range(span)]
    ends = ends + [(two, one) for one, two in ends]
    up, down = (shift(unit, 1, 0, last), shift(unit, -1, 1, planes))
    keyvals = {0: keyval}
    singles = [m for m in range(1, span) if m & (m - 1) == 0]
    for m in singles:
        keyvals[m] = swap(keyval, m)
    up, down, far, *arrived = tie(up, down, unit, *[keyvals[m] for m in singles])
    keyvals.update(zip(singles, arrived))
    far = send(far, ends)
    for m in range(1, span):
        if m & (m - 1):
            keyvals[m] = swap(keyvals[m & (m - 1)], m & -m)
    keyvals = [keyvals[m] for m in range(span)]

    def meet(units, offsets, keyvals, acc, final=False):
        return visit(me, entries, units, offsets, keyvals, acc, final, count, span, fanout)

    keys, values, acc, query_acc = meet([unit], (0,), keyvals, None)
    up_parts, down_parts = ([], [])
    for s in range(1, last):
        if s + 1 < last:
            next_up, next_down = (shift(up, 1, s, last), shift(down, -1, 1, planes - s))
        final = s + 1 == last
        units, offsets = ([up, down], (-s, s))
        if final:
            units, offsets = (units + [far], offsets + (None,))
        acc, up_part, down_part, *rest = meet(units, offsets, [keys, values], acc, final)
        up_parts.append(up_part)
        down_parts.append(down_part)
        if not final:
            up, down = (next_up, next_down)
    far_part, sent, kept = rest

    up_back, down_back = (up_parts[-1], down_parts[-1])
    for t in range(last - 1, 0, -1):
        up_back = shift(up_back, -1, t, planes)
        down_back = shift(down_back, 1, 0, planes - t)
        if t > 1:
            up_back = merge(up_parts[t - 2], up_back)
            down_back = merge(down_parts[t - 2], down_back)
    query_acc = query_acc + wide(send(far_part, ends)) + wide(up_back) + wide(down_back)

    bit = 1
    while True:
        kept = kept + swap(sent, bit).astype(jnp.float32)
        bit = bit * 2
        if bit == span:
            break
        halves = kept.reshape((2, kept.shape[1] // 2, 2) + kept.shape[2:])
        kept = halves[:, :, 0]
        sent = halves[:, :, 1].astype(jnp.bfloat16)
    query_grad = query_acc.reshape(count * BLK, width).astype(jnp.bfloat16)
    key_grad = kept[0, 0].reshape(count * BLK, width).astype(jnp.bfloat16)
    value_grad = kept[1, 0].reshape(count * BLK, width).astype(jnp.bfloat16)
    return (query_grad, key_grad, value_grad)


def solution(mesh):
    in_specs = (
        P(("grp", "qb"), None),
        P(("grp", "qb"), None),
        P(("grp", "qb"), None),
        P(("grp", "qb"), None),
        P(("grp", "qb"), None),
        P(("grp", "qb")),
        P("grp", None),
    )
    out_specs = (P(("grp", "qb"), None), P(("grp", "qb"), None), P(("grp", "qb"), None))
    return jax.shard_map(body, mesh=mesh, in_specs=in_specs, out_specs=out_specs, check_vma=False)
```

```python
import functools

import jax
import jax.numpy as jnp
from jax import lax
from jax.experimental import pallas as pl
from jax.experimental.pallas import tpu as pltpu
from jax.sharding import PartitionSpec as P

BLK = 128
GLOB = 2
TILE = 16
PAIRS = 3
TURNS = 3
FAR = 1e30
COST = 20
LIMIT = 16 * 2**20


def pieces(row):
    high = row.astype(jnp.bfloat16)
    rest = row - high.astype(jnp.float32)
    middle = rest.astype(jnp.bfloat16)
    low = (rest - middle.astype(jnp.float32)).astype(jnp.bfloat16)
    return [high.astype(jnp.float32), middle.astype(jnp.float32), low.astype(jnp.float32)]


def stat_rows(count):
    return -(-count // TILE) * TILE


def placed(array, space):
    return pltpu.with_memory_space_constraint(array, space)


def groups_of(count):
    return next(groups for groups in (3, 4, 2, 1) if count % groups == 0)


def pack_kernel(query, grad, output, lse, unit, output_s, delta_s, sems):
    count, width = lse.shape
    rows = stat_rows(count)
    groups = groups_of(count)
    group = count // groups
    ones = jnp.ones((TILE, width), jnp.bfloat16)
    held = count * BLK
    loads = []
    for g in range(groups):
        at = pl.ds(g * group * BLK, group * BLK)
        after = pl.ds(held + g * group * BLK, group * BLK)
        loads.append(
            [
                pltpu.make_async_copy(grad.at[at], unit.at[after], sems.at[0, g]),
                pltpu.make_async_copy(output.at[at], output_s.at[at], sems.at[1, g]),
                pltpu.make_async_copy(query.at[at], unit.at[at], sems.at[2, g]),
            ]
        )
    for kind in range(3):
        for load in loads:
            load[kind].start()

    def total(part):
        return lax.dot_general(
            ones, part, (((1,), (1,)), ((), ())), preferred_element_type=jnp.float32
        )

    delta_s[...] = jnp.zeros(delta_s.shape, jnp.float32)
    for g in range(groups):
        loads[g][0].wait()
        loads[g][1].wait()
        highs, lows = ([], [])
        for k in range(g * group, (g + 1) * group):
            grads = unit[held + k * BLK : held + (k + 1) * BLK, :].astype(jnp.float32)
            product = grads * output_s[k * BLK : (k + 1) * BLK, :].astype(jnp.float32)
            highs.append(product.astype(jnp.bfloat16))
            lows.append((product - highs[-1].astype(jnp.float32)).astype(jnp.bfloat16))
        sums = [total(high) + total(low) for high, low in zip(highs, lows)]
        for k in range(group):
            delta_s[g * group + k : g * group + k + 1, :] = sums[k][0:1]
    lines = lse[...]
    if rows > count:
        lines = jnp.concatenate([lines, jnp.zeros((rows - count, width), jnp.float32)], 0)
    stats = pieces(lines) + pieces(delta_s[...])
    unit[2 * held :, :] = jnp.concatenate(stats, 0).astype(jnp.bfloat16)
    for load in loads:
        load[2].wait()


def pack(query, grad, output, lse):
    count, width = lse.shape
    rows = stat_rows(count)
    hbm = pl.BlockSpec(memory_space=pltpu.HBM)
    return pl.pallas_call(
        pack_kernel,
        out_shape=jax.ShapeDtypeStruct((2 * count * BLK + 6 * rows, width), jnp.bfloat16),
        in_specs=[hbm, hbm, hbm, pl.BlockSpec(memory_space=pltpu.VMEM)],
        out_specs=pl.BlockSpec(memory_space=pltpu.VMEM),
        scratch_shapes=[
            pltpu.VMEM(query.shape, jnp.bfloat16),
            pltpu.VMEM((rows, width), jnp.float32),
            pltpu.SemaphoreType.DMA((3, groups_of(count))),
        ],
        compiler_params=pltpu.CompilerParams(vmem_limit_bytes=LIMIT),
        name="pack",
    )(*[placed(array, pltpu.HBM) for array in (query, grad, output)], lse)


def join_kernel(key, value, keyval, sems):
    rows = key.shape[0]
    copies = [
        pltpu.make_async_copy(key, keyval.at[pl.ds(0, rows)], sems.at[0]),
        pltpu.make_async_copy(value, keyval.at[pl.ds(rows, rows)], sems.at[1]),
    ]
    for copy in copies:
        copy.start()
    for copy in copies:
        copy.wait()


def join(key, value):
    rows, width = key.shape
    hbm = pl.BlockSpec(memory_space=pltpu.HBM)
    return pl.pallas_call(
        join_kernel,
        out_shape=jax.ShapeDtypeStruct((2 * rows, width), key.dtype),
        in_specs=[hbm, hbm],
        out_specs=pl.BlockSpec(memory_space=pltpu.VMEM),
        scratch_shapes=[pltpu.SemaphoreType.DMA((2,))],
        compiler_params=pltpu.CompilerParams(vmem_limit_bytes=LIMIT),
        name="join",
    )(placed(key, pltpu.HBM), placed(value, pltpu.HBM))


def pair_grads(pairs, scaling):
    def outer(one, two):
        return lax.dot_general(
            one, two, (((1,), (1,)), ((), ())), preferred_element_type=jnp.float32
        )

    def inner(one, two):
        return jnp.dot(one, two, preferred_element_type=jnp.float32)

    def flipped(one, two):
        return lax.dot_general(
            one, two, (((0,), (0,)), ((), ())), preferred_element_type=jnp.float32
        )

    scores = [outer(keys, queries) for keys, _, queries, _, _, _, _ in pairs]
    dweights = [outer(values, grads) for _, values, _, grads, _, _, _ in pairs]
    probs = []
    for score, (_, _, _, _, lse, _, mask) in zip(scores, pairs):
        prob = jnp.exp(score * scaling - lse)
        probs.append(prob if mask is None else jnp.where(mask, prob, 0.0))
    prob_lows = [prob.astype(jnp.bfloat16) for prob in probs]
    score_lows = [
        (prob * (dweight - pair[5])).astype(jnp.bfloat16)
        for prob, dweight, pair in zip(probs, dweights, pairs)
    ]
    value_parts = [inner(low, pair[3]) for low, pair in zip(prob_lows, pairs)]
    key_parts = [inner(low, pair[2]) for low, pair in zip(score_lows, pairs)]
    query_parts = [flipped(low, pair[0]) for low, pair in zip(score_lows, pairs)]
    return list(zip(query_parts, key_parts, value_parts))


class Visitor:
    def __init__(
        self, count, unit, lse, delta, dq, keys, values, acc, layout=None, lists=None, values_at=0
    ):
        self.count = count
        self.unit, self.lse, self.delta = (unit, lse, delta)
        self.dq, self.keys, self.values, self.acc = (dq, keys, values, acc)
        self.layout, self.lists, self.values_at = (layout, lists, values_at)
        self.width = unit.shape[1]
        self.scaling = self.width ** (-0.5)
        self.held = keys.shape[0] // BLK

    def begin(self, clear=True):
        count = self.count
        rows = stat_rows(count)
        stats = self.unit[2 * count * BLK :, :].astype(jnp.float32)
        lines = [stats[k * rows : (k + 1) * rows] for k in range(6)]
        self.lse[...] = lines[0] + lines[1] + lines[2]
        self.delta[...] = lines[3] + lines[4] + lines[5]

        def step(q, carry):
            self.dq[q] = jnp.zeros(self.dq.shape[1:], jnp.float32)
            return carry

        if clear:
            lax.fori_loop(0, count, step, 0)

    def rows(self, array, block, blocks=1):
        return array[pl.ds(pl.multiple_of(block * BLK, BLK), blocks * BLK), :]

    def pair(self, q, j, keys=1, shift=0.0, mask=None):
        return (
            self.rows(self.keys, j, keys),
            self.rows(self.values, self.values_at + j, keys),
            self.rows(self.unit, q),
            self.rows(self.unit, self.count + q),
            self.lse[pl.ds(q, 1), :] + shift,
            self.delta[pl.ds(q, 1), :],
            mask,
        )

    def window(self):
        count, width = (self.count, self.width)
        chunk = 2 if count % 2 == 0 else 1

        def step(c, carry):
            places, pairs = ([], [])
            for k in range(chunk):
                q = c * chunk + k
                start = jnp.clip(q - 1, 0, count - 3)
                block = lax.broadcasted_iota(jnp.int32, (3 * BLK, BLK), 0) // BLK
                block = block + start - q
                places.append((q, start))
                pairs.append(self.pair(q, start, 3, 0.0, (block >= -1) & (block <= 1)))
            parts = pair_grads(pairs, self.scaling)
            for (q, start), (query_part, key_part, value_part) in zip(places, parts):
                self.dq[q] += query_part
                self.acc[pl.ds(start, 3), 0] += key_part.reshape(3, BLK, width)
                self.acc[pl.ds(start, 3), 1] += value_part.reshape(3, BLK, width)
            return carry

        lax.fori_loop(0, count // chunk, step, 0)

    def anchors(self):
        count, width = (self.count, self.width)
        chunk = 2 if count % 2 == 0 else 1
        turns = next(turns for turns in (TURNS, 2, 1) if count % (turns * chunk) == 0)

        def step(c, carry):
            places, pairs = ([], [])
            for k in range(turns):
                at = (c * turns + k) * chunk
                places.append(pl.ds(at, chunk))
                pairs.append(
                    (
                        self.keys[0 : GLOB * BLK, :],
                        self.values[0 : GLOB * BLK, :],
                        self.rows(self.unit, at, chunk),
                        self.rows(self.unit, count + at, chunk),
                        jnp.concatenate(
                            [self.lse[pl.ds(at + i, 1), :] for i in range(chunk)], 1
                        ),
                        jnp.concatenate(
                            [self.delta[pl.ds(at + i, 1), :] for i in range(chunk)], 1
                        ),
                        None,
                    )
                )
            parts = pair_grads(pairs, self.scaling)
            for blocks, (query_part, _, _) in zip(places, parts):
                self.dq[blocks] += query_part.reshape(chunk, BLK, width)
            key_part = sum(part[1] for part in parts)
            value_part = sum(part[2] for part in parts)
            self.acc[0:GLOB, 0] += key_part.reshape(GLOB, BLK, width)
            self.acc[0:GLOB, 1] += value_part.reshape(GLOB, BLK, width)
            return carry

        lax.fori_loop(0, count // (chunk * turns), step, 0)

    def scattered(self, guest, low, fanout, near):
        who, whom, far = self.lists
        count = self.count

        def note(at, q, target):
            local = target - low
            hit = (local >= 0) & (local < self.held)
            who[at] = q
            whom[at] = local
            far[at] = 0.0
            return at + hit.astype(jnp.int32)

        def gather(q, at):
            block = guest * count + q
            for r in range(fanout):
                at = note(at, q, self.layout[block * fanout + r])
            return at

        found = lax.fori_loop(0, count, gather, 0)
        if near:
            found = note(found, 0, guest * count - 1)
            found = note(found, count - 1, (guest + 1) * count)
        for k in range(PAIRS - 1):
            who[found + k] = 0
            whom[found + k] = 0
            far[found + k] = FAR

        def step(g, carry):
            places, pairs = ([], [])
            for k in range(PAIRS):
                at = g * PAIRS + k
                places.append((who[at], whom[at]))
                pairs.append(self.pair(who[at], whom[at], 1, far[at]))
            parts = pair_grads(pairs, self.scaling)
            for (q, j), (query_part, key_part, value_part) in zip(places, parts):
                self.dq[q] += query_part
                self.acc[j, 0] += key_part
                self.acc[j, 1] += value_part
            return carry

        lax.fori_loop(0, (found + PAIRS - 1) // PAIRS, step, 0)

    def finish(self, out):
        def step(q, carry):
            out[q] = (self.dq[q] * self.scaling).astype(out.dtype)
            return carry

        lax.fori_loop(0, self.count, step, 0)


def own_kernel(unit, keyval, acc, dq, lse, delta):
    def clear(b, carry):
        acc[b] = jnp.zeros(acc.shape[1:], jnp.float32)
        return carry

    count = dq.shape[0]
    lax.fori_loop(0, count, clear, 0)
    own = Visitor(count, unit, lse, delta, dq, keyval, keyval, acc, values_at=count)
    own.begin()
    own.window()


def visit_kernel(plan, me_ref, layout, *refs):
    offsets, count, span, fanout = plan
    refs = list(refs)
    first = offsets == (0,)
    guests = [refs.pop(0) for _ in offsets]
    me = me_ref[0]
    shards = me_ref[1]
    seat = lax.rem(me, span)
    row = lax.div(me, span)
    low = row * span * count
    if first:
        parts = [refs.pop(0) for _ in range(span)]
        acc_own, dq_own = (refs.pop(0), refs.pop(0))
        keys, values = (refs.pop(0), refs.pop(0))
    else:
        keys, values = (refs.pop(0), refs.pop(0))
        refs.pop(0)
    acc = refs.pop(0)
    outs = [refs.pop(0) for _ in offsets]
    sums = outs if first else [refs.pop(0) for _ in offsets]
    lse, delta = (refs.pop(0), refs.pop(0))
    lists = refs
    if first:

        def lay(b, carry):
            for m in range(span):
                there = jnp.bitwise_xor(seat, m) * count + b
                if m == 0:
                    acc[there] = acc_own[b]
                    sums[0][b] = dq_own[b]
                else:
                    acc[there] = jnp.zeros(acc.shape[1:], jnp.float32)
                there = pl.ds(pl.multiple_of(there * BLK, BLK), BLK)
                here = pl.ds(pl.multiple_of(b * BLK, BLK), BLK)
                keys[there, :] = parts[m][here, :]
                here = pl.ds(pl.multiple_of((count + b) * BLK, BLK), BLK)
                values[there, :] = parts[m][here, :]
            return carry

        lax.fori_loop(0, count, lay, 0)

    for v, offset in enumerate(offsets):
        if offset is None:
            guest = jnp.where(row == 0, me + shards - span, me + span - shards)
            present = (row == 0) | (me + span >= shards)
        else:
            guest = me + offset * span
            present = (guest >= 0) & (guest < shards)
        visitor = Visitor(count, guests[v], lse, delta, sums[v], keys, values, acc, layout, lists)

        @pl.when(present)
        def _(visitor=visitor, offset=offset, guest=guest, out=outs[v]):
            visitor.begin(offset != 0)
            @pl.when(row == 0)
            def _():
                visitor.anchors()

            visitor.scattered(guest, low, fanout, offset in (-1, 0, 1))
            visitor.finish(out)


def sum_of(m, which, b, acc, place, scaling, parts, arrived):
    total = acc[place, which]
    if which == 0:
        total = total * scaling
    for part, units in zip(parts, arrived):
        total = total + part[which, units.index(m), b].astype(jnp.float32)
    return total.astype(jnp.bfloat16)


def share_kernel(plan, me_ref, acc, *refs):
    span, wanted, arrived = plan
    parts, out = (refs[:-1], refs[-1])
    count = acc.shape[0] // span
    scaling = acc.shape[3] ** (-0.5)
    seat = lax.rem(me_ref[0], span)

    def step(b, carry):
        for k, m in enumerate(wanted):
            place = jnp.bitwise_xor(seat, m) * count + b
            for which in range(2):
                out[which, k, b] = sum_of(m, which, b, acc, place, scaling, parts, arrived)
        return carry

    lax.fori_loop(0, count, step, 0)


def finish_kernel(plan, me_ref, acc, *refs):
    span, arrived = plan
    parts, outs = (refs[: len(arrived)], refs[len(arrived) : len(arrived) + 2])
    held_s, sems = refs[len(arrived) + 2 :]
    count = acc.shape[0] // span
    scaling = acc.shape[3] ** (-0.5)
    seat = lax.rem(me_ref[0], span)
    groups = groups_of(count)
    group = count // groups
    copies = []
    for g in range(groups):
        for b in range(g * group, (g + 1) * group):
            for which in range(2):
                held_s[which, b * BLK : (b + 1) * BLK, :] = sum_of(
                    0, which, b, acc, seat * count + b, scaling, parts, arrived
                )
        for which in range(2):
            at = pl.ds(g * group * BLK, group * BLK)
            copies.append(
                pltpu.make_async_copy(
                    held_s.at[which, at], outs[which].at[at], sems.at[which, g]
                )
            )
            copies[-1].start()
    for copy in copies:
        copy.wait()


SMEM = pl.BlockSpec(memory_space=pltpu.SMEM)
VMEM = pl.BlockSpec(memory_space=pltpu.VMEM)


def own_visit(unit, keyval, count):
    width = unit.shape[1]
    stats = pltpu.VMEM((stat_rows(count), width), jnp.float32)
    return pl.pallas_call(
        own_kernel,
        out_shape=(
            jax.ShapeDtypeStruct((count, 2, BLK, width), jnp.float32),
            jax.ShapeDtypeStruct((count, BLK, width), jnp.float32),
        ),
        scratch_shapes=[stats, stats],
        compiler_params=pltpu.CompilerParams(vmem_limit_bytes=LIMIT),
        name="own",
    )(unit, keyval)


def share(me, acc, span, wanted, arrived, parts):
    held, _, _, width = acc.shape
    return pl.pallas_call(
        functools.partial(share_kernel, (span, wanted, arrived)),
        out_shape=jax.ShapeDtypeStruct((2, len(wanted), held // span, BLK, width), jnp.bfloat16),
        in_specs=[SMEM] + [VMEM] * (1 + len(parts)),
        out_specs=VMEM,
        compiler_params=pltpu.CompilerParams(vmem_limit_bytes=LIMIT),
        name="share",
    )(me, acc, *parts)


def finish(me, acc, span, arrived, parts):
    held, _, _, width = acc.shape
    count = held // span
    shape = (count * BLK, width)
    hbm = pl.BlockSpec(memory_space=pltpu.HBM)
    return pl.pallas_call(
        functools.partial(finish_kernel, (span, arrived)),
        out_shape=[jax.ShapeDtypeStruct(shape, jnp.bfloat16)] * 2,
        in_specs=[SMEM] + [VMEM] * (1 + len(parts)),
        out_specs=[hbm, hbm],
        scratch_shapes=[
            pltpu.VMEM((2,) + shape, jnp.bfloat16),
            pltpu.SemaphoreType.DMA((2, groups_of(count))),
        ],
        compiler_params=pltpu.CompilerParams(vmem_limit_bytes=LIMIT),
        name="finish",
    )(me, acc, *parts)


def add_kernel(base, *refs):
    parts, out = (refs[:-1], refs[-1])

    def step(b, carry):
        total = base[b]
        for part in parts:
            total = total + part[b].astype(jnp.float32)
        if len(out.shape) == 3:
            out[b] = total
        else:
            out[pl.ds(pl.multiple_of(b * BLK, BLK), BLK), :] = total.astype(out.dtype)
        return carry

    lax.fori_loop(0, base.shape[0], step, 0)


def add(base, parts, final, weight):
    count, _, width = base.shape
    if final:
        out = jax.ShapeDtypeStruct((count * BLK, width), jnp.bfloat16)
    else:
        out = jax.ShapeDtypeStruct(base.shape, jnp.float32)
    return pl.pallas_call(
        add_kernel,
        out_shape=out,
        cost_estimate=pl.CostEstimate(
            flops=weight * count * 10 * BLK * BLK * width, bytes_accessed=0, transcendentals=0
        ),
        compiler_params=pltpu.CompilerParams(vmem_limit_bytes=LIMIT),
        name="add",
    )(base, *parts)


def visit(me, layout, units, offsets, keyvals, acc, query_acc, weight, count, span, fanout):
    first = query_acc is not None
    width = units[0].shape[1]
    held = span * count
    plan = (offsets, count, span, fanout)
    operands = units + keyvals
    keys = jax.ShapeDtypeStruct((held * BLK, width), jnp.bfloat16)
    outs = [jax.ShapeDtypeStruct((held, 2, BLK, width), jnp.float32)]
    if first:
        outs = [keys, keys] + outs
        aliases = {}
        operands = operands + [acc, query_acc]
    else:
        aliases = {len(operands) + 2: 0}
        operands = operands + [placed(acc, pltpu.VMEM)]
    kind = jnp.float32 if first else jnp.bfloat16
    outs += [jax.ShapeDtypeStruct((count, BLK, width), kind)] * len(units)
    entries = count * fanout + 2 + PAIRS
    stats = pltpu.VMEM((stat_rows(count), width), jnp.float32)
    return list(
        pl.pallas_call(
            functools.partial(visit_kernel, plan),
            out_shape=outs,
            in_specs=[SMEM, SMEM] + [VMEM] * len(operands),
            out_specs=[VMEM] * len(outs),
            input_output_aliases=aliases,
            scratch_shapes=[pltpu.VMEM((count, BLK, width), jnp.float32)]
            * (0 if first else len(units))
            + [
                stats,
                stats,
                pltpu.SMEM((entries,), jnp.int32),
                pltpu.SMEM((entries,), jnp.int32),
                pltpu.SMEM((entries,), jnp.float32),
            ],
            compiler_params=pltpu.CompilerParams(vmem_limit_bytes=LIMIT),
            cost_estimate=pl.CostEstimate(
                flops=weight * count * 10 * BLK * BLK * width,
                bytes_accessed=0,
                transcendentals=len(offsets) * count * BLK * BLK,
            ),
            name="visit",
        )(me, layout, *operands)
    )


def body(query_rows, key_rows, value_rows, output_rows, output_grad, logsumexp, layout):
    shards = lax.axis_size("qb")
    myself = lax.axis_index("qb")
    width = query_rows.shape[1]
    count = query_rows.shape[0] // BLK
    fanout = layout.shape[1]
    span = 4
    while shards // span > 16:
        span = span * 2
    planes = shards // span

    def send(array, pairs):
        return lax.ppermute(array, "qb", pairs)

    def swap(array, bit):
        return send(array, [(i, i ^ bit) for i in range(shards)])

    def shift(array, planes_away, low, high):
        return send(
            array,
            [
                (p * span + e, (p + planes_away) * span + e)
                for p in range(low, high)
                for e in range(span)
            ],
        )

    me = jnp.stack([myself, jnp.int32(shards)]).astype(jnp.int32)
    entries = layout.reshape(-1)
    unit = pack(query_rows, output_grad, output_rows, logsumexp.reshape(count, BLK))
    keyval = join(key_rows, value_rows)

    def merge(one, two):
        return (one.astype(jnp.float32) + two.astype(jnp.float32)).astype(jnp.bfloat16)

    def tie(*arrays):
        return lax.optimization_barrier(arrays)

    last = planes - 1
    up, down = (shift(unit, 1, 0, last), shift(unit, -1, 1, planes))
    keyvals = {0: keyval}
    singles = [m for m in range(1, span) if m & (m - 1) == 0]
    for m in singles:
        keyvals[m] = swap(keyval, m)
    acc, query_acc = own_visit(unit, keyval, count)
    up, down, query_acc = tie(up, down, query_acc)
    for m in range(1, span):
        if m & (m - 1):
            keyvals[m] = swap(keyvals[m & (m - 1)], m & -m)
    keyvals = [keyvals[m] for m in range(span)]

    def meet(units, offsets, keyvals, acc, query_acc=None, weight=0):
        return visit(
            me, entries, units, offsets, keyvals, acc, query_acc, weight, count, span, fanout
        )

    keys, values, acc, query_acc = meet([unit], (0,), keyvals, acc, query_acc)
    above = myself >= shards // 2
    inward = [(p * span + e, q * span + e) for p, q in ((last - 1, last), (1, 0)) for e in range(span)]
    ends = [(last * span + e, e) for e in range(span)]
    ends = ends + [(two, one) for one, two in ends]
    up_parts, down_parts = ([], [])
    for s in range(1, last):
        if s + 1 < last:
            next_up, next_down = (shift(up, 1, s, last), shift(down, -1, 1, planes - s))
        else:
            up, down, query_acc = tie(up, down, query_acc)
            far = send(jnp.where(above, up, down), inward)
        acc, up_part, down_part = meet([up, down], (-s, s), [keys, values], acc)
        up_parts.append(up_part)
        down_parts.append(down_part)
        if s + 1 < last:
            up, down = (next_up, next_down)

    acc, far_part = meet([far], (None,), [keys, values], acc, None, COST)

    up_back, down_back = (up_parts[-1], down_parts[-1])
    for t in range(last - 1, 1, -1):
        up_back, down_back = (shift(up_back, -1, t, planes), shift(down_back, 1, 0, planes - t))
        if t == 2:
            up_back, down_back, far_part = tie(up_back, down_back, far_part)
        up_back = merge(up_parts[t - 2], up_back)
        down_back = merge(down_parts[t - 2], down_back)
    acc, up_back, down_back = tie(acc, up_back, down_back)
    query_acc = add(query_acc, [send(far_part, ends)], False, COST)
    query_grad = add(
        query_acc, [shift(up_back, -1, 1, planes), shift(down_back, 1, 0, planes - 1)], True, 1
    )

    wanted = tuple(range(span))
    arrived, parts = ((), ())
    bit = 1
    while bit < span:
        theirs = tuple(m for m in wanted if m & bit)
        wanted = tuple(m for m in wanted if not m & bit)
        sent = share(me, acc, span, theirs, arrived, parts)
        arrived, parts = (arrived + (wanted,), parts + (swap(sent, bit),))
        bit = bit * 2
    *parts, query_grad = tie(*parts, query_grad)
    key_grad, value_grad = finish(me, acc, span, arrived, parts)
    return (query_grad, key_grad, value_grad)


def solution(mesh):
    in_specs = (
        P(("grp", "qb"), None),
        P(("grp", "qb"), None),
        P(("grp", "qb"), None),
        P(("grp", "qb"), None),
        P(("grp", "qb"), None),
        P(("grp", "qb")),
        P("grp", None),
    )
    out_specs = (P(("grp", "qb"), None), P(("grp", "qb"), None), P(("grp", "qb"), None))
    return jax.shard_map(body, mesh=mesh, in_specs=in_specs, out_specs=out_specs, check_vma=False)
```

```python
import functools

import jax
import jax.numpy as jnp
from jax import lax
from jax.experimental import pallas as pl
from jax.experimental.pallas import tpu as pltpu
from jax.sharding import PartitionSpec as P

BLK = 128
GLOB = 2
TILE = 16
PAIRS = 6
TURNS = 3
FAR = 1e30
COST = 20
LIMIT = 16 * 2**20


def pieces(row):
    high = row.astype(jnp.bfloat16)
    rest = row - high.astype(jnp.float32)
    middle = rest.astype(jnp.bfloat16)
    low = (rest - middle.astype(jnp.float32)).astype(jnp.bfloat16)
    return [high.astype(jnp.float32), middle.astype(jnp.float32), low.astype(jnp.float32)]


def stat_rows(count):
    return -(-count // TILE) * TILE


def placed(array, space):
    return pltpu.with_memory_space_constraint(array, space)


def groups_of(count):
    return next(groups for groups in (3, 4, 2, 1) if count % groups == 0)


def pack_kernel(query, grad, output, lse, unit, output_s, delta_s, sems):
    count, width = lse.shape
    rows = stat_rows(count)
    groups = groups_of(count)
    group = count // groups
    ones = jnp.ones((TILE, width), jnp.bfloat16)
    held = count * BLK
    loads = []
    for g in range(groups):
        at = pl.ds(g * group * BLK, group * BLK)
        after = pl.ds(held + g * group * BLK, group * BLK)
        loads.append(
            [
                pltpu.make_async_copy(grad.at[at], unit.at[after], sems.at[0, g]),
                pltpu.make_async_copy(output.at[at], output_s.at[at], sems.at[1, g]),
                pltpu.make_async_copy(query.at[at], unit.at[at], sems.at[2, g]),
            ]
        )
    for kind in range(3):
        for load in loads:
            load[kind].start()

    def total(part):
        return lax.dot_general(
            ones, part, (((1,), (1,)), ((), ())), preferred_element_type=jnp.float32
        )

    delta_s[...] = jnp.zeros(delta_s.shape, jnp.float32)
    for g in range(groups):
        loads[g][0].wait()
        loads[g][1].wait()
        highs, lows = ([], [])
        for k in range(g * group, (g + 1) * group):
            grads = unit[held + k * BLK : held + (k + 1) * BLK, :].astype(jnp.float32)
            product = grads * output_s[k * BLK : (k + 1) * BLK, :].astype(jnp.float32)
            highs.append(product.astype(jnp.bfloat16))
            lows.append((product - highs[-1].astype(jnp.float32)).astype(jnp.bfloat16))
        sums = [total(high) + total(low) for high, low in zip(highs, lows)]
        for k in range(group):
            delta_s[g * group + k : g * group + k + 1, :] = sums[k][0:1]
    lines = lse[...]
    if rows > count:
        lines = jnp.concatenate([lines, jnp.zeros((rows - count, width), jnp.float32)], 0)
    stats = pieces(lines) + pieces(delta_s[...])
    unit[2 * held :, :] = jnp.concatenate(stats, 0).astype(jnp.bfloat16)
    for load in loads:
        load[2].wait()


def pack(query, grad, output, lse):
    count, width = lse.shape
    rows = stat_rows(count)
    hbm = pl.BlockSpec(memory_space=pltpu.HBM)
    return pl.pallas_call(
        pack_kernel,
        out_shape=jax.ShapeDtypeStruct((2 * count * BLK + 6 * rows, width), jnp.bfloat16),
        in_specs=[hbm, hbm, hbm, pl.BlockSpec(memory_space=pltpu.VMEM)],
        out_specs=pl.BlockSpec(memory_space=pltpu.VMEM),
        scratch_shapes=[
            pltpu.VMEM(query.shape, jnp.bfloat16),
            pltpu.VMEM((rows, width), jnp.float32),
            pltpu.SemaphoreType.DMA((3, groups_of(count))),
        ],
        compiler_params=pltpu.CompilerParams(vmem_limit_bytes=LIMIT),
        name="pack",
    )(*[placed(array, pltpu.HBM) for array in (query, grad, output)], lse)


def join_kernel(key, value, keyval, sems):
    rows = key.shape[0]
    copies = [
        pltpu.make_async_copy(key, keyval.at[pl.ds(0, rows)], sems.at[0]),
        pltpu.make_async_copy(value, keyval.at[pl.ds(rows, rows)], sems.at[1]),
    ]
    for copy in copies:
        copy.start()
    for copy in copies:
        copy.wait()


def join(key, value):
    rows, width = key.shape
    hbm = pl.BlockSpec(memory_space=pltpu.HBM)
    return pl.pallas_call(
        join_kernel,
        out_shape=jax.ShapeDtypeStruct((2 * rows, width), key.dtype),
        in_specs=[hbm, hbm],
        out_specs=pl.BlockSpec(memory_space=pltpu.VMEM),
        scratch_shapes=[pltpu.SemaphoreType.DMA((2,))],
        compiler_params=pltpu.CompilerParams(vmem_limit_bytes=LIMIT),
        name="join",
    )(placed(key, pltpu.HBM), placed(value, pltpu.HBM))


def pair_grads(pairs, scaling):
    def outer(one, two):
        return lax.dot_general(
            one, two, (((1,), (1,)), ((), ())), preferred_element_type=jnp.float32
        )

    def inner(one, two):
        return jnp.dot(one, two, preferred_element_type=jnp.float32)

    def flipped(one, two):
        return lax.dot_general(
            one, two, (((0,), (0,)), ((), ())), preferred_element_type=jnp.float32
        )

    scores = [outer(keys, queries) for keys, _, queries, _, _, _, _ in pairs]
    dweights = [outer(values, grads) for _, values, _, grads, _, _, _ in pairs]
    probs = []
    for score, (_, _, _, _, lse, _, mask) in zip(scores, pairs):
        prob = jnp.exp(score * scaling - lse)
        probs.append(prob if mask is None else jnp.where(mask, prob, 0.0))
    prob_lows = [prob.astype(jnp.bfloat16) for prob in probs]
    score_lows = [
        (prob * (dweight - pair[5])).astype(jnp.bfloat16)
        for prob, dweight, pair in zip(probs, dweights, pairs)
    ]
    value_parts = [inner(low, pair[3]) for low, pair in zip(prob_lows, pairs)]
    key_parts = [inner(low, pair[2]) for low, pair in zip(score_lows, pairs)]
    query_parts = [flipped(low, pair[0]) for low, pair in zip(score_lows, pairs)]
    return list(zip(query_parts, key_parts, value_parts))


class Visitor:
    def __init__(
        self, count, unit, lse, delta, dq, keys, values, acc, layout=None, lists=None, values_at=0
    ):
        self.count = count
        self.unit, self.lse, self.delta = (unit, lse, delta)
        self.dq, self.keys, self.values, self.acc = (dq, keys, values, acc)
        self.layout, self.lists, self.values_at = (layout, lists, values_at)
        self.width = unit.shape[1]
        self.scaling = self.width ** (-0.5)
        self.held = keys.shape[0] // BLK

    def begin(self, clear=True):
        count = self.count
        rows = stat_rows(count)
        stats = self.unit[2 * count * BLK :, :].astype(jnp.float32)
        lines = [stats[k * rows : (k + 1) * rows] for k in range(6)]
        self.lse[...] = lines[0] + lines[1] + lines[2]
        self.delta[...] = lines[3] + lines[4] + lines[5]

        def step(q, carry):
            self.dq[q] = jnp.zeros(self.dq.shape[1:], jnp.float32)
            return carry

        if clear:
            lax.fori_loop(0, count, step, 0)

    def rows(self, array, block, blocks=1):
        return array[pl.ds(pl.multiple_of(block * BLK, BLK), blocks * BLK), :]

    def pair(self, q, j, keys=1, shift=0.0, mask=None):
        return (
            self.rows(self.keys, j, keys),
            self.rows(self.values, self.values_at + j, keys),
            self.rows(self.unit, q),
            self.rows(self.unit, self.count + q),
            self.lse[pl.ds(q, 1), :] + shift,
            self.delta[pl.ds(q, 1), :],
            mask,
        )

    def window(self):
        count, width = (self.count, self.width)
        chunk = 2 if count % 2 == 0 else 1

        def step(c, carry):
            places, pairs = ([], [])
            for k in range(chunk):
                q = c * chunk + k
                start = jnp.clip(q - 1, 0, count - 3)
                block = lax.broadcasted_iota(jnp.int32, (3 * BLK, BLK), 0) // BLK
                block = block + start - q
                places.append((q, start))
                pairs.append(self.pair(q, start, 3, 0.0, (block >= -1) & (block <= 1)))
            parts = pair_grads(pairs, self.scaling)
            for (q, start), (query_part, key_part, value_part) in zip(places, parts):
                self.dq[q] += query_part
                self.acc[pl.ds(start, 3), 0] += key_part.reshape(3, BLK, width)
                self.acc[pl.ds(start, 3), 1] += value_part.reshape(3, BLK, width)
            return carry

        lax.fori_loop(0, count // chunk, step, 0)

    def anchors(self):
        count, width = (self.count, self.width)
        chunk = 2 if count % 2 == 0 else 1
        turns = next(turns for turns in (TURNS, 2, 1) if count % (turns * chunk) == 0)

        def step(c, carry):
            places, pairs = ([], [])
            for k in range(turns):
                at = (c * turns + k) * chunk
                places.append(pl.ds(at, chunk))
                pairs.append(
                    (
                        self.keys[0 : GLOB * BLK, :],
                        self.values[0 : GLOB * BLK, :],
                        self.rows(self.unit, at, chunk),
                        self.rows(self.unit, count + at, chunk),
                        jnp.concatenate(
                            [self.lse[pl.ds(at + i, 1), :] for i in range(chunk)], 1
                        ),
                        jnp.concatenate(
                            [self.delta[pl.ds(at + i, 1), :] for i in range(chunk)], 1
                        ),
                        None,
                    )
                )
            parts = pair_grads(pairs, self.scaling)
            for blocks, (query_part, _, _) in zip(places, parts):
                self.dq[blocks] += query_part.reshape(chunk, BLK, width)
            key_part = sum(part[1] for part in parts)
            value_part = sum(part[2] for part in parts)
            self.acc[0:GLOB, 0] += key_part.reshape(GLOB, BLK, width)
            self.acc[0:GLOB, 1] += value_part.reshape(GLOB, BLK, width)
            return carry

        lax.fori_loop(0, count // (chunk * turns), step, 0)

    def scattered(self, guest, low, fanout, near):
        who, whom, far = self.lists
        count = self.count

        def note(at, q, target):
            local = target - low
            hit = (local >= 0) & (local < self.held)
            who[at] = q
            whom[at] = local
            far[at] = 0.0
            return at + hit.astype(jnp.int32)

        def gather(q, at):
            block = guest * count + q
            for r in range(fanout):
                at = note(at, q, self.layout[block * fanout + r])
            return at

        found = lax.fori_loop(0, count, gather, 0)
        if near:
            found = note(found, 0, guest * count - 1)
            found = note(found, count - 1, (guest + 1) * count)
        for k in range(PAIRS - 1):
            who[found + k] = 0
            whom[found + k] = 0
            far[found + k] = FAR

        def step(g, carry):
            places, pairs = ([], [])
            for k in range(PAIRS):
                at = g * PAIRS + k
                places.append((who[at], whom[at]))
                pairs.append(self.pair(who[at], whom[at], 1, far[at]))
            parts = pair_grads(pairs, self.scaling)
            for (q, j), (query_part, key_part, value_part) in zip(places, parts):
                self.dq[q] += query_part
                self.acc[j, 0] += key_part
                self.acc[j, 1] += value_part
            return carry

        lax.fori_loop(0, (found + PAIRS - 1) // PAIRS, step, 0)

    def finish(self, out):
        def step(q, carry):
            out[q] = (self.dq[q] * self.scaling).astype(out.dtype)
            return carry

        lax.fori_loop(0, self.count, step, 0)


def own_kernel(unit, keyval, acc, dq, lse, delta):
    def clear(b, carry):
        acc[b] = jnp.zeros(acc.shape[1:], jnp.float32)
        return carry

    count = dq.shape[0]
    lax.fori_loop(0, count, clear, 0)
    own = Visitor(count, unit, lse, delta, dq, keyval, keyval, acc, values_at=count)
    own.begin()
    own.window()


def visit_kernel(plan, me_ref, layout, *refs):
    offsets, count, span, fanout = plan
    refs = list(refs)
    first = offsets == (0,)
    guests = [refs.pop(0) for _ in offsets]
    me = me_ref[0]
    shards = me_ref[1]
    seat = lax.rem(me, span)
    row = lax.div(me, span)
    low = row * span * count
    side = 1 - 2 * lax.rem(row, 2)
    if first:
        parts = [refs.pop(0) for _ in range(span)]
        acc_own, dq_own = (refs.pop(0), refs.pop(0))
        keys, values = (refs.pop(0), refs.pop(0))
    else:
        keys, values = (refs.pop(0), refs.pop(0))
        refs.pop(0)
    acc = refs.pop(0)
    outs = [refs.pop(0) for _ in offsets]
    sums = outs if first else [refs.pop(0) for _ in offsets]
    lse, delta = (refs.pop(0), refs.pop(0))
    lists = refs
    if first:

        def lay(b, carry):
            for m in range(span):
                there = jnp.bitwise_xor(seat, m) * count + b
                if m == 0:
                    acc[there] = acc_own[b]
                    sums[0][b] = dq_own[b]
                else:
                    acc[there] = jnp.zeros(acc.shape[1:], jnp.float32)
                there = pl.ds(pl.multiple_of(there * BLK, BLK), BLK)
                here = pl.ds(pl.multiple_of(b * BLK, BLK), BLK)
                keys[there, :] = parts[m][here, :]
                here = pl.ds(pl.multiple_of((count + b) * BLK, BLK), BLK)
                values[there, :] = parts[m][here, :]
            return carry

        lax.fori_loop(0, count, lay, 0)

    for v, offset in enumerate(offsets):
        guest = me + offset * span * side
        present = (guest >= 0) & (guest < shards)
        visitor = Visitor(count, guests[v], lse, delta, sums[v], keys, values, acc, layout, lists)

        @pl.when(present)
        def _(visitor=visitor, offset=offset, guest=guest, out=outs[v]):
            visitor.begin(offset != 0)
            @pl.when(row == 0)
            def _():
                visitor.anchors()

            visitor.scattered(guest, low, fanout, offset in (-1, 0, 1))
            visitor.finish(out)


def sum_of(m, which, b, acc, place, scaling, parts, arrived):
    total = acc[place, which]
    if which == 0:
        total = total * scaling
    for part, units in zip(parts, arrived):
        total = total + part[which, units.index(m), b].astype(jnp.float32)
    return total.astype(jnp.bfloat16)


def share_kernel(plan, me_ref, acc, *refs):
    span, wanted, arrived = plan
    parts, out = (refs[:-1], refs[-1])
    count = acc.shape[0] // span
    scaling = acc.shape[3] ** (-0.5)
    seat = lax.rem(me_ref[0], span)

    def step(b, carry):
        for k, m in enumerate(wanted):
            place = jnp.bitwise_xor(seat, m) * count + b
            for which in range(2):
                out[which, k, b] = sum_of(m, which, b, acc, place, scaling, parts, arrived)
        return carry

    lax.fori_loop(0, count, step, 0)


def finish_kernel(plan, me_ref, acc, *refs):
    span, arrived = plan
    parts, outs = (refs[: len(arrived)], refs[len(arrived) : len(arrived) + 2])
    held_s, sems = refs[len(arrived) + 2 :]
    count = acc.shape[0] // span
    scaling = acc.shape[3] ** (-0.5)
    seat = lax.rem(me_ref[0], span)
    groups = groups_of(count)
    group = count // groups
    copies = []
    for g in range(groups):
        for b in range(g * group, (g + 1) * group):
            for which in range(2):
                held_s[which, b * BLK : (b + 1) * BLK, :] = sum_of(
                    0, which, b, acc, seat * count + b, scaling, parts, arrived
                )
        for which in range(2):
            at = pl.ds(g * group * BLK, group * BLK)
            copies.append(
                pltpu.make_async_copy(
                    held_s.at[which, at], outs[which].at[at], sems.at[which, g]
                )
            )
            copies[-1].start()
    for copy in copies:
        copy.wait()


SMEM = pl.BlockSpec(memory_space=pltpu.SMEM)
VMEM = pl.BlockSpec(memory_space=pltpu.VMEM)


def own_visit(unit, keyval, count):
    width = unit.shape[1]
    stats = pltpu.VMEM((stat_rows(count), width), jnp.float32)
    return pl.pallas_call(
        own_kernel,
        out_shape=(
            jax.ShapeDtypeStruct((count, 2, BLK, width), jnp.float32),
            jax.ShapeDtypeStruct((count, BLK, width), jnp.float32),
        ),
        scratch_shapes=[stats, stats],
        compiler_params=pltpu.CompilerParams(vmem_limit_bytes=LIMIT),
        name="own",
    )(unit, keyval)


def share(me, acc, span, wanted, arrived, parts):
    held, _, _, width = acc.shape
    return pl.pallas_call(
        functools.partial(share_kernel, (span, wanted, arrived)),
        out_shape=jax.ShapeDtypeStruct((2, len(wanted), held // span, BLK, width), jnp.bfloat16),
        in_specs=[SMEM] + [VMEM] * (1 + len(parts)),
        out_specs=VMEM,
        compiler_params=pltpu.CompilerParams(vmem_limit_bytes=LIMIT),
        name="share",
    )(me, acc, *parts)


def finish(me, acc, span, arrived, parts):
    held, _, _, width = acc.shape
    count = held // span
    shape = (count * BLK, width)
    hbm = pl.BlockSpec(memory_space=pltpu.HBM)
    return pl.pallas_call(
        functools.partial(finish_kernel, (span, arrived)),
        out_shape=[jax.ShapeDtypeStruct(shape, jnp.bfloat16)] * 2,
        in_specs=[SMEM] + [VMEM] * (1 + len(parts)),
        out_specs=[hbm, hbm],
        scratch_shapes=[
            pltpu.VMEM((2,) + shape, jnp.bfloat16),
            pltpu.SemaphoreType.DMA((2, groups_of(count))),
        ],
        compiler_params=pltpu.CompilerParams(vmem_limit_bytes=LIMIT),
        name="finish",
    )(me, acc, *parts)


def add_kernel(base, *refs):
    parts, out = (refs[:-1], refs[-1])

    def step(b, carry):
        total = base[b]
        for part in parts:
            total = total + part[b].astype(jnp.float32)
        if len(out.shape) == 3:
            out[b] = total
        else:
            out[pl.ds(pl.multiple_of(b * BLK, BLK), BLK), :] = total.astype(out.dtype)
        return carry

    lax.fori_loop(0, base.shape[0], step, 0)


def add(base, parts, final, weight):
    count, _, width = base.shape
    if final:
        out = jax.ShapeDtypeStruct((count * BLK, width), jnp.bfloat16)
    else:
        out = jax.ShapeDtypeStruct(base.shape, jnp.float32)
    return pl.pallas_call(
        add_kernel,
        out_shape=out,
        cost_estimate=pl.CostEstimate(
            flops=weight * count * 10 * BLK * BLK * width, bytes_accessed=0, transcendentals=0
        ),
        compiler_params=pltpu.CompilerParams(vmem_limit_bytes=LIMIT),
        name="add",
    )(base, *parts)


def visit(me, layout, units, offsets, keyvals, acc, query_acc, weight, count, span, fanout):
    first = query_acc is not None
    width = units[0].shape[1]
    held = span * count
    plan = (offsets, count, span, fanout)
    operands = units + keyvals
    keys = jax.ShapeDtypeStruct((held * BLK, width), jnp.bfloat16)
    outs = [jax.ShapeDtypeStruct((held, 2, BLK, width), jnp.float32)]
    if first:
        outs = [keys, keys] + outs
        aliases = {}
        operands = operands + [acc, query_acc]
    else:
        aliases = {len(operands) + 2: 0}
        operands = operands + [placed(acc, pltpu.VMEM)]
    kind = jnp.float32 if first else jnp.bfloat16
    outs += [jax.ShapeDtypeStruct((count, BLK, width), kind)] * len(units)
    entries = count * fanout + 2 + PAIRS
    stats = pltpu.VMEM((stat_rows(count), width), jnp.float32)
    return list(
        pl.pallas_call(
            functools.partial(visit_kernel, plan),
            out_shape=outs,
            in_specs=[SMEM, SMEM] + [VMEM] * len(operands),
            out_specs=[VMEM] * len(outs),
            input_output_aliases=aliases,
            scratch_shapes=[pltpu.VMEM((count, BLK, width), jnp.float32)]
            * (0 if first else len(units))
            + [
                stats,
                stats,
                pltpu.SMEM((entries,), jnp.int32),
                pltpu.SMEM((entries,), jnp.int32),
                pltpu.SMEM((entries,), jnp.float32),
            ],
            compiler_params=pltpu.CompilerParams(vmem_limit_bytes=LIMIT),
            cost_estimate=pl.CostEstimate(
                flops=weight * count * 10 * BLK * BLK * width,
                bytes_accessed=0,
                transcendentals=len(offsets) * count * BLK * BLK,
            ),
            name="visit",
        )(me, layout, *operands)
    )


def body(query_rows, key_rows, value_rows, output_rows, output_grad, logsumexp, layout):
    shards = lax.axis_size("qb")
    myself = lax.axis_index("qb")
    width = query_rows.shape[1]
    count = query_rows.shape[0] // BLK
    fanout = layout.shape[1]
    span = 4
    while shards // span > 16:
        span = span * 2
    planes = shards // span

    def send(array, pairs):
        return lax.ppermute(array, "qb", pairs)

    def swap(array, bit):
        return send(array, [(i, i ^ bit) for i in range(shards)])

    def hop(s, odd, back=False):
        pairs = []
        for p in range(odd, planes - 1, 2):
            if p >= s - 1:
                pairs.append((p, p + 1))
            if p + 1 <= planes - s:
                pairs.append((p + 1, p))
        if back:
            pairs = [(q, p) for p, q in pairs]
        return [(p * span + e, q * span + e) for p, q in pairs for e in range(span)]

    me = jnp.stack([myself, jnp.int32(shards)]).astype(jnp.int32)
    entries = layout.reshape(-1)
    unit = pack(query_rows, output_grad, output_rows, logsumexp.reshape(count, BLK))
    keyval = join(key_rows, value_rows)

    def merge(one, two):
        return (one.astype(jnp.float32) + two.astype(jnp.float32)).astype(jnp.bfloat16)

    def tie(*arrays):
        return lax.optimization_barrier(arrays)

    last = planes - 1
    odd, even = (send(unit, hop(1, 1)), send(unit, hop(1, 0)))
    keyvals = {0: keyval}
    singles = [m for m in range(1, span) if m & (m - 1) == 0]
    for m in singles:
        keyvals[m] = swap(keyval, m)
    acc, query_acc = own_visit(unit, keyval, count)
    even, query_acc = tie(even, query_acc)
    for m in range(1, span):
        if m & (m - 1):
            keyvals[m] = swap(keyvals[m & (m - 1)], m & -m)
    keyvals = [keyvals[m] for m in range(span)]

    def meet(units, offsets, keyvals, acc, query_acc=None, weight=0):
        return visit(
            me, entries, units, offsets, keyvals, acc, query_acc, weight, count, span, fanout
        )

    keys, values, acc, query_acc = meet([unit], (0,), keyvals, acc, query_acc)
    ends = [(last * span + e, e) for e in range(span)]
    ends = ends + [(two, one) for one, two in ends]
    even_parts, odd_parts = ([], [])
    for s in range(1, last):
        if s + 1 < last:
            next_even, next_odd = (send(odd, hop(s + 1, 0)), send(even, hop(s + 1, 1)))
        else:
            odd, query_acc = tie(odd, query_acc)
            far = send(odd, hop(last, 0))
        if s + 2 == last:
            acc, next_even = tie(acc, next_even)
        acc, even_part, odd_part = meet([even, odd], (s, -s), [keys, values], acc)
        even_parts.append(even_part)
        odd_parts.append(odd_part)
        if s + 1 < last:
            even, odd = (next_even, next_odd)
    acc, far_part = meet([far], (last,), [keys, values], acc, None, COST)

    even_back, odd_back = (even_parts[-1], odd_parts[-1])
    for t in range(last - 1, 1, -1):
        even_back, odd_back = (send(even_back, hop(t, 0, True)), send(odd_back, hop(t, 1, True)))
        if t == 2:
            even_back, odd_back, far_part = tie(even_back, odd_back, far_part)
        even_back, odd_back = (
            merge(even_parts[t - 2], odd_back),
            merge(odd_parts[t - 2], even_back),
        )
    acc, even_back, odd_back = tie(acc, even_back, odd_back)
    backs = [send(even_back, hop(1, 0, True)), send(odd_back, hop(1, 1, True))]
    query_acc = add(query_acc, backs, False, COST)
    query_grad = add(query_acc, [send(far_part, ends)], True, 1)

    wanted = tuple(range(span))
    arrived, parts = ((), ())
    bit = 1
    while bit < span:
        theirs = tuple(m for m in wanted if m & bit)
        wanted = tuple(m for m in wanted if not m & bit)
        sent = share(me, acc, span, theirs, arrived, parts)
        arrived, parts = (arrived + (wanted,), parts + (swap(sent, bit),))
        bit = bit * 2
    *parts, query_grad = tie(*parts, query_grad)
    key_grad, value_grad = finish(me, acc, span, arrived, parts)
    return (query_grad, key_grad, value_grad)


def solution(mesh):
    in_specs = (
        P(("grp", "qb"), None),
        P(("grp", "qb"), None),
        P(("grp", "qb"), None),
        P(("grp", "qb"), None),
        P(("grp", "qb"), None),
        P(("grp", "qb")),
        P("grp", None),
    )
    out_specs = (P(("grp", "qb"), None), P(("grp", "qb"), None), P(("grp", "qb"), None))
    return jax.shard_map(body, mesh=mesh, in_specs=in_specs, out_specs=out_specs, check_vma=False)
```

```python
import functools

import jax
import jax.numpy as jnp
from jax import lax
from jax.experimental import pallas as pl
from jax.experimental.pallas import tpu as pltpu
from jax.sharding import PartitionSpec as P

BLK = 128
GLOB = 2
TILE = 16
CODE = 256
PAIRS = 6
TURNS = 3
FAR = 1e30
COST = 20
LIMIT = 16 * 2**20


def pieces(row):
    high = row.astype(jnp.bfloat16)
    rest = row - high.astype(jnp.float32)
    middle = rest.astype(jnp.bfloat16)
    low = (rest - middle.astype(jnp.float32)).astype(jnp.bfloat16)
    return [high.astype(jnp.float32), middle.astype(jnp.float32), low.astype(jnp.float32)]


def stat_rows(count):
    return -(-count // TILE) * TILE


def placed(array, space):
    return pltpu.with_memory_space_constraint(array, space)


def groups_of(count):
    return next(groups for groups in (3, 4, 2, 1) if count % groups == 0)


def pack_kernel(query, grad, output, lse_hbm, unit, output_s, lse, delta_s, sems):
    count, width = lse.shape
    rows = stat_rows(count)
    groups = groups_of(count)
    group = count // groups
    ones = jnp.ones((TILE, width), jnp.bfloat16)
    held = count * BLK
    loads = []
    for g in range(groups):
        at = pl.ds(g * group * BLK, group * BLK)
        after = pl.ds(held + g * group * BLK, group * BLK)
        loads.append(
            [
                pltpu.make_async_copy(grad.at[at], unit.at[after], sems.at[0, g]),
                pltpu.make_async_copy(output.at[at], output_s.at[at], sems.at[1, g]),
                pltpu.make_async_copy(query.at[at], unit.at[at], sems.at[2, g]),
            ]
        )
    lines = pltpu.make_async_copy(lse_hbm, lse, sems.at[3, 0])
    lines.start()
    for kind in range(3):
        for load in loads:
            load[kind].start()

    def total(part):
        return lax.dot_general(
            ones, part, (((1,), (1,)), ((), ())), preferred_element_type=jnp.float32
        )

    delta_s[...] = jnp.zeros(delta_s.shape, jnp.float32)
    for g in range(groups):
        loads[g][0].wait()
        loads[g][1].wait()
        highs, lows = ([], [])
        for k in range(g * group, (g + 1) * group):
            grads = unit[held + k * BLK : held + (k + 1) * BLK, :].astype(jnp.float32)
            product = grads * output_s[k * BLK : (k + 1) * BLK, :].astype(jnp.float32)
            highs.append(product.astype(jnp.bfloat16))
            lows.append((product - highs[-1].astype(jnp.float32)).astype(jnp.bfloat16))
        sums = [total(high) + total(low) for high, low in zip(highs, lows)]
        for k in range(group):
            delta_s[g * group + k : g * group + k + 1, :] = sums[k][0:1]
    lines.wait()
    lines = lse[...]
    if rows > count:
        lines = jnp.concatenate([lines, jnp.zeros((rows - count, width), jnp.float32)], 0)
    stats = pieces(lines) + pieces(delta_s[...])
    unit[2 * held :, :] = jnp.concatenate(stats, 0).astype(jnp.bfloat16)
    for load in loads:
        load[2].wait()


def pack(query, grad, output, lse):
    count, width = lse.shape
    rows = stat_rows(count)
    hbm = pl.BlockSpec(memory_space=pltpu.HBM)
    return pl.pallas_call(
        pack_kernel,
        out_shape=jax.ShapeDtypeStruct((2 * count * BLK + 6 * rows, width), jnp.bfloat16),
        in_specs=[hbm] * 4,
        out_specs=pl.BlockSpec(memory_space=pltpu.VMEM),
        scratch_shapes=[
            pltpu.VMEM(query.shape, jnp.bfloat16),
            pltpu.VMEM(lse.shape, jnp.float32),
            pltpu.VMEM((rows, width), jnp.float32),
            pltpu.SemaphoreType.DMA((4, groups_of(count))),
        ],
        compiler_params=pltpu.CompilerParams(vmem_limit_bytes=LIMIT),
        name="pack",
    )(*[placed(array, pltpu.HBM) for array in (query, grad, output, lse)])


def join_kernel(key, value, keyval, sems):
    rows = key.shape[0]
    copies = [
        pltpu.make_async_copy(key, keyval.at[pl.ds(0, rows)], sems.at[0]),
        pltpu.make_async_copy(value, keyval.at[pl.ds(rows, rows)], sems.at[1]),
    ]
    for copy in copies:
        copy.start()
    for copy in copies:
        copy.wait()


def join(key, value):
    rows, width = key.shape
    hbm = pl.BlockSpec(memory_space=pltpu.HBM)
    return pl.pallas_call(
        join_kernel,
        out_shape=jax.ShapeDtypeStruct((2 * rows, width), key.dtype),
        in_specs=[hbm, hbm],
        out_specs=pl.BlockSpec(memory_space=pltpu.VMEM),
        scratch_shapes=[pltpu.SemaphoreType.DMA((2,))],
        compiler_params=pltpu.CompilerParams(vmem_limit_bytes=LIMIT),
        name="join",
    )(placed(key, pltpu.HBM), placed(value, pltpu.HBM))


def pair_grads(pairs, scaling):
    def outer(one, two):
        return lax.dot_general(
            one, two, (((1,), (1,)), ((), ())), preferred_element_type=jnp.float32
        )

    def inner(one, two):
        return jnp.dot(one, two, preferred_element_type=jnp.float32)

    def flipped(one, two):
        return lax.dot_general(
            one, two, (((0,), (0,)), ((), ())), preferred_element_type=jnp.float32
        )

    scores = [outer(keys, queries) for keys, _, queries, _, _, _, _ in pairs]
    dweights = [outer(values, grads) for _, values, _, grads, _, _, _ in pairs]
    probs = []
    for score, (_, _, _, _, lse, _, mask) in zip(scores, pairs):
        prob = jnp.exp(score * scaling - lse)
        probs.append(prob if mask is None else jnp.where(mask, prob, 0.0))
    prob_lows = [prob.astype(jnp.bfloat16) for prob in probs]
    score_lows = [
        (prob * (dweight - pair[5])).astype(jnp.bfloat16)
        for prob, dweight, pair in zip(probs, dweights, pairs)
    ]
    value_parts = [inner(low, pair[3]) for low, pair in zip(prob_lows, pairs)]
    key_parts = [inner(low, pair[2]) for low, pair in zip(score_lows, pairs)]
    query_parts = [flipped(low, pair[0]) for low, pair in zip(score_lows, pairs)]
    return list(zip(query_parts, key_parts, value_parts))


class Visitor:
    def __init__(
        self, count, unit, lse, delta, dq, keys, values, acc, layout=None, lists=None, values_at=0
    ):
        self.count = count
        self.unit, self.lse, self.delta = (unit, lse, delta)
        self.dq, self.keys, self.values, self.acc = (dq, keys, values, acc)
        self.layout, self.lists, self.values_at = (layout, lists, values_at)
        self.width = unit.shape[1]
        self.scaling = self.width ** (-0.5)

    def begin(self, clear=True):
        count = self.count
        rows = stat_rows(count)
        stats = self.unit[2 * count * BLK :, :].astype(jnp.float32)
        lines = [stats[k * rows : (k + 1) * rows] for k in range(6)]
        self.lse[...] = lines[0] + lines[1] + lines[2]
        self.delta[...] = lines[3] + lines[4] + lines[5]

        def step(q, carry):
            self.dq[q] = jnp.zeros(self.dq.shape[1:], jnp.float32)
            return carry

        if clear:
            lax.fori_loop(0, count, step, 0)

    def rows(self, array, block, blocks=1):
        return array[pl.ds(pl.multiple_of(block * BLK, BLK), blocks * BLK), :]

    def pair(self, q, j, keys=1, shift=0.0, mask=None):
        return (
            self.rows(self.keys, j, keys),
            self.rows(self.values, self.values_at + j, keys),
            self.rows(self.unit, q),
            self.rows(self.unit, self.count + q),
            self.lse[pl.ds(q, 1), :] + shift,
            self.delta[pl.ds(q, 1), :],
            mask,
        )

    def window(self):
        count, width = (self.count, self.width)
        chunk = 2 if count % 2 == 0 else 1

        def step(c, carry):
            places, pairs = ([], [])
            for k in range(chunk):
                q = c * chunk + k
                start = jnp.clip(q - 1, 0, count - 3)
                block = lax.broadcasted_iota(jnp.int32, (3 * BLK, BLK), 0) // BLK
                block = block + start - q
                places.append((q, start))
                pairs.append(self.pair(q, start, 3, 0.0, (block >= -1) & (block <= 1)))
            parts = pair_grads(pairs, self.scaling)
            for (q, start), (query_part, key_part, value_part) in zip(places, parts):
                self.dq[q] += query_part
                self.acc[pl.ds(start, 3), 0] += key_part.reshape(3, BLK, width)
                self.acc[pl.ds(start, 3), 1] += value_part.reshape(3, BLK, width)
            return carry

        lax.fori_loop(0, count // chunk, step, 0)

    def anchors(self, base):
        count, width = (self.count, self.width)
        chunk = 2 if count % 2 == 0 else 1
        turns = next(turns for turns in (TURNS, 2, 1) if count % (turns * chunk) == 0)
        globals_ = pl.ds(base, GLOB)

        def step(c, carry):
            places, pairs = ([], [])
            for k in range(turns):
                at = (c * turns + k) * chunk
                places.append(pl.ds(at, chunk))
                pairs.append(
                    (
                        self.rows(self.keys, base, GLOB),
                        self.rows(self.values, base, GLOB),
                        self.rows(self.unit, at, chunk),
                        self.rows(self.unit, count + at, chunk),
                        jnp.concatenate(
                            [self.lse[pl.ds(at + i, 1), :] for i in range(chunk)], 1
                        ),
                        jnp.concatenate(
                            [self.delta[pl.ds(at + i, 1), :] for i in range(chunk)], 1
                        ),
                        None,
                    )
                )
            parts = pair_grads(pairs, self.scaling)
            for blocks, (query_part, _, _) in zip(places, parts):
                self.dq[blocks] += query_part.reshape(chunk, BLK, width)
            key_part = sum(part[1] for part in parts)
            value_part = sum(part[2] for part in parts)
            self.acc[globals_, 0] += key_part.reshape(GLOB, BLK, width)
            self.acc[globals_, 1] += value_part.reshape(GLOB, BLK, width)
            return carry

        lax.fori_loop(0, count // (chunk * turns), step, 0)

    def scattered(self, guest, me, span, fanout, near):
        who, whom, far = self.lists
        count = self.count

        def note(at, q, owner, block):
            unit = jnp.bitwise_xor(owner, me)
            hit = (unit >= 0) & (unit < span)
            who[at] = q
            whom[at] = unit * count + block
            far[at] = 0.0
            return at + hit.astype(jnp.int32)

        def gather(q, at):
            entry = (guest * count + q) * fanout
            for r in range(fanout):
                code = self.layout[entry + r]
                at = note(at, q, lax.shift_right_logical(code, CODE.bit_length() - 1), code & (CODE - 1))
            return at

        found = lax.fori_loop(0, count, gather, 0)
        if near:
            found = note(found, 0, guest - 1, count - 1)
            found = note(found, count - 1, guest + 1, 0)
        for k in range(PAIRS - 1):
            who[found + k] = 0
            whom[found + k] = 0
            far[found + k] = FAR

        def step(g, carry):
            places, pairs = ([], [])
            for k in range(PAIRS):
                at = g * PAIRS + k
                places.append((who[at], whom[at]))
                pairs.append(self.pair(who[at], whom[at], 1, far[at]))
            parts = pair_grads(pairs, self.scaling)
            for (q, j), (query_part, key_part, value_part) in zip(places, parts):
                self.dq[q] += query_part
                self.acc[j, 0] += key_part
                self.acc[j, 1] += value_part
            return carry

        lax.fori_loop(0, (found + PAIRS - 1) // PAIRS, step, 0)

    def finish(self, out):
        def step(q, carry):
            out[q] = (self.dq[q] * self.scaling).astype(out.dtype)
            return carry

        lax.fori_loop(0, self.count, step, 0)


def own_kernel(unit, keyval, acc, dq, lse, delta):
    def clear(b, carry):
        acc[b] = jnp.zeros(acc.shape[1:], jnp.float32)
        return carry

    count = dq.shape[0]
    lax.fori_loop(0, count, clear, 0)
    own = Visitor(count, unit, lse, delta, dq, keyval, keyval, acc, values_at=count)
    own.begin()
    own.window()


def visit_kernel(plan, me_ref, layout, *refs):
    offsets, count, span, fanout = plan
    refs = list(refs)
    first = offsets == (0,)
    guests = [refs.pop(0) for _ in offsets]
    me = me_ref[0]
    shards = me_ref[1]
    seat = lax.rem(me, span)
    row = lax.div(me, span)
    side = 1 - 2 * lax.rem(row, 2)
    if first:
        parts = [refs.pop(0) for _ in range(span)]
        acc_own, dq_own = (refs.pop(0), refs.pop(0))
        keys, values = (refs.pop(0), refs.pop(0))
    else:
        keys, values = (refs.pop(0), refs.pop(0))
        refs.pop(0)
    acc = refs.pop(0)
    outs = [refs.pop(0) for _ in offsets]
    sums = outs if first else [refs.pop(0) for _ in offsets]
    lse, delta = (refs.pop(0), refs.pop(0))
    lists = refs
    if first:

        def lay(b, carry):
            for m in range(span):
                there = m * count + b
                if m == 0:
                    acc[there] = acc_own[b]
                    sums[0][b] = dq_own[b]
                else:
                    acc[there] = jnp.zeros(acc.shape[1:], jnp.float32)
                there = pl.ds(pl.multiple_of(there * BLK, BLK), BLK)
                here = pl.ds(pl.multiple_of(b * BLK, BLK), BLK)
                keys[there, :] = parts[m][here, :]
                here = pl.ds(pl.multiple_of((count + b) * BLK, BLK), BLK)
                values[there, :] = parts[m][here, :]
            return carry

        lax.fori_loop(0, count, lay, 0)

    for v, offset in enumerate(offsets):
        guest = me + offset * span * side
        present = (guest >= 0) & (guest < shards)
        visitor = Visitor(count, guests[v], lse, delta, sums[v], keys, values, acc, layout, lists)

        @pl.when(present)
        def _(visitor=visitor, offset=offset, guest=guest, out=outs[v]):
            visitor.begin(offset != 0)
            @pl.when(row == 0)
            def _():
                visitor.anchors(seat * count)

            visitor.scattered(guest, me, span, fanout, offset in (-1, 0, 1))
            visitor.finish(out)


def sum_of(m, which, b, acc, place, scaling, parts, arrived):
    total = acc[place, which]
    if which == 0:
        total = total * scaling
    for part, units in zip(parts, arrived):
        total = total + part[which, units.index(m), b].astype(jnp.float32)
    return total.astype(jnp.bfloat16)


def share_kernel(plan, acc, *refs):
    span, wanted, arrived = plan
    parts, out = (refs[:-1], refs[-1])
    count = acc.shape[0] // span
    scaling = acc.shape[3] ** (-0.5)

    def step(b, carry):
        for k, m in enumerate(wanted):
            place = m * count + b
            for which in range(2):
                out[which, k, b] = sum_of(m, which, b, acc, place, scaling, parts, arrived)
        return carry

    lax.fori_loop(0, count, step, 0)


def finish_kernel(plan, acc, *refs):
    span, arrived = plan
    parts, outs = (refs[: len(arrived)], refs[len(arrived) : len(arrived) + 2])
    held_s, sems = refs[len(arrived) + 2 :]
    count = acc.shape[0] // span
    scaling = acc.shape[3] ** (-0.5)
    groups = groups_of(count)
    group = count // groups
    copies = []
    for g in range(groups):
        for b in range(g * group, (g + 1) * group):
            for which in range(2):
                held_s[which, b * BLK : (b + 1) * BLK, :] = sum_of(
                    0, which, b, acc, b, scaling, parts, arrived
                )
        for which in range(2):
            at = pl.ds(g * group * BLK, group * BLK)
            copies.append(
                pltpu.make_async_copy(
                    held_s.at[which, at], outs[which].at[at], sems.at[which, g]
                )
            )
            copies[-1].start()
    for copy in copies:
        copy.wait()


SMEM = pl.BlockSpec(memory_space=pltpu.SMEM)
VMEM = pl.BlockSpec(memory_space=pltpu.VMEM)


def own_visit(unit, keyval, count):
    width = unit.shape[1]
    stats = pltpu.VMEM((stat_rows(count), width), jnp.float32)
    return pl.pallas_call(
        own_kernel,
        out_shape=(
            jax.ShapeDtypeStruct((count, 2, BLK, width), jnp.float32),
            jax.ShapeDtypeStruct((count, BLK, width), jnp.float32),
        ),
        scratch_shapes=[stats, stats],
        compiler_params=pltpu.CompilerParams(vmem_limit_bytes=LIMIT),
        name="own",
    )(unit, keyval)


def share(acc, span, wanted, arrived, parts):
    held, _, _, width = acc.shape
    return pl.pallas_call(
        functools.partial(share_kernel, (span, wanted, arrived)),
        out_shape=jax.ShapeDtypeStruct((2, len(wanted), held // span, BLK, width), jnp.bfloat16),
        in_specs=[VMEM] * (1 + len(parts)),
        out_specs=VMEM,
        compiler_params=pltpu.CompilerParams(vmem_limit_bytes=LIMIT),
        name="share",
    )(acc, *parts)


def finish(acc, span, arrived, parts):
    held, _, _, width = acc.shape
    count = held // span
    shape = (count * BLK, width)
    hbm = pl.BlockSpec(memory_space=pltpu.HBM)
    return pl.pallas_call(
        functools.partial(finish_kernel, (span, arrived)),
        out_shape=[jax.ShapeDtypeStruct(shape, jnp.bfloat16)] * 2,
        in_specs=[VMEM] * (1 + len(parts)),
        out_specs=[hbm, hbm],
        scratch_shapes=[
            pltpu.VMEM((2,) + shape, jnp.bfloat16),
            pltpu.SemaphoreType.DMA((2, groups_of(count))),
        ],
        compiler_params=pltpu.CompilerParams(vmem_limit_bytes=LIMIT),
        name="finish",
    )(acc, *parts)


def add_kernel(base, *refs):
    parts, out = (refs[:-1], refs[-1])

    def step(b, carry):
        total = base[b]
        for part in parts:
            total = total + part[b].astype(jnp.float32)
        if len(out.shape) == 3:
            out[b] = total
        else:
            out[pl.ds(pl.multiple_of(b * BLK, BLK), BLK), :] = total.astype(out.dtype)
        return carry

    lax.fori_loop(0, base.shape[0], step, 0)


def add(base, parts, final, weight):
    count, _, width = base.shape
    if final:
        out = jax.ShapeDtypeStruct((count * BLK, width), jnp.bfloat16)
    else:
        out = jax.ShapeDtypeStruct(base.shape, jnp.float32)
    return pl.pallas_call(
        add_kernel,
        out_shape=out,
        cost_estimate=pl.CostEstimate(
            flops=weight * count * 10 * BLK * BLK * width, bytes_accessed=0, transcendentals=0
        ),
        compiler_params=pltpu.CompilerParams(vmem_limit_bytes=LIMIT),
        name="add",
    )(base, *parts)


def visit(me, layout, units, offsets, keyvals, acc, query_acc, weight, count, span, fanout):
    first = query_acc is not None
    width = units[0].shape[1]
    held = span * count
    plan = (offsets, count, span, fanout)
    operands = units + keyvals
    keys = jax.ShapeDtypeStruct((held * BLK, width), jnp.bfloat16)
    outs = [jax.ShapeDtypeStruct((held, 2, BLK, width), jnp.float32)]
    if first:
        outs = [keys, keys] + outs
        aliases = {}
        operands = operands + [acc, query_acc]
    else:
        aliases = {len(operands) + 2: 0}
        operands = operands + [placed(acc, pltpu.VMEM)]
    kind = jnp.float32 if first else jnp.bfloat16
    outs += [jax.ShapeDtypeStruct((count, BLK, width), kind)] * len(units)
    entries = count * fanout + 2 + PAIRS
    stats = pltpu.VMEM((stat_rows(count), width), jnp.float32)
    return list(
        pl.pallas_call(
            functools.partial(visit_kernel, plan),
            out_shape=outs,
            in_specs=[SMEM, SMEM] + [VMEM] * len(operands),
            out_specs=[VMEM] * len(outs),
            input_output_aliases=aliases,
            scratch_shapes=[pltpu.VMEM((count, BLK, width), jnp.float32)]
            * (0 if first else len(units))
            + [
                stats,
                stats,
                pltpu.SMEM((entries,), jnp.int32),
                pltpu.SMEM((entries,), jnp.int32),
                pltpu.SMEM((entries,), jnp.float32),
            ],
            compiler_params=pltpu.CompilerParams(vmem_limit_bytes=LIMIT),
            cost_estimate=pl.CostEstimate(
                flops=weight * count * 10 * BLK * BLK * width,
                bytes_accessed=0,
                transcendentals=len(offsets) * count * BLK * BLK,
            ),
            name="visit",
        )(me, layout, *operands)
    )


def body(query_rows, key_rows, value_rows, output_rows, output_grad, logsumexp, layout):
    shards = lax.axis_size("qb")
    myself = lax.axis_index("qb")
    width = query_rows.shape[1]
    count = query_rows.shape[0] // BLK
    fanout = layout.shape[1]
    span = 4
    while shards // span > 16:
        span = span * 2
    planes = shards // span

    def send(array, pairs):
        return lax.ppermute(array, "qb", pairs)

    def swap(array, bit):
        return send(array, [(i, i ^ bit) for i in range(shards)])

    def hop(s, odd, back=False):
        pairs = []
        for p in range(odd, planes - 1, 2):
            if p >= s - 1:
                pairs.append((p, p + 1))
            if p + 1 <= planes - s:
                pairs.append((p + 1, p))
        if back:
            pairs = [(q, p) for p, q in pairs]
        return [(p * span + e, q * span + e) for p, q in pairs for e in range(span)]

    me = jnp.stack([myself, jnp.int32(shards)]).astype(jnp.int32)
    entries = (layout // count * CODE + layout % count).reshape(-1)
    unit = pack(query_rows, output_grad, output_rows, logsumexp.reshape(count, BLK))
    keyval = join(key_rows, value_rows)

    def merge(one, two):
        return (one.astype(jnp.float32) + two.astype(jnp.float32)).astype(jnp.bfloat16)

    def tie(*arrays):
        return lax.optimization_barrier(arrays)

    last = planes - 1
    odd, even = (send(unit, hop(1, 1)), send(unit, hop(1, 0)))
    keyvals = {0: keyval}
    singles = [m for m in range(1, span) if m & (m - 1) == 0]
    for m in singles:
        keyvals[m] = swap(keyval, m)
    acc, query_acc = own_visit(unit, keyval, count)
    even, query_acc = tie(even, query_acc)
    for m in range(1, span):
        if m & (m - 1):
            keyvals[m] = swap(keyvals[m & (m - 1)], m & -m)
    keyvals = [keyvals[m] for m in range(span)]

    def meet(units, offsets, keyvals, acc, query_acc=None, weight=0):
        return visit(
            me, entries, units, offsets, keyvals, acc, query_acc, weight, count, span, fanout
        )

    keys, values, acc, query_acc = meet([unit], (0,), keyvals, acc, query_acc)
    ends = [(last * span + e, e) for e in range(span)]
    ends = ends + [(two, one) for one, two in ends]
    even_parts, odd_parts = ([], [])
    for s in range(1, last):
        if s + 1 < last:
            next_even, next_odd = (send(odd, hop(s + 1, 0)), send(even, hop(s + 1, 1)))
        else:
            odd, query_acc = tie(odd, query_acc)
            far = send(odd, hop(last, 0))
        if s + 2 == last:
            acc, next_even = tie(acc, next_even)
        acc, even_part, odd_part = meet([even, odd], (s, -s), [keys, values], acc)
        even_parts.append(even_part)
        odd_parts.append(odd_part)
        if s + 1 < last:
            even, odd = (next_even, next_odd)
    acc, far_part = meet([far], (last,), [keys, values], acc, None, COST)

    even_back, odd_back = (even_parts[-1], odd_parts[-1])
    for t in range(last - 1, 1, -1):
        even_back, odd_back = (send(even_back, hop(t, 0, True)), send(odd_back, hop(t, 1, True)))
        if t == 2:
            even_back, odd_back, far_part = tie(even_back, odd_back, far_part)
        even_back, odd_back = (
            merge(even_parts[t - 2], odd_back),
            merge(odd_parts[t - 2], even_back),
        )
    acc, even_back, odd_back = tie(acc, even_back, odd_back)
    backs = [send(even_back, hop(1, 0, True)), send(odd_back, hop(1, 1, True))]
    query_acc = add(query_acc, backs, False, COST)
    query_grad = add(query_acc, [send(far_part, ends)], True, 1)

    wanted = tuple(range(span))
    arrived, parts = ((), ())
    bit = 1
    while bit < span:
        theirs = tuple(m for m in wanted if m & bit)
        wanted = tuple(m for m in wanted if not m & bit)
        sent = share(acc, span, theirs, arrived, parts)
        arrived, parts = (arrived + (wanted,), parts + (swap(sent, bit),))
        bit = bit * 2
    *parts, query_grad = tie(*parts, query_grad)
    key_grad, value_grad = finish(acc, span, arrived, parts)
    return (query_grad, key_grad, value_grad)


def solution(mesh):
    in_specs = (
        P(("grp", "qb"), None),
        P(("grp", "qb"), None),
        P(("grp", "qb"), None),
        P(("grp", "qb"), None),
        P(("grp", "qb"), None),
        P(("grp", "qb")),
        P("grp", None),
    )
    out_specs = (P(("grp", "qb"), None), P(("grp", "qb"), None), P(("grp", "qb"), None))
    return jax.shard_map(body, mesh=mesh, in_specs=in_specs, out_specs=out_specs, check_vma=False)
```

```python
import functools

import jax
import jax.numpy as jnp
from jax import lax
from jax.experimental import pallas as pl
from jax.experimental.pallas import tpu as pltpu
from jax.sharding import PartitionSpec as P

BLK = 128
GLOB = 2
TILE = 16
CODE = 256
PAIRS = 6
TURNS = 3
FAR = 1e30
COST = 20
LIMIT = 16 * 2**20


def pieces(row):
    high = row.astype(jnp.bfloat16).astype(jnp.float32)
    return [high, row - high]


def stat_rows(count):
    return -(-4 * count // TILE) * TILE


def placed(array, space):
    return pltpu.with_memory_space_constraint(array, space)


def groups_of(count):
    return next(groups for groups in (3, 4, 2, 1) if count % groups == 0)


def pack_kernel(query, grad, output, lse_hbm, unit, output_s, lse, delta_s, stat_s, sems):
    count, width = lse.shape
    groups = groups_of(count)
    group = count // groups
    ones = jnp.ones((TILE, width), jnp.bfloat16)
    held = count * BLK
    loads = []
    for g in range(groups):
        at = pl.ds(g * group * BLK, group * BLK)
        after = pl.ds(held + g * group * BLK, group * BLK)
        loads.append(
            [
                pltpu.make_async_copy(grad.at[at], unit.at[after], sems.at[0, g]),
                pltpu.make_async_copy(output.at[at], output_s.at[at], sems.at[1, g]),
                pltpu.make_async_copy(query.at[at], unit.at[at], sems.at[2, g]),
            ]
        )
    lines = pltpu.make_async_copy(lse_hbm, lse, sems.at[3, 0])
    lines.start()
    for kind in range(3):
        for load in loads:
            load[kind].start()

    def total(part):
        return lax.dot_general(
            ones, part, (((1,), (1,)), ((), ())), preferred_element_type=jnp.float32
        )

    for g in range(groups):
        loads[g][0].wait()
        loads[g][1].wait()
        highs, lows = ([], [])
        for k in range(g * group, (g + 1) * group):
            grads = unit[held + k * BLK : held + (k + 1) * BLK, :].astype(jnp.float32)
            product = grads * output_s[k * BLK : (k + 1) * BLK, :].astype(jnp.float32)
            highs.append(product.astype(jnp.bfloat16))
            lows.append((product - highs[-1].astype(jnp.float32)).astype(jnp.bfloat16))
        sums = [total(high) + total(low) for high, low in zip(highs, lows)]
        for k in range(group):
            delta_s[g * group + k : g * group + k + 1, :] = sums[k][0:1]
    lines.wait()
    stat_s[...] = jnp.zeros(stat_s.shape, jnp.float32)
    for k, line in enumerate(pieces(lse[...]) + pieces(delta_s[...])):
        stat_s[k * count : (k + 1) * count, :] = line
    unit[2 * held :, :] = stat_s[...].astype(jnp.bfloat16)
    for load in loads:
        load[2].wait()


def pack(query, grad, output, lse):
    count, width = lse.shape
    rows = stat_rows(count)
    hbm = pl.BlockSpec(memory_space=pltpu.HBM)
    return pl.pallas_call(
        pack_kernel,
        out_shape=jax.ShapeDtypeStruct((2 * count * BLK + rows, width), jnp.bfloat16),
        in_specs=[hbm] * 4,
        out_specs=pl.BlockSpec(memory_space=pltpu.VMEM),
        scratch_shapes=[
            pltpu.VMEM(query.shape, jnp.bfloat16),
            pltpu.VMEM(lse.shape, jnp.float32),
            pltpu.VMEM(lse.shape, jnp.float32),
            pltpu.VMEM((rows, width), jnp.float32),
            pltpu.SemaphoreType.DMA((4, groups_of(count))),
        ],
        compiler_params=pltpu.CompilerParams(vmem_limit_bytes=LIMIT),
        name="pack",
    )(*[placed(array, pltpu.HBM) for array in (query, grad, output, lse)])


def join_kernel(key, value, keyval, sems):
    rows = key.shape[0]
    copies = [
        pltpu.make_async_copy(key, keyval.at[pl.ds(0, rows)], sems.at[0]),
        pltpu.make_async_copy(value, keyval.at[pl.ds(rows, rows)], sems.at[1]),
    ]
    for copy in copies:
        copy.start()
    for copy in copies:
        copy.wait()


def join(key, value):
    rows, width = key.shape
    hbm = pl.BlockSpec(memory_space=pltpu.HBM)
    return pl.pallas_call(
        join_kernel,
        out_shape=jax.ShapeDtypeStruct((2 * rows, width), key.dtype),
        in_specs=[hbm, hbm],
        out_specs=pl.BlockSpec(memory_space=pltpu.VMEM),
        scratch_shapes=[pltpu.SemaphoreType.DMA((2,))],
        compiler_params=pltpu.CompilerParams(vmem_limit_bytes=LIMIT),
        name="join",
    )(placed(key, pltpu.HBM), placed(value, pltpu.HBM))


def pair_grads(pairs, scaling):
    def outer(one, two):
        return lax.dot_general(
            one, two, (((1,), (1,)), ((), ())), preferred_element_type=jnp.float32
        )

    def inner(one, two):
        return jnp.dot(one, two, preferred_element_type=jnp.float32)

    def flipped(one, two):
        return lax.dot_general(
            one, two, (((0,), (0,)), ((), ())), preferred_element_type=jnp.float32
        )

    scores = [outer(keys, queries) for keys, _, queries, _, _, _, _ in pairs]
    dweights = [outer(values, grads) for _, values, _, grads, _, _, _ in pairs]
    probs = []
    for score, (_, _, _, _, lse, _, mask) in zip(scores, pairs):
        prob = jnp.exp(score * scaling - lse)
        probs.append(prob if mask is None else jnp.where(mask, prob, 0.0))
    prob_lows = [prob.astype(jnp.bfloat16) for prob in probs]
    score_lows = [
        (prob * (dweight - pair[5])).astype(jnp.bfloat16)
        for prob, dweight, pair in zip(probs, dweights, pairs)
    ]
    value_parts = [inner(low, pair[3]) for low, pair in zip(prob_lows, pairs)]
    key_parts = [inner(low, pair[2]) for low, pair in zip(score_lows, pairs)]
    query_parts = [flipped(low, pair[0]) for low, pair in zip(score_lows, pairs)]
    return list(zip(query_parts, key_parts, value_parts))


class Visitor:
    def __init__(
        self, count, unit, stat, dq, keys, values, acc, layout=None, lists=None, values_at=0
    ):
        self.count = count
        self.unit, self.stat = (unit, stat)
        self.dq, self.keys, self.values, self.acc = (dq, keys, values, acc)
        self.layout, self.lists, self.values_at = (layout, lists, values_at)
        self.width = unit.shape[1]
        self.scaling = self.width ** (-0.5)

    def begin(self, clear=True):
        count = self.count
        self.stat[...] = self.unit[2 * count * BLK :, :].astype(jnp.float32)

        def step(q, carry):
            self.dq[q] = jnp.zeros(self.dq.shape[1:], jnp.float32)
            return carry

        if clear:
            lax.fori_loop(0, count, step, 0)

    def rows(self, array, block, blocks=1):
        return array[pl.ds(pl.multiple_of(block * BLK, BLK), blocks * BLK), :]

    def line(self, q, kind):
        at = 2 * kind * self.count + q
        return self.stat[pl.ds(at, 1), :] + self.stat[pl.ds(at + self.count, 1), :]

    def pair(self, q, j, keys=1, shift=0.0, mask=None):
        return (
            self.rows(self.keys, j, keys),
            self.rows(self.values, self.values_at + j, keys),
            self.rows(self.unit, q),
            self.rows(self.unit, self.count + q),
            self.line(q, 0) + shift,
            self.line(q, 1),
            mask,
        )

    def window(self):
        count, width = (self.count, self.width)
        chunk = 2 if count % 2 == 0 else 1

        def step(c, carry):
            places, pairs = ([], [])
            for k in range(chunk):
                q = c * chunk + k
                start = jnp.clip(q - 1, 0, count - 3)
                block = lax.broadcasted_iota(jnp.int32, (3 * BLK, BLK), 0) // BLK
                block = block + start - q
                places.append((q, start))
                pairs.append(self.pair(q, start, 3, 0.0, (block >= -1) & (block <= 1)))
            parts = pair_grads(pairs, self.scaling)
            for (q, start), (query_part, key_part, value_part) in zip(places, parts):
                self.dq[q] += query_part
                self.acc[pl.ds(start, 3), 0] += key_part.reshape(3, BLK, width)
                self.acc[pl.ds(start, 3), 1] += value_part.reshape(3, BLK, width)
            return carry

        lax.fori_loop(0, count // chunk, step, 0)

    def anchors(self, base):
        count, width = (self.count, self.width)
        chunk = 2 if count % 2 == 0 else 1
        turns = next(turns for turns in (TURNS, 2, 1) if count % (turns * chunk) == 0)
        globals_ = pl.ds(base, GLOB)

        def step(c, carry):
            places, pairs = ([], [])
            for k in range(turns):
                at = (c * turns + k) * chunk
                places.append(pl.ds(at, chunk))
                pairs.append(
                    (
                        self.rows(self.keys, base, GLOB),
                        self.rows(self.values, base, GLOB),
                        self.rows(self.unit, at, chunk),
                        self.rows(self.unit, count + at, chunk),
                        jnp.concatenate(
                            [self.line(at + i, 0) for i in range(chunk)], 1
                        ),
                        jnp.concatenate(
                            [self.line(at + i, 1) for i in range(chunk)], 1
                        ),
                        None,
                    )
                )
            parts = pair_grads(pairs, self.scaling)
            for blocks, (query_part, _, _) in zip(places, parts):
                self.dq[blocks] += query_part.reshape(chunk, BLK, width)
            key_part = sum(part[1] for part in parts)
            value_part = sum(part[2] for part in parts)
            self.acc[globals_, 0] += key_part.reshape(GLOB, BLK, width)
            self.acc[globals_, 1] += value_part.reshape(GLOB, BLK, width)
            return carry

        lax.fori_loop(0, count // (chunk * turns), step, 0)

    def scattered(self, guest, me, span, fanout, near):
        who, whom, far = self.lists
        count = self.count

        def note(at, q, owner, block):
            unit = jnp.bitwise_xor(owner, me)
            hit = (unit >= 0) & (unit < span)
            who[at] = q
            whom[at] = unit * count + block
            far[at] = 0.0
            return at + hit.astype(jnp.int32)

        def gather(q, at):
            entry = (guest * count + q) * fanout
            for r in range(fanout):
                code = self.layout[entry + r]
                at = note(at, q, lax.shift_right_logical(code, CODE.bit_length() - 1), code & (CODE - 1))
            return at

        found = lax.fori_loop(0, count, gather, 0)
        if near:
            found = note(found, 0, guest - 1, count - 1)
            found = note(found, count - 1, guest + 1, 0)
        for k in range(PAIRS - 1):
            who[found + k] = 0
            whom[found + k] = 0
            far[found + k] = FAR

        def step(g, carry):
            places, pairs = ([], [])
            for k in range(PAIRS):
                at = g * PAIRS + k
                places.append((who[at], whom[at]))
                pairs.append(self.pair(who[at], whom[at], 1, far[at]))
            parts = pair_grads(pairs, self.scaling)
            for (q, j), (query_part, key_part, value_part) in zip(places, parts):
                self.dq[q] += query_part
                self.acc[j, 0] += key_part
                self.acc[j, 1] += value_part
            return carry

        lax.fori_loop(0, (found + PAIRS - 1) // PAIRS, step, 0)

    def finish(self, out):
        def step(q, carry):
            out[q] = (self.dq[q] * self.scaling).astype(out.dtype)
            return carry

        lax.fori_loop(0, self.count, step, 0)


def own_kernel(unit, keyval, acc, dq, stat):
    def clear(b, carry):
        acc[b] = jnp.zeros(acc.shape[1:], jnp.float32)
        return carry

    count = dq.shape[0]
    lax.fori_loop(0, count, clear, 0)
    own = Visitor(count, unit, stat, dq, keyval, keyval, acc, values_at=count)
    own.begin()
    own.window()


def visit_kernel(plan, me_ref, layout, *refs):
    offsets, count, span, fanout = plan
    refs = list(refs)
    first = offsets == (0,)
    guests = [refs.pop(0) for _ in offsets]
    me = me_ref[0]
    shards = me_ref[1]
    seat = lax.rem(me, span)
    row = lax.div(me, span)
    side = 1 - 2 * lax.rem(row, 2)
    if first:
        parts = [refs.pop(0) for _ in range(span)]
        acc_own, dq_own = (refs.pop(0), refs.pop(0))
        keys, values = (refs.pop(0), refs.pop(0))
    else:
        keys, values = (refs.pop(0), refs.pop(0))
        refs.pop(0)
    acc = refs.pop(0)
    outs = [refs.pop(0) for _ in offsets]
    sums = outs if first else [refs.pop(0) for _ in offsets]
    stat = refs.pop(0)
    lists = refs
    if first:

        def lay(b, carry):
            for m in range(span):
                there = m * count + b
                if m == 0:
                    acc[there] = acc_own[b]
                    sums[0][b] = dq_own[b]
                else:
                    acc[there] = jnp.zeros(acc.shape[1:], jnp.float32)
                there = pl.ds(pl.multiple_of(there * BLK, BLK), BLK)
                here = pl.ds(pl.multiple_of(b * BLK, BLK), BLK)
                keys[there, :] = parts[m][here, :]
                here = pl.ds(pl.multiple_of((count + b) * BLK, BLK), BLK)
                values[there, :] = parts[m][here, :]
            return carry

        lax.fori_loop(0, count, lay, 0)

    for v, offset in enumerate(offsets):
        guest = me + offset * span * side
        present = (guest >= 0) & (guest < shards)
        visitor = Visitor(count, guests[v], stat, sums[v], keys, values, acc, layout, lists)

        @pl.when(present)
        def _(visitor=visitor, offset=offset, guest=guest, out=outs[v]):
            visitor.begin(offset != 0)
            @pl.when(row == 0)
            def _():
                visitor.anchors(seat * count)

            visitor.scattered(guest, me, span, fanout, offset in (-1, 0, 1))
            visitor.finish(out)


def sum_of(m, which, b, acc, place, scaling, parts, arrived):
    total = acc[place, which]
    if which == 0:
        total = total * scaling
    for part, units in zip(parts, arrived):
        total = total + part[which, units.index(m), b].astype(jnp.float32)
    return total.astype(jnp.bfloat16)


def share_kernel(plan, acc, *refs):
    span, wanted, arrived = plan
    parts, out = (refs[:-1], refs[-1])
    count = acc.shape[0] // span
    scaling = acc.shape[3] ** (-0.5)

    def step(b, carry):
        for k, m in enumerate(wanted):
            place = m * count + b
            for which in range(2):
                out[which, k, b] = sum_of(m, which, b, acc, place, scaling, parts, arrived)
        return carry

    lax.fori_loop(0, count, step, 0)


def finish_kernel(plan, acc, *refs):
    span, arrived = plan
    parts, outs = (refs[: len(arrived)], refs[len(arrived) : len(arrived) + 2])
    held_s, sems = refs[len(arrived) + 2 :]
    count = acc.shape[0] // span
    scaling = acc.shape[3] ** (-0.5)
    groups = groups_of(count)
    group = count // groups
    copies = []
    for g in range(groups):
        for b in range(g * group, (g + 1) * group):
            for which in range(2):
                held_s[which, b * BLK : (b + 1) * BLK, :] = sum_of(
                    0, which, b, acc, b, scaling, parts, arrived
                )
        for which in range(2):
            at = pl.ds(g * group * BLK, group * BLK)
            copies.append(
                pltpu.make_async_copy(
                    held_s.at[which, at], outs[which].at[at], sems.at[which, g]
                )
            )
            copies[-1].start()
    for copy in copies:
        copy.wait()


SMEM = pl.BlockSpec(memory_space=pltpu.SMEM)
VMEM = pl.BlockSpec(memory_space=pltpu.VMEM)


def own_visit(unit, keyval, count):
    width = unit.shape[1]
    stats = pltpu.VMEM((stat_rows(count), width), jnp.float32)
    return pl.pallas_call(
        own_kernel,
        out_shape=(
            jax.ShapeDtypeStruct((count, 2, BLK, width), jnp.float32),
            jax.ShapeDtypeStruct((count, BLK, width), jnp.float32),
        ),
        scratch_shapes=[stats],
        compiler_params=pltpu.CompilerParams(vmem_limit_bytes=LIMIT),
        name="own",
    )(unit, keyval)


def share(acc, span, wanted, arrived, parts):
    held, _, _, width = acc.shape
    return pl.pallas_call(
        functools.partial(share_kernel, (span, wanted, arrived)),
        out_shape=jax.ShapeDtypeStruct((2, len(wanted), held // span, BLK, width), jnp.bfloat16),
        in_specs=[VMEM] * (1 + len(parts)),
        out_specs=VMEM,
        compiler_params=pltpu.CompilerParams(vmem_limit_bytes=LIMIT),
        name="share",
    )(acc, *parts)


def finish(acc, span, arrived, parts):
    held, _, _, width = acc.shape
    count = held // span
    shape = (count * BLK, width)
    hbm = pl.BlockSpec(memory_space=pltpu.HBM)
    return pl.pallas_call(
        functools.partial(finish_kernel, (span, arrived)),
        out_shape=[jax.ShapeDtypeStruct(shape, jnp.bfloat16)] * 2,
        in_specs=[VMEM] * (1 + len(parts)),
        out_specs=[hbm, hbm],
        scratch_shapes=[
            pltpu.VMEM((2,) + shape, jnp.bfloat16),
            pltpu.SemaphoreType.DMA((2, groups_of(count))),
        ],
        compiler_params=pltpu.CompilerParams(vmem_limit_bytes=LIMIT),
        name="finish",
    )(acc, *parts)


def add_kernel(base, *refs):
    parts, out = (refs[:-1], refs[-1])

    def step(b, carry):
        total = base[b]
        for part in parts:
            total = total + part[b].astype(jnp.float32)
        if len(out.shape) == 3:
            out[b] = total
        else:
            out[pl.ds(pl.multiple_of(b * BLK, BLK), BLK), :] = total.astype(out.dtype)
        return carry

    lax.fori_loop(0, base.shape[0], step, 0)


def add(base, parts, final, weight):
    count, _, width = base.shape
    if final:
        out = jax.ShapeDtypeStruct((count * BLK, width), jnp.bfloat16)
    else:
        out = jax.ShapeDtypeStruct(base.shape, jnp.float32)
    return pl.pallas_call(
        add_kernel,
        out_shape=out,
        cost_estimate=pl.CostEstimate(
            flops=weight * count * 10 * BLK * BLK * width, bytes_accessed=0, transcendentals=0
        ),
        compiler_params=pltpu.CompilerParams(vmem_limit_bytes=LIMIT),
        name="add",
    )(base, *parts)


def visit(me, layout, units, offsets, keyvals, acc, query_acc, weight, count, span, fanout):
    first = query_acc is not None
    width = units[0].shape[1]
    held = span * count
    plan = (offsets, count, span, fanout)
    operands = units + keyvals
    keys = jax.ShapeDtypeStruct((held * BLK, width), jnp.bfloat16)
    outs = [jax.ShapeDtypeStruct((held, 2, BLK, width), jnp.float32)]
    if first:
        outs = [keys, keys] + outs
        aliases = {}
        operands = operands + [acc, query_acc]
    else:
        aliases = {len(operands) + 2: 0}
        operands = operands + [placed(acc, pltpu.VMEM)]
    kind = jnp.float32 if first else jnp.bfloat16
    outs += [jax.ShapeDtypeStruct((count, BLK, width), kind)] * len(units)
    entries = count * fanout + 2 + PAIRS
    stats = pltpu.VMEM((stat_rows(count), width), jnp.float32)
    return list(
        pl.pallas_call(
            functools.partial(visit_kernel, plan),
            out_shape=outs,
            in_specs=[SMEM, SMEM] + [VMEM] * len(operands),
            out_specs=[VMEM] * len(outs),
            input_output_aliases=aliases,
            scratch_shapes=[pltpu.VMEM((count, BLK, width), jnp.float32)]
            * (0 if first else len(units))
            + [
                stats,
                pltpu.SMEM((entries,), jnp.int32),
                pltpu.SMEM((entries,), jnp.int32),
                pltpu.SMEM((entries,), jnp.float32),
            ],
            compiler_params=pltpu.CompilerParams(vmem_limit_bytes=LIMIT),
            cost_estimate=pl.CostEstimate(
                flops=weight * count * 10 * BLK * BLK * width,
                bytes_accessed=0,
                transcendentals=len(offsets) * count * BLK * BLK,
            ),
            name="visit",
        )(me, layout, *operands)
    )


def body(query_rows, key_rows, value_rows, output_rows, output_grad, logsumexp, layout):
    shards = lax.axis_size("qb")
    myself = lax.axis_index("qb")
    width = query_rows.shape[1]
    count = query_rows.shape[0] // BLK
    fanout = layout.shape[1]
    span = 4
    while shards // span > 16:
        span = span * 2
    planes = shards // span

    def send(array, pairs):
        return lax.ppermute(array, "qb", pairs)

    def swap(array, bit):
        return send(array, [(i, i ^ bit) for i in range(shards)])

    def hop(s, odd, back=False):
        pairs = []
        for p in range(odd, planes - 1, 2):
            if p >= s - 1:
                pairs.append((p, p + 1))
            if p + 1 <= planes - s:
                pairs.append((p + 1, p))
        if back:
            pairs = [(q, p) for p, q in pairs]
        return [(p * span + e, q * span + e) for p, q in pairs for e in range(span)]

    me = jnp.stack([myself, jnp.int32(shards)]).astype(jnp.int32)
    entries = (layout // count * CODE + layout % count).reshape(-1)
    unit = pack(query_rows, output_grad, output_rows, logsumexp.reshape(count, BLK))
    keyval = join(key_rows, value_rows)

    def merge(one, two):
        return (one.astype(jnp.float32) + two.astype(jnp.float32)).astype(jnp.bfloat16)

    def tie(*arrays):
        return lax.optimization_barrier(arrays)

    last = planes - 1
    odd, even = (send(unit, hop(1, 1)), send(unit, hop(1, 0)))
    keyvals = {0: keyval}
    singles = [m for m in range(1, span) if m & (m - 1) == 0]
    for m in singles:
        keyvals[m] = swap(keyval, m)
    acc, query_acc = own_visit(unit, keyval, count)
    even, query_acc = tie(even, query_acc)
    for m in range(1, span):
        if m & (m - 1):
            keyvals[m] = swap(keyvals[m & (m - 1)], m & -m)
    keyvals = [keyvals[m] for m in range(span)]

    def meet(units, offsets, keyvals, acc, query_acc=None, weight=0):
        return visit(
            me, entries, units, offsets, keyvals, acc, query_acc, weight, count, span, fanout
        )

    keys, values, acc, query_acc = meet([unit], (0,), keyvals, acc, query_acc)
    ends = [(last * span + e, e) for e in range(span)]
    ends = ends + [(two, one) for one, two in ends]
    even_parts, odd_parts = ([], [])
    for s in range(1, last):
        if s + 1 < last:
            next_even, next_odd = (send(odd, hop(s + 1, 0)), send(even, hop(s + 1, 1)))
        else:
            odd, query_acc = tie(odd, query_acc)
            far = send(odd, hop(last, 0))
        if s + 2 == last:
            acc, next_even = tie(acc, next_even)
        acc, even_part, odd_part = meet([even, odd], (s, -s), [keys, values], acc)
        even_parts.append(even_part)
        odd_parts.append(odd_part)
        if s + 1 < last:
            even, odd = (next_even, next_odd)
    acc, far_part = meet([far], (last,), [keys, values], acc, None, COST)

    even_back, odd_back = (even_parts[-1], odd_parts[-1])
    for t in range(last - 1, 1, -1):
        even_back, odd_back = (send(even_back, hop(t, 0, True)), send(odd_back, hop(t, 1, True)))
        if t == 2:
            even_back, odd_back, far_part = tie(even_back, odd_back, far_part)
        even_back, odd_back = (
            merge(even_parts[t - 2], odd_back),
            merge(odd_parts[t - 2], even_back),
        )
    acc, even_back, odd_back = tie(acc, even_back, odd_back)
    backs = [send(even_back, hop(1, 0, True)), send(odd_back, hop(1, 1, True))]
    query_acc = add(query_acc, backs, False, COST)
    query_grad = add(query_acc, [send(far_part, ends)], True, 1)

    wanted = tuple(range(span))
    arrived, parts = ((), ())
    bit = 1
    while bit < span:
        theirs = tuple(m for m in wanted if m & bit)
        wanted = tuple(m for m in wanted if not m & bit)
        sent = share(acc, span, theirs, arrived, parts)
        arrived, parts = (arrived + (wanted,), parts + (swap(sent, bit),))
        bit = bit * 2
    *parts, query_grad = tie(*parts, query_grad)
    key_grad, value_grad = finish(acc, span, arrived, parts)
    return (query_grad, key_grad, value_grad)


def solution(mesh):
    in_specs = (
        P(("grp", "qb"), None),
        P(("grp", "qb"), None),
        P(("grp", "qb"), None),
        P(("grp", "qb"), None),
        P(("grp", "qb"), None),
        P(("grp", "qb")),
        P("grp", None),
    )
    out_specs = (P(("grp", "qb"), None), P(("grp", "qb"), None), P(("grp", "qb"), None))
    return jax.shard_map(body, mesh=mesh, in_specs=in_specs, out_specs=out_specs, check_vma=False)
```

```python
import functools

import jax
import jax.numpy as jnp
from jax import lax
from jax.experimental import pallas as pl
from jax.experimental.pallas import tpu as pltpu
from jax.sharding import PartitionSpec as P

BLK = 128
GLOB = 2
TILE = 16
CODE = 256
PAIRS = 5
TURNS = 6
FAR = 1e30
COST = 20
LIMIT = 16 * 2**20


def pieces(row):
    high = row.astype(jnp.bfloat16).astype(jnp.float32)
    return [high, row - high]


def stat_rows(count):
    return -(-4 * count // TILE) * TILE


def placed(array, space):
    return pltpu.with_memory_space_constraint(array, space)


def groups_of(count):
    return next(groups for groups in (2, 3, 1) if count % groups == 0)


def pack_kernel(query, grad, output, lse_hbm, unit, output_s, lse, delta_s, stat_s, sems):
    count, width = lse.shape
    groups = groups_of(count)
    group = count // groups
    ones = jnp.ones((TILE, width), jnp.bfloat16)
    held = count * BLK
    loads = []
    for g in range(groups):
        at = pl.ds(g * group * BLK, group * BLK)
        after = pl.ds(held + g * group * BLK, group * BLK)
        loads.append(
            [
                pltpu.make_async_copy(grad.at[at], unit.at[after], sems.at[0, g]),
                pltpu.make_async_copy(output.at[at], output_s.at[at], sems.at[1, g]),
                pltpu.make_async_copy(query.at[at], unit.at[at], sems.at[2, g]),
            ]
        )
    lines = pltpu.make_async_copy(lse_hbm, lse, sems.at[3, 0])
    lines.start()
    for kind in range(3):
        for load in loads:
            load[kind].start()

    def total(part):
        return lax.dot_general(
            ones, part, (((1,), (1,)), ((), ())), preferred_element_type=jnp.float32
        )

    for g in range(groups):
        loads[g][0].wait()
        loads[g][1].wait()
        highs, lows = ([], [])
        for k in range(g * group, (g + 1) * group):
            grads = unit[held + k * BLK : held + (k + 1) * BLK, :].astype(jnp.float32)
            product = grads * output_s[k * BLK : (k + 1) * BLK, :].astype(jnp.float32)
            highs.append(product.astype(jnp.bfloat16))
            lows.append((product - highs[-1].astype(jnp.float32)).astype(jnp.bfloat16))
        sums = [total(high) + total(low) for high, low in zip(highs, lows)]
        for k in range(group):
            delta_s[g * group + k : g * group + k + 1, :] = sums[k][0:1]
    lines.wait()
    stat_s[...] = jnp.zeros(stat_s.shape, jnp.float32)
    for k, line in enumerate(pieces(lse[...]) + pieces(delta_s[...])):
        stat_s[k * count : (k + 1) * count, :] = line
    unit[2 * held :, :] = stat_s[...].astype(jnp.bfloat16)
    for load in loads:
        load[2].wait()


def pack(query, grad, output, lse):
    count, width = lse.shape
    rows = stat_rows(count)
    hbm = pl.BlockSpec(memory_space=pltpu.HBM)
    return pl.pallas_call(
        pack_kernel,
        out_shape=jax.ShapeDtypeStruct((2 * count * BLK + rows, width), jnp.bfloat16),
        in_specs=[hbm] * 4,
        out_specs=pl.BlockSpec(memory_space=pltpu.VMEM),
        scratch_shapes=[
            pltpu.VMEM(query.shape, jnp.bfloat16),
            pltpu.VMEM(lse.shape, jnp.float32),
            pltpu.VMEM(lse.shape, jnp.float32),
            pltpu.VMEM((rows, width), jnp.float32),
            pltpu.SemaphoreType.DMA((4, groups_of(count))),
        ],
        compiler_params=pltpu.CompilerParams(vmem_limit_bytes=LIMIT),
        name="pack",
    )(*[placed(array, pltpu.HBM) for array in (query, grad, output, lse)])


def join_kernel(key, value, keyval, sems):
    rows = key.shape[0]
    copies = [
        pltpu.make_async_copy(key, keyval.at[pl.ds(0, rows)], sems.at[0]),
        pltpu.make_async_copy(value, keyval.at[pl.ds(rows, rows)], sems.at[1]),
    ]
    for copy in copies:
        copy.start()
    for copy in copies:
        copy.wait()


def join(key, value):
    rows, width = key.shape
    hbm = pl.BlockSpec(memory_space=pltpu.HBM)
    return pl.pallas_call(
        join_kernel,
        out_shape=jax.ShapeDtypeStruct((2 * rows, width), key.dtype),
        in_specs=[hbm, hbm],
        out_specs=pl.BlockSpec(memory_space=pltpu.VMEM),
        scratch_shapes=[pltpu.SemaphoreType.DMA((2,))],
        compiler_params=pltpu.CompilerParams(vmem_limit_bytes=LIMIT),
        name="join",
    )(placed(key, pltpu.HBM), placed(value, pltpu.HBM))


def pair_grads(pairs, scaling):
    def outer(one, two):
        return lax.dot_general(
            one, two, (((1,), (1,)), ((), ())), preferred_element_type=jnp.float32
        )

    def inner(one, two):
        return jnp.dot(one, two, preferred_element_type=jnp.float32)

    def flipped(one, two):
        return lax.dot_general(
            one, two, (((0,), (0,)), ((), ())), preferred_element_type=jnp.float32
        )

    scores = [outer(keys, queries) for keys, _, queries, _, _, _, _ in pairs]
    dweights = [outer(values, grads) for _, values, _, grads, _, _, _ in pairs]
    probs = []
    for score, (_, _, _, _, lse, _, mask) in zip(scores, pairs):
        prob = jnp.exp(score * scaling - lse)
        probs.append(prob if mask is None else jnp.where(mask, prob, 0.0))
    prob_lows = [prob.astype(jnp.bfloat16) for prob in probs]
    score_lows = [
        (prob * (dweight - pair[5])).astype(jnp.bfloat16)
        for prob, dweight, pair in zip(probs, dweights, pairs)
    ]
    value_parts = [inner(low, pair[3]) for low, pair in zip(prob_lows, pairs)]
    key_parts = [inner(low, pair[2]) for low, pair in zip(score_lows, pairs)]
    query_parts = [flipped(low, pair[0]) for low, pair in zip(score_lows, pairs)]
    return list(zip(query_parts, key_parts, value_parts))


class Visitor:
    def __init__(
        self, count, unit, stat, dq, keys, values, acc, layout=None, lists=None, values_at=0
    ):
        self.count = count
        self.unit, self.stat = (unit, stat)
        self.dq, self.keys, self.values, self.acc = (dq, keys, values, acc)
        self.layout, self.lists, self.values_at = (layout, lists, values_at)
        self.width = unit.shape[1]
        self.scaling = self.width ** (-0.5)

    def begin(self, clear=True):
        count = self.count
        self.stat[...] = self.unit[2 * count * BLK :, :].astype(jnp.float32)

        def step(q, carry):
            self.dq[q] = jnp.zeros(self.dq.shape[1:], jnp.float32)
            return carry

        if clear:
            lax.fori_loop(0, count, step, 0)

    def rows(self, array, block, blocks=1):
        return array[pl.ds(pl.multiple_of(block * BLK, BLK), blocks * BLK), :]

    def line(self, q, kind):
        at = 2 * kind * self.count + q
        return self.stat[pl.ds(at, 1), :] + self.stat[pl.ds(at + self.count, 1), :]

    def pair(self, q, j, keys=1, shift=0.0, mask=None):
        return (
            self.rows(self.keys, j, keys),
            self.rows(self.values, self.values_at + j, keys),
            self.rows(self.unit, q),
            self.rows(self.unit, self.count + q),
            self.line(q, 0) + shift,
            self.line(q, 1),
            mask,
        )

    def window(self):
        count, width = (self.count, self.width)
        chunk = 2 if count % 2 == 0 else 1

        def step(c, carry):
            places, pairs = ([], [])
            for k in range(chunk):
                q = c * chunk + k
                start = jnp.clip(q - 1, 0, count - 3)
                block = lax.broadcasted_iota(jnp.int32, (3 * BLK, BLK), 0) // BLK
                block = block + start - q
                places.append((q, start))
                pairs.append(self.pair(q, start, 3, 0.0, (block >= -1) & (block <= 1)))
            parts = pair_grads(pairs, self.scaling)
            for (q, start), (query_part, key_part, value_part) in zip(places, parts):
                self.dq[q] += query_part
                self.acc[pl.ds(start, 3), 0] += key_part.reshape(3, BLK, width)
                self.acc[pl.ds(start, 3), 1] += value_part.reshape(3, BLK, width)
            return carry

        lax.fori_loop(0, count // chunk, step, 0)

    def anchors(self, base):
        count, width = (self.count, self.width)
        chunk = 2 if count % 2 == 0 else 1
        turns = next(turns for turns in (TURNS, 2, 1) if count % (turns * chunk) == 0)
        globals_ = pl.ds(base, GLOB)

        def step(c, carry):
            places, pairs = ([], [])
            for k in range(turns):
                at = (c * turns + k) * chunk
                places.append(pl.ds(at, chunk))
                pairs.append(
                    (
                        self.rows(self.keys, base, GLOB),
                        self.rows(self.values, base, GLOB),
                        self.rows(self.unit, at, chunk),
                        self.rows(self.unit, count + at, chunk),
                        jnp.concatenate(
                            [self.line(at + i, 0) for i in range(chunk)], 1
                        ),
                        jnp.concatenate(
                            [self.line(at + i, 1) for i in range(chunk)], 1
                        ),
                        None,
                    )
                )
            parts = pair_grads(pairs, self.scaling)
            for blocks, (query_part, _, _) in zip(places, parts):
                self.dq[blocks] += query_part.reshape(chunk, BLK, width)
            key_part = sum(part[1] for part in parts)
            value_part = sum(part[2] for part in parts)
            self.acc[globals_, 0] += key_part.reshape(GLOB, BLK, width)
            self.acc[globals_, 1] += value_part.reshape(GLOB, BLK, width)
            return carry

        lax.fori_loop(0, count // (chunk * turns), step, 0)

    def scattered(self, guest, me, span, fanout, near):
        who, whom, far = self.lists
        count = self.count

        def note(at, q, owner, block):
            unit = jnp.bitwise_xor(owner, me)
            hit = (unit >= 0) & (unit < span)
            who[at] = q
            whom[at] = unit * count + block
            far[at] = 0.0
            return at + hit.astype(jnp.int32)

        group = count // groups_of(count)

        def gather(g, at):
            first = (guest * count + g * group) * fanout
            codes = [self.layout[first + k] for k in range(group * fanout)]
            for k, code in enumerate(codes):
                owner = lax.shift_right_logical(code, CODE.bit_length() - 1)
                at = note(at, g * group + k // fanout, owner, code & (CODE - 1))
            return at

        found = lax.fori_loop(0, count // group, gather, 0)
        if near:
            found = note(found, 0, guest - 1, count - 1)
            found = note(found, count - 1, guest + 1, 0)
        for k in range(PAIRS - 1):
            who[found + k] = 0
            whom[found + k] = 0
            far[found + k] = FAR

        def step(g, carry):
            places, pairs = ([], [])
            for k in range(PAIRS):
                at = g * PAIRS + k
                places.append((who[at], whom[at]))
                pairs.append(self.pair(who[at], whom[at], 1, far[at]))
            parts = pair_grads(pairs, self.scaling)
            for (q, j), (query_part, key_part, value_part) in zip(places, parts):
                self.dq[q] += query_part
                self.acc[j, 0] += key_part
                self.acc[j, 1] += value_part
            return carry

        lax.fori_loop(0, (found + PAIRS - 1) // PAIRS, step, 0)

    def finish(self, out):
        def step(q, carry):
            out[q] = (self.dq[q] * self.scaling).astype(out.dtype)
            return carry

        lax.fori_loop(0, self.count, step, 0)


def own_kernel(unit, keyval, acc, dq, stat):
    def clear(b, carry):
        acc[b] = jnp.zeros(acc.shape[1:], jnp.float32)
        return carry

    count = dq.shape[0]
    lax.fori_loop(0, count, clear, 0)
    own = Visitor(count, unit, stat, dq, keyval, keyval, acc, values_at=count)
    own.begin()
    own.window()


def visit_kernel(plan, me_ref, layout, *refs):
    offsets, count, span, fanout = plan
    refs = list(refs)
    first = offsets == (0,)
    guests = [refs.pop(0) for _ in offsets]
    me = me_ref[0]
    shards = me_ref[1]
    seat = lax.rem(me, span)
    row = lax.div(me, span)
    side = 1 - 2 * lax.rem(row, 2)
    if first:
        parts = [refs.pop(0) for _ in range(span)]
        acc_own, dq_own = (refs.pop(0), refs.pop(0))
        keys, values = (refs.pop(0), refs.pop(0))
    else:
        keys, values = (refs.pop(0), refs.pop(0))
        refs.pop(0)
    acc = refs.pop(0)
    outs = [refs.pop(0) for _ in offsets]
    sums = outs if first else [refs.pop(0) for _ in offsets]
    stat = refs.pop(0)
    lists = refs
    if first:

        def lay(b, carry):
            for m in range(span):
                there = m * count + b
                if m == 0:
                    acc[there] = acc_own[b]
                    sums[0][b] = dq_own[b]
                else:
                    acc[there] = jnp.zeros(acc.shape[1:], jnp.float32)
                there = pl.ds(pl.multiple_of(there * BLK, BLK), BLK)
                here = pl.ds(pl.multiple_of(b * BLK, BLK), BLK)
                keys[there, :] = parts[m][here, :]
                here = pl.ds(pl.multiple_of((count + b) * BLK, BLK), BLK)
                values[there, :] = parts[m][here, :]
            return carry

        lax.fori_loop(0, count, lay, 0)

    for v, offset in enumerate(offsets):
        guest = me + offset * span * side
        present = (guest >= 0) & (guest < shards)
        visitor = Visitor(count, guests[v], stat, sums[v], keys, values, acc, layout, lists)

        @pl.when(present)
        def _(visitor=visitor, offset=offset, guest=guest, out=outs[v]):
            visitor.begin(offset != 0)
            @pl.when(row == 0)
            def _():
                visitor.anchors(seat * count)

            visitor.scattered(guest, me, span, fanout, offset in (-1, 0, 1))
            visitor.finish(out)


def sum_of(m, which, b, acc, place, scaling, parts, arrived):
    total = acc[place, which]
    if which == 0:
        total = total * scaling
    for part, units in zip(parts, arrived):
        total = total + part[which, units.index(m), b].astype(jnp.float32)
    return total.astype(jnp.bfloat16)


def share_kernel(plan, acc, *refs):
    span, wanted, arrived = plan
    parts, out = (refs[:-1], refs[-1])
    count = acc.shape[0] // span
    scaling = acc.shape[3] ** (-0.5)

    def step(b, carry):
        for k, m in enumerate(wanted):
            place = m * count + b
            for which in range(2):
                out[which, k, b] = sum_of(m, which, b, acc, place, scaling, parts, arrived)
        return carry

    lax.fori_loop(0, count, step, 0)


def finish_kernel(plan, acc, *refs):
    span, arrived = plan
    parts, outs = (refs[: len(arrived)], refs[len(arrived) : len(arrived) + 2])
    held_s, sems = refs[len(arrived) + 2 :]
    count = acc.shape[0] // span
    scaling = acc.shape[3] ** (-0.5)
    groups = groups_of(count)
    group = count // groups
    copies = []
    for g in range(groups):
        for b in range(g * group, (g + 1) * group):
            for which in range(2):
                held_s[which, b * BLK : (b + 1) * BLK, :] = sum_of(
                    0, which, b, acc, b, scaling, parts, arrived
                )
        for which in range(2):
            at = pl.ds(g * group * BLK, group * BLK)
            copies.append(
                pltpu.make_async_copy(
                    held_s.at[which, at], outs[which].at[at], sems.at[which, g]
                )
            )
            copies[-1].start()
    for copy in copies:
        copy.wait()


SMEM = pl.BlockSpec(memory_space=pltpu.SMEM)
VMEM = pl.BlockSpec(memory_space=pltpu.VMEM)


def own_visit(unit, keyval, count):
    width = unit.shape[1]
    stats = pltpu.VMEM((stat_rows(count), width), jnp.float32)
    return pl.pallas_call(
        own_kernel,
        out_shape=(
            jax.ShapeDtypeStruct((count, 2, BLK, width), jnp.float32),
            jax.ShapeDtypeStruct((count, BLK, width), jnp.float32),
        ),
        scratch_shapes=[stats],
        compiler_params=pltpu.CompilerParams(vmem_limit_bytes=LIMIT),
        name="own",
    )(unit, keyval)


def share(acc, span, wanted, arrived, parts):
    held, _, _, width = acc.shape
    return pl.pallas_call(
        functools.partial(share_kernel, (span, wanted, arrived)),
        out_shape=jax.ShapeDtypeStruct((2, len(wanted), held // span, BLK, width), jnp.bfloat16),
        in_specs=[VMEM] * (1 + len(parts)),
        out_specs=VMEM,
        compiler_params=pltpu.CompilerParams(vmem_limit_bytes=LIMIT),
        name="share",
    )(acc, *parts)


def finish(acc, span, arrived, parts):
    held, _, _, width = acc.shape
    count = held // span
    shape = (count * BLK, width)
    hbm = pl.BlockSpec(memory_space=pltpu.HBM)
    return pl.pallas_call(
        functools.partial(finish_kernel, (span, arrived)),
        out_shape=[jax.ShapeDtypeStruct(shape, jnp.bfloat16)] * 2,
        in_specs=[VMEM] * (1 + len(parts)),
        out_specs=[hbm, hbm],
        scratch_shapes=[
            pltpu.VMEM((2,) + shape, jnp.bfloat16),
            pltpu.SemaphoreType.DMA((2, groups_of(count))),
        ],
        compiler_params=pltpu.CompilerParams(vmem_limit_bytes=LIMIT),
        name="finish",
    )(acc, *parts)


def add_kernel(base, *refs):
    parts, out = (refs[:-1], refs[-1])

    def step(b, carry):
        total = base[b]
        for part in parts:
            total = total + part[b].astype(jnp.float32)
        if len(out.shape) == 3:
            out[b] = total
        else:
            out[pl.ds(pl.multiple_of(b * BLK, BLK), BLK), :] = total.astype(out.dtype)
        return carry

    lax.fori_loop(0, base.shape[0], step, 0)


def add(base, parts, final, weight):
    count, _, width = base.shape
    if final:
        out = jax.ShapeDtypeStruct((count * BLK, width), jnp.bfloat16)
    else:
        out = jax.ShapeDtypeStruct(base.shape, jnp.float32)
    return pl.pallas_call(
        add_kernel,
        out_shape=out,
        cost_estimate=pl.CostEstimate(
            flops=weight * count * 10 * BLK * BLK * width, bytes_accessed=0, transcendentals=0
        ),
        compiler_params=pltpu.CompilerParams(vmem_limit_bytes=LIMIT),
        name="add",
    )(base, *parts)


def visit(me, layout, units, offsets, keyvals, acc, query_acc, weight, count, span, fanout):
    first = query_acc is not None
    width = units[0].shape[1]
    held = span * count
    plan = (offsets, count, span, fanout)
    operands = units + keyvals
    keys = jax.ShapeDtypeStruct((held * BLK, width), jnp.bfloat16)
    outs = [jax.ShapeDtypeStruct((held, 2, BLK, width), jnp.float32)]
    if first:
        outs = [keys, keys] + outs
        aliases = {}
        operands = operands + [acc, query_acc]
    else:
        aliases = {len(operands) + 2: 0}
        operands = operands + [placed(acc, pltpu.VMEM)]
    kind = jnp.float32 if first else jnp.bfloat16
    outs += [jax.ShapeDtypeStruct((count, BLK, width), kind)] * len(units)
    entries = count * fanout + 2 + PAIRS
    stats = pltpu.VMEM((stat_rows(count), width), jnp.float32)
    return list(
        pl.pallas_call(
            functools.partial(visit_kernel, plan),
            out_shape=outs,
            in_specs=[SMEM, SMEM] + [VMEM] * len(operands),
            out_specs=[VMEM] * len(outs),
            input_output_aliases=aliases,
            scratch_shapes=[pltpu.VMEM((count, BLK, width), jnp.float32)]
            * (0 if first else len(units))
            + [
                stats,
                pltpu.SMEM((entries,), jnp.int32),
                pltpu.SMEM((entries,), jnp.int32),
                pltpu.SMEM((entries,), jnp.float32),
            ],
            compiler_params=pltpu.CompilerParams(vmem_limit_bytes=LIMIT),
            cost_estimate=pl.CostEstimate(
                flops=weight * count * 10 * BLK * BLK * width,
                bytes_accessed=0,
                transcendentals=len(offsets) * count * BLK * BLK,
            ),
            name="visit",
        )(me, layout, *operands)
    )


def body(query_rows, key_rows, value_rows, output_rows, output_grad, logsumexp, layout):
    shards = lax.axis_size("qb")
    myself = lax.axis_index("qb")
    width = query_rows.shape[1]
    count = query_rows.shape[0] // BLK
    fanout = layout.shape[1]
    span = 4
    while shards // span > 16:
        span = span * 2
    planes = shards // span

    def send(array, pairs):
        return lax.ppermute(array, "qb", pairs)

    def swap(array, bit):
        return send(array, [(i, i ^ bit) for i in range(shards)])

    def hop(s, odd, back=False):
        pairs = []
        for p in range(odd, planes - 1, 2):
            if p >= s - 1:
                pairs.append((p, p + 1))
            if p + 1 <= planes - s:
                pairs.append((p + 1, p))
        if back:
            pairs = [(q, p) for p, q in pairs]
        return [(p * span + e, q * span + e) for p, q in pairs for e in range(span)]

    me = jnp.stack([myself, jnp.int32(shards)]).astype(jnp.int32)
    entries = (layout // count * CODE + layout % count).reshape(-1)
    unit = pack(query_rows, output_grad, output_rows, logsumexp.reshape(count, BLK))
    keyval = join(key_rows, value_rows)

    def merge(one, two):
        return (one.astype(jnp.float32) + two.astype(jnp.float32)).astype(jnp.bfloat16)

    def tie(*arrays):
        return lax.optimization_barrier(arrays)

    last = planes - 1
    odd, even = (send(unit, hop(1, 1)), send(unit, hop(1, 0)))
    keyvals = {0: keyval}
    singles = [m for m in range(1, span) if m & (m - 1) == 0]
    for m in singles:
        keyvals[m] = swap(keyval, m)
    acc, query_acc = own_visit(unit, keyval, count)
    even, query_acc = tie(even, query_acc)
    for m in range(1, span):
        if m & (m - 1):
            keyvals[m] = swap(keyvals[m & (m - 1)], m & -m)
    keyvals = [keyvals[m] for m in range(span)]

    def meet(units, offsets, keyvals, acc, query_acc=None, weight=0):
        return visit(
            me, entries, units, offsets, keyvals, acc, query_acc, weight, count, span, fanout
        )

    keys, values, acc, query_acc = meet([unit], (0,), keyvals, acc, query_acc)
    ends = [(last * span + e, e) for e in range(span)]
    ends = ends + [(two, one) for one, two in ends]
    even_parts, odd_parts = ([], [])
    for s in range(1, last):
        if s + 1 < last:
            next_even, next_odd = (send(odd, hop(s + 1, 0)), send(even, hop(s + 1, 1)))
        else:
            odd, query_acc = tie(odd, query_acc)
            far = send(odd, hop(last, 0))
        if s + 2 == last:
            acc, next_even = tie(acc, next_even)
        acc, even_part, odd_part = meet([even, odd], (s, -s), [keys, values], acc)
        even_parts.append(even_part)
        odd_parts.append(odd_part)
        if s + 1 < last:
            even, odd = (next_even, next_odd)
    acc, far_part = meet([far], (last,), [keys, values], acc, None, COST)

    even_back, odd_back = (even_parts[-1], odd_parts[-1])
    for t in range(last - 1, 1, -1):
        even_back, odd_back = (send(even_back, hop(t, 0, True)), send(odd_back, hop(t, 1, True)))
        if t == 2:
            even_back, odd_back, far_part = tie(even_back, odd_back, far_part)
        even_back, odd_back = (
            merge(even_parts[t - 2], odd_back),
            merge(odd_parts[t - 2], even_back),
        )
    acc, even_back, odd_back = tie(acc, even_back, odd_back)
    backs = [send(even_back, hop(1, 0, True)), send(odd_back, hop(1, 1, True))]
    query_acc = add(query_acc, backs, False, COST)
    query_grad = add(query_acc, [send(far_part, ends)], True, 1)

    wanted = tuple(range(span))
    arrived, parts = ((), ())
    bit = 1
    while bit < span:
        theirs = tuple(m for m in wanted if m & bit)
        wanted = tuple(m for m in wanted if not m & bit)
        sent = share(acc, span, theirs, arrived, parts)
        arrived, parts = (arrived + (wanted,), parts + (swap(sent, bit),))
        bit = bit * 2
    *parts, query_grad = tie(*parts, query_grad)
    key_grad, value_grad = finish(acc, span, arrived, parts)
    return (query_grad, key_grad, value_grad)


def solution(mesh):
    in_specs = (
        P(("grp", "qb"), None),
        P(("grp", "qb"), None),
        P(("grp", "qb"), None),
        P(("grp", "qb"), None),
        P(("grp", "qb"), None),
        P(("grp", "qb")),
        P("grp", None),
    )
    out_specs = (P(("grp", "qb"), None), P(("grp", "qb"), None), P(("grp", "qb"), None))
    return jax.shard_map(body, mesh=mesh, in_specs=in_specs, out_specs=out_specs, check_vma=False)
```

```python
import functools

import jax
import jax.numpy as jnp
from jax import lax
from jax.experimental import pallas as pl
from jax.experimental.pallas import tpu as pltpu
from jax.sharding import PartitionSpec as P

BLK = 128
GLOB = 2
TILE = 16
CODE = 256
PAIRS = 5
TURNS = 6
FAR = 1e30
COST = 20
LIMIT = 16 * 2**20


def pieces(row):
    high = row.astype(jnp.bfloat16).astype(jnp.float32)
    return [high, row - high]


def stat_rows(count):
    return -(-4 * count // TILE) * TILE


def placed(array, space):
    return pltpu.with_memory_space_constraint(array, space)


def groups_of(count):
    return next(groups for groups in (2, 3, 1) if count % groups == 0)


def pack_kernel(
    query, grad, output, lse_hbm, key, value, unit, keyval, output_s, lse, delta_s, stat_s, sems
):
    count, width = lse.shape
    groups = groups_of(count)
    group = count // groups
    ones = jnp.ones((TILE, width), jnp.bfloat16)
    held = count * BLK
    loads = []
    for g in range(groups):
        at = pl.ds(g * group * BLK, group * BLK)
        after = pl.ds(held + g * group * BLK, group * BLK)
        loads.append(
            [
                pltpu.make_async_copy(grad.at[at], unit.at[after], sems.at[0, g]),
                pltpu.make_async_copy(output.at[at], output_s.at[at], sems.at[1, g]),
                pltpu.make_async_copy(query.at[at], unit.at[at], sems.at[2, g]),
            ]
        )
    lines = pltpu.make_async_copy(lse_hbm, lse, sems.at[3, 0])
    lines.start()
    for kind in range(3):
        for load in loads:
            load[kind].start()
    joins = [
        pltpu.make_async_copy(key, keyval.at[pl.ds(0, held)], sems.at[4, 0]),
        pltpu.make_async_copy(value, keyval.at[pl.ds(held, held)], sems.at[5, 0]),
    ]
    for join in joins:
        join.start()

    def total(part):
        return lax.dot_general(
            ones, part, (((1,), (1,)), ((), ())), preferred_element_type=jnp.float32
        )

    for g in range(groups):
        loads[g][0].wait()
        loads[g][1].wait()
        highs, lows = ([], [])
        for k in range(g * group, (g + 1) * group):
            grads = unit[held + k * BLK : held + (k + 1) * BLK, :].astype(jnp.float32)
            product = grads * output_s[k * BLK : (k + 1) * BLK, :].astype(jnp.float32)
            highs.append(product.astype(jnp.bfloat16))
            lows.append((product - highs[-1].astype(jnp.float32)).astype(jnp.bfloat16))
        sums = [total(high) + total(low) for high, low in zip(highs, lows)]
        for k in range(group):
            delta_s[g * group + k : g * group + k + 1, :] = sums[k][0:1]
    lines.wait()
    stat_s[...] = jnp.zeros(stat_s.shape, jnp.float32)
    for k, line in enumerate(pieces(lse[...]) + pieces(delta_s[...])):
        stat_s[k * count : (k + 1) * count, :] = line
    unit[2 * held :, :] = stat_s[...].astype(jnp.bfloat16)
    for load in loads:
        load[2].wait()
    for join in joins:
        join.wait()


def pack(query, grad, output, lse, key, value):
    count, width = lse.shape
    rows = stat_rows(count)
    hbm = pl.BlockSpec(memory_space=pltpu.HBM)
    return pl.pallas_call(
        pack_kernel,
        out_shape=(
            jax.ShapeDtypeStruct((2 * count * BLK + rows, width), jnp.bfloat16),
            jax.ShapeDtypeStruct((2 * count * BLK, width), jnp.bfloat16),
        ),
        in_specs=[hbm] * 6,
        out_specs=[pl.BlockSpec(memory_space=pltpu.VMEM)] * 2,
        scratch_shapes=[
            pltpu.VMEM(query.shape, jnp.bfloat16),
            pltpu.VMEM(lse.shape, jnp.float32),
            pltpu.VMEM(lse.shape, jnp.float32),
            pltpu.VMEM((rows, width), jnp.float32),
            pltpu.SemaphoreType.DMA((6, groups_of(count))),
        ],
        compiler_params=pltpu.CompilerParams(vmem_limit_bytes=LIMIT),
        name="pack",
    )(*[placed(array, pltpu.HBM) for array in (query, grad, output, lse, key, value)])


def pair_grads(pairs, scaling):
    def outer(one, two):
        return lax.dot_general(
            one, two, (((1,), (1,)), ((), ())), preferred_element_type=jnp.float32
        )

    def inner(one, two):
        return jnp.dot(one, two, preferred_element_type=jnp.float32)

    def flipped(one, two):
        return lax.dot_general(
            one, two, (((0,), (0,)), ((), ())), preferred_element_type=jnp.float32
        )

    scores = [outer(keys, queries) for keys, _, queries, _, _, _, _ in pairs]
    dweights = [outer(values, grads) for _, values, _, grads, _, _, _ in pairs]
    probs = []
    for score, (_, _, _, _, lse, _, mask) in zip(scores, pairs):
        prob = jnp.exp(score * scaling - lse)
        probs.append(prob if mask is None else jnp.where(mask, prob, 0.0))
    prob_lows = [prob.astype(jnp.bfloat16) for prob in probs]
    score_lows = [
        (prob * (dweight - pair[5])).astype(jnp.bfloat16)
        for prob, dweight, pair in zip(probs, dweights, pairs)
    ]
    value_parts = [inner(low, pair[3]) for low, pair in zip(prob_lows, pairs)]
    key_parts = [inner(low, pair[2]) for low, pair in zip(score_lows, pairs)]
    query_parts = [flipped(low, pair[0]) for low, pair in zip(score_lows, pairs)]
    return list(zip(query_parts, key_parts, value_parts))


class Visitor:
    def __init__(
        self, count, unit, stat, dq, keys, values, acc, layout=None, lists=None, values_at=0
    ):
        self.count = count
        self.unit, self.stat = (unit, stat)
        self.dq, self.keys, self.values, self.acc = (dq, keys, values, acc)
        self.layout, self.lists, self.values_at = (layout, lists, values_at)
        self.width = unit.shape[1]
        self.scaling = self.width ** (-0.5)

    def begin(self, clear=True):
        count = self.count
        self.stat[...] = self.unit[2 * count * BLK :, :].astype(jnp.float32)

        def step(q, carry):
            self.dq[q] = jnp.zeros(self.dq.shape[1:], jnp.float32)
            return carry

        if clear:
            lax.fori_loop(0, count, step, 0)

    def rows(self, array, block, blocks=1):
        return array[pl.ds(pl.multiple_of(block * BLK, BLK), blocks * BLK), :]

    def line(self, q, kind):
        at = 2 * kind * self.count + q
        return self.stat[pl.ds(at, 1), :] + self.stat[pl.ds(at + self.count, 1), :]

    def pair(self, q, j, keys=1, shift=0.0, mask=None):
        return (
            self.rows(self.keys, j, keys),
            self.rows(self.values, self.values_at + j, keys),
            self.rows(self.unit, q),
            self.rows(self.unit, self.count + q),
            self.line(q, 0) + shift,
            self.line(q, 1),
            mask,
        )

    def window(self):
        count, width = (self.count, self.width)
        chunk = 2 if count % 2 == 0 else 1

        def step(c, carry):
            places, pairs = ([], [])
            for k in range(chunk):
                q = c * chunk + k
                start = jnp.clip(q - 1, 0, count - 3)
                block = lax.broadcasted_iota(jnp.int32, (3 * BLK, BLK), 0) // BLK
                block = block + start - q
                places.append((q, start))
                pairs.append(self.pair(q, start, 3, 0.0, (block >= -1) & (block <= 1)))
            parts = pair_grads(pairs, self.scaling)
            for (q, start), (query_part, key_part, value_part) in zip(places, parts):
                self.dq[q] += query_part
                self.acc[pl.ds(start, 3), 0] += key_part.reshape(3, BLK, width)
                self.acc[pl.ds(start, 3), 1] += value_part.reshape(3, BLK, width)
            return carry

        lax.fori_loop(0, count // chunk, step, 0)

    def anchors(self, base):
        count, width = (self.count, self.width)
        chunk = 2 if count % 2 == 0 else 1
        turns = next(turns for turns in (TURNS, 2, 1) if count % (turns * chunk) == 0)
        globals_ = pl.ds(base, GLOB)

        def step(c, carry):
            places, pairs = ([], [])
            for k in range(turns):
                at = (c * turns + k) * chunk
                places.append(pl.ds(at, chunk))
                pairs.append(
                    (
                        self.rows(self.keys, base, GLOB),
                        self.rows(self.values, base, GLOB),
                        self.rows(self.unit, at, chunk),
                        self.rows(self.unit, count + at, chunk),
                        jnp.concatenate(
                            [self.line(at + i, 0) for i in range(chunk)], 1
                        ),
                        jnp.concatenate(
                            [self.line(at + i, 1) for i in range(chunk)], 1
                        ),
                        None,
                    )
                )
            parts = pair_grads(pairs, self.scaling)
            for blocks, (query_part, _, _) in zip(places, parts):
                self.dq[blocks] += query_part.reshape(chunk, BLK, width)
            key_part = sum(part[1] for part in parts)
            value_part = sum(part[2] for part in parts)
            self.acc[globals_, 0] += key_part.reshape(GLOB, BLK, width)
            self.acc[globals_, 1] += value_part.reshape(GLOB, BLK, width)
            return carry

        lax.fori_loop(0, count // (chunk * turns), step, 0)

    def scattered(self, guest, me, span, fanout, near):
        who, whom, far = self.lists
        count = self.count

        def note(at, q, owner, block):
            unit = jnp.bitwise_xor(owner, me)
            hit = (unit >= 0) & (unit < span)
            who[at] = q
            whom[at] = unit * count + block
            far[at] = 0.0
            return at + hit.astype(jnp.int32)

        group = count // groups_of(count)

        def gather(g, at):
            first = (guest * count + g * group) * fanout
            codes = [self.layout[first + k] for k in range(group * fanout)]
            for k, code in enumerate(codes):
                owner = lax.shift_right_logical(code, CODE.bit_length() - 1)
                at = note(at, g * group + k // fanout, owner, code & (CODE - 1))
            return at

        found = lax.fori_loop(0, count // group, gather, 0)
        if near:
            found = note(found, 0, guest - 1, count - 1)
            found = note(found, count - 1, guest + 1, 0)
        for k in range(PAIRS - 1):
            who[found + k] = 0
            whom[found + k] = 0
            far[found + k] = FAR

        def step(g, carry):
            places, pairs = ([], [])
            for k in range(PAIRS):
                at = g * PAIRS + k
                places.append((who[at], whom[at]))
                pairs.append(self.pair(who[at], whom[at], 1, far[at]))
            parts = pair_grads(pairs, self.scaling)
            for (q, j), (query_part, key_part, value_part) in zip(places, parts):
                self.dq[q] += query_part
                self.acc[j, 0] += key_part
                self.acc[j, 1] += value_part
            return carry

        lax.fori_loop(0, (found + PAIRS - 1) // PAIRS, step, 0)

    def finish(self, out):
        def step(q, carry):
            out[q] = (self.dq[q] * self.scaling).astype(out.dtype)
            return carry

        lax.fori_loop(0, self.count, step, 0)


def own_kernel(unit, keyval, acc, dq, stat):
    def clear(b, carry):
        acc[b] = jnp.zeros(acc.shape[1:], jnp.float32)
        return carry

    count = dq.shape[0]
    lax.fori_loop(0, count, clear, 0)
    own = Visitor(count, unit, stat, dq, keyval, keyval, acc, values_at=count)
    own.begin()
    own.window()


def visit_kernel(plan, me_ref, layout, *refs):
    offsets, count, span, fanout = plan
    refs = list(refs)
    first = offsets == (0,)
    guests = [refs.pop(0) for _ in offsets]
    me = me_ref[0]
    shards = me_ref[1]
    seat = lax.rem(me, span)
    row = lax.div(me, span)
    side = 1 - 2 * lax.rem(row, 2)
    if first:
        parts = [refs.pop(0) for _ in range(span)]
        acc_own, dq_own = (refs.pop(0), refs.pop(0))
        keys, values = (refs.pop(0), refs.pop(0))
    else:
        keys, values = (refs.pop(0), refs.pop(0))
        refs.pop(0)
    acc = refs.pop(0)
    outs = [refs.pop(0) for _ in offsets]
    sums = outs if first else [refs.pop(0) for _ in offsets]
    stat = refs.pop(0)
    lists = refs
    if first:

        def lay(b, carry):
            for m in range(span):
                there = m * count + b
                if m == 0:
                    acc[there] = acc_own[b]
                    sums[0][b] = dq_own[b]
                else:
                    acc[there] = jnp.zeros(acc.shape[1:], jnp.float32)
                there = pl.ds(pl.multiple_of(there * BLK, BLK), BLK)
                here = pl.ds(pl.multiple_of(b * BLK, BLK), BLK)
                keys[there, :] = parts[m][here, :]
                here = pl.ds(pl.multiple_of((count + b) * BLK, BLK), BLK)
                values[there, :] = parts[m][here, :]
            return carry

        lax.fori_loop(0, count, lay, 0)

    for v, offset in enumerate(offsets):
        guest = me + offset * span * side
        present = (guest >= 0) & (guest < shards)
        visitor = Visitor(count, guests[v], stat, sums[v], keys, values, acc, layout, lists)

        @pl.when(present)
        def _(visitor=visitor, offset=offset, guest=guest, out=outs[v]):
            visitor.begin(offset != 0)
            @pl.when(row == 0)
            def _():
                visitor.anchors(seat * count)

            visitor.scattered(guest, me, span, fanout, offset in (-1, 0, 1))
            visitor.finish(out)


def sum_of(m, which, b, acc, place, scaling, parts, arrived):
    total = acc[place, which]
    if which == 0:
        total = total * scaling
    for part, units in zip(parts, arrived):
        total = total + part[which, units.index(m), b].astype(jnp.float32)
    return total.astype(jnp.bfloat16)


def share_kernel(plan, acc, *refs):
    span, wanted, arrived = plan
    parts, out = (refs[:-1], refs[-1])
    count = acc.shape[0] // span
    scaling = acc.shape[3] ** (-0.5)

    def step(b, carry):
        for k, m in enumerate(wanted):
            place = m * count + b
            for which in range(2):
                out[which, k, b] = sum_of(m, which, b, acc, place, scaling, parts, arrived)
        return carry

    lax.fori_loop(0, count, step, 0)


def finish_kernel(plan, acc, *refs):
    span, arrived = plan
    parts, outs = (refs[: len(arrived)], refs[len(arrived) : len(arrived) + 2])
    held_s, sems = refs[len(arrived) + 2 :]
    count = acc.shape[0] // span
    scaling = acc.shape[3] ** (-0.5)
    groups = groups_of(count)
    group = count // groups
    copies = []
    for g in range(groups):
        for b in range(g * group, (g + 1) * group):
            for which in range(2):
                held_s[which, b * BLK : (b + 1) * BLK, :] = sum_of(
                    0, which, b, acc, b, scaling, parts, arrived
                )
        for which in range(2):
            at = pl.ds(g * group * BLK, group * BLK)
            copies.append(
                pltpu.make_async_copy(
                    held_s.at[which, at], outs[which].at[at], sems.at[which, g]
                )
            )
            copies[-1].start()
    for copy in copies:
        copy.wait()


SMEM = pl.BlockSpec(memory_space=pltpu.SMEM)
VMEM = pl.BlockSpec(memory_space=pltpu.VMEM)


def own_visit(unit, keyval, count):
    width = unit.shape[1]
    stats = pltpu.VMEM((stat_rows(count), width), jnp.float32)
    return pl.pallas_call(
        own_kernel,
        out_shape=(
            jax.ShapeDtypeStruct((count, 2, BLK, width), jnp.float32),
            jax.ShapeDtypeStruct((count, BLK, width), jnp.float32),
        ),
        scratch_shapes=[stats],
        compiler_params=pltpu.CompilerParams(vmem_limit_bytes=LIMIT),
        name="own",
    )(unit, keyval)


def share(acc, span, wanted, arrived, parts):
    held, _, _, width = acc.shape
    return pl.pallas_call(
        functools.partial(share_kernel, (span, wanted, arrived)),
        out_shape=jax.ShapeDtypeStruct((2, len(wanted), held // span, BLK, width), jnp.bfloat16),
        in_specs=[VMEM] * (1 + len(parts)),
        out_specs=VMEM,
        compiler_params=pltpu.CompilerParams(vmem_limit_bytes=LIMIT),
        name="share",
    )(acc, *parts)


def finish(acc, span, arrived, parts):
    held, _, _, width = acc.shape
    count = held // span
    shape = (count * BLK, width)
    hbm = pl.BlockSpec(memory_space=pltpu.HBM)
    return pl.pallas_call(
        functools.partial(finish_kernel, (span, arrived)),
        out_shape=[jax.ShapeDtypeStruct(shape, jnp.bfloat16)] * 2,
        in_specs=[VMEM] * (1 + len(parts)),
        out_specs=[hbm, hbm],
        scratch_shapes=[
            pltpu.VMEM((2,) + shape, jnp.bfloat16),
            pltpu.SemaphoreType.DMA((2, groups_of(count))),
        ],
        compiler_params=pltpu.CompilerParams(vmem_limit_bytes=LIMIT),
        name="finish",
    )(acc, *parts)


def add_kernel(base, *refs):
    parts, out = (refs[:-1], refs[-1])

    def step(b, carry):
        total = base[b]
        for part in parts:
            total = total + part[b].astype(jnp.float32)
        if len(out.shape) == 3:
            out[b] = total
        else:
            out[pl.ds(pl.multiple_of(b * BLK, BLK), BLK), :] = total.astype(out.dtype)
        return carry

    lax.fori_loop(0, base.shape[0], step, 0)


def add(base, parts, final, weight):
    count, _, width = base.shape
    if final:
        out = jax.ShapeDtypeStruct((count * BLK, width), jnp.bfloat16)
    else:
        out = jax.ShapeDtypeStruct(base.shape, jnp.float32)
    return pl.pallas_call(
        add_kernel,
        out_shape=out,
        cost_estimate=pl.CostEstimate(
            flops=weight * count * 10 * BLK * BLK * width, bytes_accessed=0, transcendentals=0
        ),
        compiler_params=pltpu.CompilerParams(vmem_limit_bytes=LIMIT),
        name="add",
    )(base, *parts)


def visit(me, layout, units, offsets, keyvals, acc, query_acc, weight, count, span, fanout):
    first = query_acc is not None
    width = units[0].shape[1]
    held = span * count
    plan = (offsets, count, span, fanout)
    operands = units + keyvals
    keys = jax.ShapeDtypeStruct((held * BLK, width), jnp.bfloat16)
    outs = [jax.ShapeDtypeStruct((held, 2, BLK, width), jnp.float32)]
    if first:
        outs = [keys, keys] + outs
        aliases = {}
        operands = operands + [acc, query_acc]
    else:
        aliases = {len(operands) + 2: 0}
        operands = operands + [placed(acc, pltpu.VMEM)]
    kind = jnp.float32 if first else jnp.bfloat16
    outs += [jax.ShapeDtypeStruct((count, BLK, width), kind)] * len(units)
    entries = count * fanout + 2 + PAIRS
    stats = pltpu.VMEM((stat_rows(count), width), jnp.float32)
    return list(
        pl.pallas_call(
            functools.partial(visit_kernel, plan),
            out_shape=outs,
            in_specs=[SMEM, SMEM] + [VMEM] * len(operands),
            out_specs=[VMEM] * len(outs),
            input_output_aliases=aliases,
            scratch_shapes=[pltpu.VMEM((count, BLK, width), jnp.float32)]
            * (0 if first else len(units))
            + [
                stats,
                pltpu.SMEM((entries,), jnp.int32),
                pltpu.SMEM((entries,), jnp.int32),
                pltpu.SMEM((entries,), jnp.float32),
            ],
            compiler_params=pltpu.CompilerParams(vmem_limit_bytes=LIMIT),
            cost_estimate=pl.CostEstimate(
                flops=weight * count * 10 * BLK * BLK * width,
                bytes_accessed=0,
                transcendentals=len(offsets) * count * BLK * BLK,
            ),
            name="visit",
        )(me, layout, *operands)
    )


def body(query_rows, key_rows, value_rows, output_rows, output_grad, logsumexp, layout):
    shards = lax.axis_size("qb")
    myself = lax.axis_index("qb")
    width = query_rows.shape[1]
    count = query_rows.shape[0] // BLK
    fanout = layout.shape[1]
    span = 4
    while shards // span > 16:
        span = span * 2
    planes = shards // span

    def send(array, pairs):
        return lax.ppermute(array, "qb", pairs)

    def swap(array, bit):
        return send(array, [(i, i ^ bit) for i in range(shards)])

    def hop(s, odd, back=False):
        pairs = []
        for p in range(odd, planes - 1, 2):
            if p >= s - 1:
                pairs.append((p, p + 1))
            if p + 1 <= planes - s:
                pairs.append((p + 1, p))
        if back:
            pairs = [(q, p) for p, q in pairs]
        return [(p * span + e, q * span + e) for p, q in pairs for e in range(span)]

    me = jnp.stack([myself, jnp.int32(shards)]).astype(jnp.int32)
    entries = (layout // count * CODE + layout % count).reshape(-1)
    unit, keyval = pack(
        query_rows, output_grad, output_rows, logsumexp.reshape(count, BLK), key_rows, value_rows
    )

    def merge(one, two):
        return (one.astype(jnp.float32) + two.astype(jnp.float32)).astype(jnp.bfloat16)

    def tie(*arrays):
        return lax.optimization_barrier(arrays)

    last = planes - 1
    odd, even = (send(unit, hop(1, 1)), send(unit, hop(1, 0)))
    keyvals = {0: keyval}
    singles = [m for m in range(1, span) if m & (m - 1) == 0]
    for m in singles:
        keyvals[m] = swap(keyval, m)
    acc, query_acc = own_visit(unit, keyval, count)
    even, query_acc = tie(even, query_acc)
    for m in range(1, span):
        if m & (m - 1):
            keyvals[m] = swap(keyvals[m & (m - 1)], m & -m)
    keyvals = [keyvals[m] for m in range(span)]

    def meet(units, offsets, keyvals, acc, query_acc=None, weight=0):
        return visit(
            me, entries, units, offsets, keyvals, acc, query_acc, weight, count, span, fanout
        )

    keys, values, acc, query_acc = meet([unit], (0,), keyvals, acc, query_acc)
    ends = [(last * span + e, e) for e in range(span)]
    ends = ends + [(two, one) for one, two in ends]
    even_parts, odd_parts = ([], [])
    for s in range(1, last):
        if s + 1 < last:
            next_even, next_odd = (send(odd, hop(s + 1, 0)), send(even, hop(s + 1, 1)))
        else:
            odd, query_acc = tie(odd, query_acc)
            far = send(odd, hop(last, 0))
        if s + 2 == last:
            acc, next_even = tie(acc, next_even)
        acc, even_part, odd_part = meet([even, odd], (s, -s), [keys, values], acc)
        even_parts.append(even_part)
        odd_parts.append(odd_part)
        if s + 1 < last:
            even, odd = (next_even, next_odd)
    acc, far_part = meet([far], (last,), [keys, values], acc, None, COST)

    even_back, odd_back = (even_parts[-1], odd_parts[-1])
    for t in range(last - 1, 1, -1):
        even_back, odd_back = (send(even_back, hop(t, 0, True)), send(odd_back, hop(t, 1, True)))
        if t == 2:
            even_back, odd_back, far_part = tie(even_back, odd_back, far_part)
        even_back, odd_back = (
            merge(even_parts[t - 2], odd_back),
            merge(odd_parts[t - 2], even_back),
        )
    acc, even_back, odd_back = tie(acc, even_back, odd_back)
    backs = [send(even_back, hop(1, 0, True)), send(odd_back, hop(1, 1, True))]
    query_acc = add(query_acc, backs, False, COST)
    query_grad = add(query_acc, [send(far_part, ends)], True, 1)

    wanted = tuple(range(span))
    arrived, parts = ((), ())
    bit = 1
    while bit < span:
        theirs = tuple(m for m in wanted if m & bit)
        wanted = tuple(m for m in wanted if not m & bit)
        sent = share(acc, span, theirs, arrived, parts)
        arrived, parts = (arrived + (wanted,), parts + (swap(sent, bit),))
        bit = bit * 2
    *parts, query_grad = tie(*parts, query_grad)
    key_grad, value_grad = finish(acc, span, arrived, parts)
    return (query_grad, key_grad, value_grad)


def solution(mesh):
    in_specs = (
        P(("grp", "qb"), None),
        P(("grp", "qb"), None),
        P(("grp", "qb"), None),
        P(("grp", "qb"), None),
        P(("grp", "qb"), None),
        P(("grp", "qb")),
        P("grp", None),
    )
    out_specs = (P(("grp", "qb"), None), P(("grp", "qb"), None), P(("grp", "qb"), None))
    return jax.shard_map(body, mesh=mesh, in_specs=in_specs, out_specs=out_specs, check_vma=False)
```

```python
import functools

import jax
import jax.numpy as jnp
from jax import lax
from jax.experimental import pallas as pl
from jax.experimental.pallas import tpu as pltpu
from jax.sharding import PartitionSpec as P

BLK = 128
GLOB = 2
TILE = 16
CODE = 256
PAIRS = 10
TURNS = 6
FAR = 1e30
COST = 20
LIMIT = 16 * 2**20


def pieces(row):
    high = row.astype(jnp.bfloat16).astype(jnp.float32)
    return [high, row - high]


def stat_rows(count):
    return -(-4 * count // TILE) * TILE


def placed(array, space):
    return pltpu.with_memory_space_constraint(array, space)


def groups_of(count):
    return next(groups for groups in (2, 3, 1) if count % groups == 0)


def pack_kernel(
    query, grad, output, lse_hbm, key, value, unit, keyval, output_s, lse, delta_s, stat_s, sems
):
    count, width = lse.shape
    groups = groups_of(count)
    group = count // groups
    ones = jnp.ones((TILE, width), jnp.bfloat16)
    held = count * BLK
    loads = []
    for g in range(groups):
        at = pl.ds(g * group * BLK, group * BLK)
        after = pl.ds(held + g * group * BLK, group * BLK)
        loads.append(
            [
                pltpu.make_async_copy(grad.at[at], unit.at[after], sems.at[0, g]),
                pltpu.make_async_copy(output.at[at], output_s.at[at], sems.at[1, g]),
                pltpu.make_async_copy(query.at[at], unit.at[at], sems.at[2, g]),
            ]
        )
    lines = pltpu.make_async_copy(lse_hbm, lse, sems.at[3, 0])
    lines.start()
    for kind in range(3):
        for load in loads:
            load[kind].start()
    joins = [
        pltpu.make_async_copy(key, keyval.at[pl.ds(0, held)], sems.at[4, 0]),
        pltpu.make_async_copy(value, keyval.at[pl.ds(held, held)], sems.at[5, 0]),
    ]
    for join in joins:
        join.start()

    def total(part):
        return lax.dot_general(
            ones, part, (((1,), (1,)), ((), ())), preferred_element_type=jnp.float32
        )

    for g in range(groups):
        loads[g][0].wait()
        loads[g][1].wait()
        highs, lows = ([], [])
        for k in range(g * group, (g + 1) * group):
            grads = unit[held + k * BLK : held + (k + 1) * BLK, :].astype(jnp.float32)
            product = grads * output_s[k * BLK : (k + 1) * BLK, :].astype(jnp.float32)
            highs.append(product.astype(jnp.bfloat16))
            lows.append((product - highs[-1].astype(jnp.float32)).astype(jnp.bfloat16))
        sums = [total(high) + total(low) for high, low in zip(highs, lows)]
        for k in range(group):
            delta_s[g * group + k : g * group + k + 1, :] = sums[k][0:1]
    lines.wait()
    stat_s[...] = jnp.zeros(stat_s.shape, jnp.float32)
    for k, line in enumerate(pieces(lse[...]) + pieces(delta_s[...])):
        stat_s[k * count : (k + 1) * count, :] = line
    unit[2 * held :, :] = stat_s[...].astype(jnp.bfloat16)
    for load in loads:
        load[2].wait()
    for join in joins:
        join.wait()


def pack(query, grad, output, lse, key, value):
    count, width = lse.shape
    rows = stat_rows(count)
    hbm = pl.BlockSpec(memory_space=pltpu.HBM)
    return pl.pallas_call(
        pack_kernel,
        out_shape=(
            jax.ShapeDtypeStruct((2 * count * BLK + rows, width), jnp.bfloat16),
            jax.ShapeDtypeStruct((2 * count * BLK, width), jnp.bfloat16),
        ),
        in_specs=[hbm] * 6,
        out_specs=[pl.BlockSpec(memory_space=pltpu.VMEM)] * 2,
        scratch_shapes=[
            pltpu.VMEM(query.shape, jnp.bfloat16),
            pltpu.VMEM(lse.shape, jnp.float32),
            pltpu.VMEM(lse.shape, jnp.float32),
            pltpu.VMEM((rows, width), jnp.float32),
            pltpu.SemaphoreType.DMA((6, groups_of(count))),
        ],
        compiler_params=pltpu.CompilerParams(vmem_limit_bytes=LIMIT),
        name="pack",
    )(*[placed(array, pltpu.HBM) for array in (query, grad, output, lse, key, value)])


def pair_grads(pairs, scaling):
    def outer(one, two):
        return lax.dot_general(
            one, two, (((1,), (1,)), ((), ())), preferred_element_type=jnp.float32
        )

    def inner(one, two):
        return jnp.dot(one, two, preferred_element_type=jnp.float32)

    def flipped(one, two):
        return lax.dot_general(
            one, two, (((0,), (0,)), ((), ())), preferred_element_type=jnp.float32
        )

    scores = [outer(keys, queries) for keys, _, queries, _, _, _, _ in pairs]
    dweights = [outer(values, grads) for _, values, _, grads, _, _, _ in pairs]
    probs = []
    for score, (_, _, _, _, lse, _, mask) in zip(scores, pairs):
        prob = jnp.exp(score * scaling - lse)
        probs.append(prob if mask is None else jnp.where(mask, prob, 0.0))
    prob_lows = [prob.astype(jnp.bfloat16) for prob in probs]
    score_lows = [
        (prob * (dweight - pair[5])).astype(jnp.bfloat16)
        for prob, dweight, pair in zip(probs, dweights, pairs)
    ]
    value_parts = [inner(low, pair[3]) for low, pair in zip(prob_lows, pairs)]
    key_parts = [inner(low, pair[2]) for low, pair in zip(score_lows, pairs)]
    query_parts = [flipped(low, pair[0]) for low, pair in zip(score_lows, pairs)]
    return list(zip(query_parts, key_parts, value_parts))


class Visitor:
    def __init__(
        self, count, unit, stat, dq, keys, values, acc, layout=None, lists=None, values_at=0
    ):
        self.count = count
        self.unit, self.stat = (unit, stat)
        self.dq, self.keys, self.values, self.acc = (dq, keys, values, acc)
        self.layout, self.lists, self.values_at = (layout, lists, values_at)
        self.width = unit.shape[1]
        self.scaling = self.width ** (-0.5)

    def begin(self, clear=True):
        count = self.count
        self.stat[...] = self.unit[2 * count * BLK :, :].astype(jnp.float32)

        def step(q, carry):
            self.dq[q] = jnp.zeros(self.dq.shape[1:], jnp.float32)
            return carry

        if clear:
            lax.fori_loop(0, count, step, 0)

    def rows(self, array, block, blocks=1):
        return array[pl.ds(pl.multiple_of(block * BLK, BLK), blocks * BLK), :]

    def line(self, q, kind):
        at = 2 * kind * self.count + q
        return self.stat[pl.ds(at, 1), :] + self.stat[pl.ds(at + self.count, 1), :]

    def pair(self, q, j, keys=1, shift=0.0, mask=None):
        return (
            self.rows(self.keys, j, keys),
            self.rows(self.values, self.values_at + j, keys),
            self.rows(self.unit, q),
            self.rows(self.unit, self.count + q),
            self.line(q, 0) + shift,
            self.line(q, 1),
            mask,
        )

    def window(self):
        count, width = (self.count, self.width)
        chunk = 2 if count % 2 == 0 else 1

        def step(c, carry):
            places, pairs = ([], [])
            for k in range(chunk):
                q = c * chunk + k
                start = jnp.clip(q - 1, 0, count - 3)
                block = lax.broadcasted_iota(jnp.int32, (3 * BLK, BLK), 0) // BLK
                block = block + start - q
                places.append((q, start))
                pairs.append(self.pair(q, start, 3, 0.0, (block >= -1) & (block <= 1)))
            parts = pair_grads(pairs, self.scaling)
            for (q, start), (query_part, key_part, value_part) in zip(places, parts):
                self.dq[q] += query_part
                self.acc[pl.ds(start, 3), 0] += key_part.reshape(3, BLK, width)
                self.acc[pl.ds(start, 3), 1] += value_part.reshape(3, BLK, width)
            return carry

        lax.fori_loop(0, count // chunk, step, 0)

    def anchors(self, base):
        count, width = (self.count, self.width)
        chunk = 2 if count % 2 == 0 else 1
        turns = next(turns for turns in (TURNS, 2, 1) if count % (turns * chunk) == 0)
        globals_ = pl.ds(base, GLOB)

        def step(c, carry):
            places, pairs = ([], [])
            for k in range(turns):
                at = (c * turns + k) * chunk
                places.append(pl.ds(at, chunk))
                pairs.append(
                    (
                        self.rows(self.keys, base, GLOB),
                        self.rows(self.values, base, GLOB),
                        self.rows(self.unit, at, chunk),
                        self.rows(self.unit, count + at, chunk),
                        jnp.concatenate(
                            [self.line(at + i, 0) for i in range(chunk)], 1
                        ),
                        jnp.concatenate(
                            [self.line(at + i, 1) for i in range(chunk)], 1
                        ),
                        None,
                    )
                )
            parts = pair_grads(pairs, self.scaling)
            for blocks, (query_part, _, _) in zip(places, parts):
                self.dq[blocks] += query_part.reshape(chunk, BLK, width)
            key_part = sum(part[1] for part in parts)
            value_part = sum(part[2] for part in parts)
            self.acc[globals_, 0] += key_part.reshape(GLOB, BLK, width)
            self.acc[globals_, 1] += value_part.reshape(GLOB, BLK, width)
            return carry

        lax.fori_loop(0, count // (chunk * turns), step, 0)

    def scattered(self, guest, me, span, fanout, near):
        who, whom, far = self.lists
        count = self.count

        def note(at, q, owner, block):
            unit = jnp.bitwise_xor(owner, me)
            hit = (unit >= 0) & (unit < span)
            who[at] = q
            whom[at] = unit * count + block
            far[at] = 0.0
            return at + hit.astype(jnp.int32)

        group = count // groups_of(count)

        def gather(g, at):
            first = (guest * count + g * group) * fanout
            codes = [self.layout[first + k] for k in range(group * fanout)]
            for k, code in enumerate(codes):
                owner = lax.shift_right_logical(code, CODE.bit_length() - 1)
                at = note(at, g * group + k // fanout, owner, code & (CODE - 1))
            return at

        found = lax.fori_loop(0, count // group, gather, 0)
        if near:
            found = note(found, 0, guest - 1, count - 1)
            found = note(found, count - 1, guest + 1, 0)
        for k in range(PAIRS - 1):
            who[found + k] = 0
            whom[found + k] = 0
            far[found + k] = FAR

        def step(g, carry):
            places, pairs = ([], [])
            for k in range(PAIRS):
                at = g * PAIRS + k
                places.append((who[at], whom[at]))
                pairs.append(self.pair(who[at], whom[at], 1, far[at]))
            parts = pair_grads(pairs, self.scaling)
            for (q, j), (query_part, key_part, value_part) in zip(places, parts):
                self.dq[q] += query_part
                self.acc[j, 0] += key_part
                self.acc[j, 1] += value_part
            return carry

        lax.fori_loop(0, (found + PAIRS - 1) // PAIRS, step, 0)

    def finish(self, out):
        def step(q, carry):
            out[q] = (self.dq[q] * self.scaling).astype(out.dtype)
            return carry

        lax.fori_loop(0, self.count, step, 0)


def own_kernel(unit, keyval, acc, dq, stat):
    def clear(b, carry):
        acc[b] = jnp.zeros(acc.shape[1:], jnp.float32)
        return carry

    count = dq.shape[0]
    lax.fori_loop(0, count, clear, 0)
    own = Visitor(count, unit, stat, dq, keyval, keyval, acc, values_at=count)
    own.begin()
    own.window()


def visit_kernel(plan, me_ref, layout, *refs):
    offsets, count, span, fanout = plan
    refs = list(refs)
    first = offsets == (0,)
    guests = [refs.pop(0) for _ in offsets]
    me = me_ref[0]
    shards = me_ref[1]
    seat = lax.rem(me, span)
    row = lax.div(me, span)
    side = 1 - 2 * lax.rem(row, 2)
    if first:
        parts = [refs.pop(0) for _ in range(span)]
        acc_own, dq_own = (refs.pop(0), refs.pop(0))
        keys, values = (refs.pop(0), refs.pop(0))
    else:
        keys, values = (refs.pop(0), refs.pop(0))
        refs.pop(0)
    acc = refs.pop(0)
    outs = [refs.pop(0) for _ in offsets]
    sums = outs if first else [refs.pop(0) for _ in offsets]
    stat = refs.pop(0)
    lists = refs
    if first:

        def lay(b, carry):
            for m in range(span):
                there = m * count + b
                if m == 0:
                    acc[there] = acc_own[b]
                    sums[0][b] = dq_own[b]
                else:
                    acc[there] = jnp.zeros(acc.shape[1:], jnp.float32)
                there = pl.ds(pl.multiple_of(there * BLK, BLK), BLK)
                here = pl.ds(pl.multiple_of(b * BLK, BLK), BLK)
                keys[there, :] = parts[m][here, :]
                here = pl.ds(pl.multiple_of((count + b) * BLK, BLK), BLK)
                values[there, :] = parts[m][here, :]
            return carry

        lax.fori_loop(0, count, lay, 0)

    for v, offset in enumerate(offsets):
        guest = me + offset * span * side
        present = (guest >= 0) & (guest < shards)
        visitor = Visitor(count, guests[v], stat, sums[v], keys, values, acc, layout, lists)

        @pl.when(present)
        def _(visitor=visitor, offset=offset, guest=guest, out=outs[v]):
            visitor.begin(offset != 0)
            @pl.when(row == 0)
            def _():
                visitor.anchors(seat * count)

            visitor.scattered(guest, me, span, fanout, offset in (-1, 0, 1))
            visitor.finish(out)


def sum_of(m, which, b, acc, place, scaling, parts, arrived):
    total = acc[place, which]
    if which == 0:
        total = total * scaling
    for part, units in zip(parts, arrived):
        total = total + part[which, units.index(m), b].astype(jnp.float32)
    return total.astype(jnp.bfloat16)


def share_kernel(plan, acc, *refs):
    span, wanted, arrived = plan
    parts, out = (refs[:-1], refs[-1])
    count = acc.shape[0] // span
    scaling = acc.shape[3] ** (-0.5)

    def step(b, carry):
        for k, m in enumerate(wanted):
            place = m * count + b
            for which in range(2):
                out[which, k, b] = sum_of(m, which, b, acc, place, scaling, parts, arrived)
        return carry

    lax.fori_loop(0, count, step, 0)


def finish_kernel(plan, acc, *refs):
    span, arrived = plan
    parts, outs = (refs[: len(arrived)], refs[len(arrived) : len(arrived) + 2])
    held_s, sems = refs[len(arrived) + 2 :]
    count = acc.shape[0] // span
    scaling = acc.shape[3] ** (-0.5)
    groups = groups_of(count)
    group = count // groups
    copies = []
    for g in range(groups):
        for b in range(g * group, (g + 1) * group):
            for which in range(2):
                held_s[which, b * BLK : (b + 1) * BLK, :] = sum_of(
                    0, which, b, acc, b, scaling, parts, arrived
                )
        for which in range(2):
            at = pl.ds(g * group * BLK, group * BLK)
            copies.append(
                pltpu.make_async_copy(
                    held_s.at[which, at], outs[which].at[at], sems.at[which, g]
                )
            )
            copies[-1].start()
    for copy in copies:
        copy.wait()


SMEM = pl.BlockSpec(memory_space=pltpu.SMEM)
VMEM = pl.BlockSpec(memory_space=pltpu.VMEM)


def own_visit(unit, keyval, count):
    width = unit.shape[1]
    stats = pltpu.VMEM((stat_rows(count), width), jnp.float32)
    return pl.pallas_call(
        own_kernel,
        out_shape=(
            jax.ShapeDtypeStruct((count, 2, BLK, width), jnp.float32),
            jax.ShapeDtypeStruct((count, BLK, width), jnp.float32),
        ),
        scratch_shapes=[stats],
        compiler_params=pltpu.CompilerParams(vmem_limit_bytes=LIMIT),
        name="own",
    )(unit, keyval)


def share(acc, span, wanted, arrived, parts):
    held, _, _, width = acc.shape
    return pl.pallas_call(
        functools.partial(share_kernel, (span, wanted, arrived)),
        out_shape=jax.ShapeDtypeStruct((2, len(wanted), held // span, BLK, width), jnp.bfloat16),
        in_specs=[VMEM] * (1 + len(parts)),
        out_specs=VMEM,
        compiler_params=pltpu.CompilerParams(vmem_limit_bytes=LIMIT),
        name="share",
    )(acc, *parts)


def finish(acc, span, arrived, parts):
    held, _, _, width = acc.shape
    count = held // span
    shape = (count * BLK, width)
    hbm = pl.BlockSpec(memory_space=pltpu.HBM)
    return pl.pallas_call(
        functools.partial(finish_kernel, (span, arrived)),
        out_shape=[jax.ShapeDtypeStruct(shape, jnp.bfloat16)] * 2,
        in_specs=[VMEM] * (1 + len(parts)),
        out_specs=[hbm, hbm],
        scratch_shapes=[
            pltpu.VMEM((2,) + shape, jnp.bfloat16),
            pltpu.SemaphoreType.DMA((2, groups_of(count))),
        ],
        compiler_params=pltpu.CompilerParams(vmem_limit_bytes=LIMIT),
        name="finish",
    )(acc, *parts)


def add_kernel(base, *refs):
    parts, out = (refs[:-1], refs[-1])

    def step(b, carry):
        total = base[b]
        for part in parts:
            total = total + part[b].astype(jnp.float32)
        if len(out.shape) == 3:
            out[b] = total
        else:
            out[pl.ds(pl.multiple_of(b * BLK, BLK), BLK), :] = total.astype(out.dtype)
        return carry

    lax.fori_loop(0, base.shape[0], step, 0)


def add(base, parts, final, weight):
    count, _, width = base.shape
    if final:
        out = jax.ShapeDtypeStruct((count * BLK, width), jnp.bfloat16)
    else:
        out = jax.ShapeDtypeStruct(base.shape, jnp.float32)
    return pl.pallas_call(
        add_kernel,
        out_shape=out,
        cost_estimate=pl.CostEstimate(
            flops=weight * count * 10 * BLK * BLK * width, bytes_accessed=0, transcendentals=0
        ),
        compiler_params=pltpu.CompilerParams(vmem_limit_bytes=LIMIT),
        name="add",
    )(base, *parts)


def visit(me, layout, units, offsets, keyvals, acc, query_acc, weight, count, span, fanout):
    first = query_acc is not None
    width = units[0].shape[1]
    held = span * count
    plan = (offsets, count, span, fanout)
    operands = units + keyvals
    keys = jax.ShapeDtypeStruct((held * BLK, width), jnp.bfloat16)
    outs = [jax.ShapeDtypeStruct((held, 2, BLK, width), jnp.float32)]
    if first:
        outs = [keys, keys] + outs
        aliases = {}
        operands = operands + [acc, query_acc]
    else:
        aliases = {len(operands) + 2: 0}
        operands = operands + [placed(acc, pltpu.VMEM)]
    kind = jnp.float32 if first else jnp.bfloat16
    outs += [jax.ShapeDtypeStruct((count, BLK, width), kind)] * len(units)
    entries = count * fanout + 2 + PAIRS
    stats = pltpu.VMEM((stat_rows(count), width), jnp.float32)
    return list(
        pl.pallas_call(
            functools.partial(visit_kernel, plan),
            out_shape=outs,
            in_specs=[SMEM, SMEM] + [VMEM] * len(operands),
            out_specs=[VMEM] * len(outs),
            input_output_aliases=aliases,
            scratch_shapes=[pltpu.VMEM((count, BLK, width), jnp.float32)]
            * (0 if first else len(units))
            + [
                stats,
                pltpu.SMEM((entries,), jnp.int32),
                pltpu.SMEM((entries,), jnp.int32),
                pltpu.SMEM((entries,), jnp.float32),
            ],
            compiler_params=pltpu.CompilerParams(vmem_limit_bytes=LIMIT),
            cost_estimate=pl.CostEstimate(
                flops=weight * count * 10 * BLK * BLK * width,
                bytes_accessed=0,
                transcendentals=len(offsets) * count * BLK * BLK,
            ),
            name="visit",
        )(me, layout, *operands)
    )


def body(query_rows, key_rows, value_rows, output_rows, output_grad, logsumexp, layout):
    shards = lax.axis_size("qb")
    myself = lax.axis_index("qb")
    width = query_rows.shape[1]
    count = query_rows.shape[0] // BLK
    fanout = layout.shape[1]
    span = 4
    while shards // span > 16:
        span = span * 2
    planes = shards // span

    def send(array, pairs):
        return lax.ppermute(array, "qb", pairs)

    def swap(array, bit):
        return send(array, [(i, i ^ bit) for i in range(shards)])

    def hop(s, odd, back=False):
        pairs = []
        for p in range(odd, planes - 1, 2):
            if p >= s - 1:
                pairs.append((p, p + 1))
            if p + 1 <= planes - s:
                pairs.append((p + 1, p))
        if back:
            pairs = [(q, p) for p, q in pairs]
        return [(p * span + e, q * span + e) for p, q in pairs for e in range(span)]

    me = jnp.stack([myself, jnp.int32(shards)]).astype(jnp.int32)
    entries = (layout // count * CODE + layout % count).reshape(-1)
    unit, keyval = pack(
        query_rows, output_grad, output_rows, logsumexp.reshape(count, BLK), key_rows, value_rows
    )

    def merge(one, two):
        return (one.astype(jnp.float32) + two.astype(jnp.float32)).astype(jnp.bfloat16)

    def tie(*arrays):
        return lax.optimization_barrier(arrays)

    last = planes - 1
    odd, even = (send(unit, hop(1, 1)), send(unit, hop(1, 0)))
    keyvals = {0: keyval}
    singles = [m for m in range(1, span) if m & (m - 1) == 0]
    for m in singles:
        keyvals[m] = swap(keyval, m)
    acc, query_acc = own_visit(unit, keyval, count)
    even, query_acc = tie(even, query_acc)
    for m in range(1, span):
        if m & (m - 1):
            keyvals[m] = swap(keyvals[m & (m - 1)], m & -m)
    keyvals = [keyvals[m] for m in range(span)]

    def meet(units, offsets, keyvals, acc, query_acc=None, weight=0):
        return visit(
            me, entries, units, offsets, keyvals, acc, query_acc, weight, count, span, fanout
        )

    keys, values, acc, query_acc = meet([unit], (0,), keyvals, acc, query_acc)
    ends = [(last * span + e, e) for e in range(span)]
    ends = ends + [(two, one) for one, two in ends]
    even_parts, odd_parts = ([], [])
    for s in range(1, last):
        if s + 1 < last:
            next_even, next_odd = (send(odd, hop(s + 1, 0)), send(even, hop(s + 1, 1)))
        else:
            odd, query_acc = tie(odd, query_acc)
            far = send(odd, hop(last, 0))
        if s + 2 == last:
            acc, next_even = tie(acc, next_even)
        acc, even_part, odd_part = meet([even, odd], (s, -s), [keys, values], acc)
        even_parts.append(even_part)
        odd_parts.append(odd_part)
        if s + 1 < last:
            even, odd = (next_even, next_odd)
    acc, far_part = meet([far], (last,), [keys, values], acc, None, COST)

    even_back, odd_back = (even_parts[-1], odd_parts[-1])
    for t in range(last - 1, 1, -1):
        even_back, odd_back = (send(even_back, hop(t, 0, True)), send(odd_back, hop(t, 1, True)))
        if t == 2:
            even_back, odd_back, far_part = tie(even_back, odd_back, far_part)
        even_back, odd_back = (
            merge(even_parts[t - 2], odd_back),
            merge(odd_parts[t - 2], even_back),
        )
    acc, even_back, odd_back = tie(acc, even_back, odd_back)
    backs = [send(even_back, hop(1, 0, True)), send(odd_back, hop(1, 1, True))]
    query_acc = add(query_acc, backs, False, COST)
    query_grad = add(query_acc, [send(far_part, ends)], True, 1)

    wanted = tuple(range(span))
    arrived, parts = ((), ())
    bit = 1
    while bit < span:
        theirs = tuple(m for m in wanted if m & bit)
        wanted = tuple(m for m in wanted if not m & bit)
        sent = share(acc, span, theirs, arrived, parts)
        arrived, parts = (arrived + (wanted,), parts + (swap(sent, bit),))
        bit = bit * 2
    *parts, query_grad = tie(*parts, query_grad)
    key_grad, value_grad = finish(acc, span, arrived, parts)
    return (query_grad, key_grad, value_grad)


def solution(mesh):
    in_specs = (
        P(("grp", "qb"), None),
        P(("grp", "qb"), None),
        P(("grp", "qb"), None),
        P(("grp", "qb"), None),
        P(("grp", "qb"), None),
        P(("grp", "qb")),
        P("grp", None),
    )
    out_specs = (P(("grp", "qb"), None), P(("grp", "qb"), None), P(("grp", "qb"), None))
    return jax.shard_map(body, mesh=mesh, in_specs=in_specs, out_specs=out_specs, check_vma=False)
```
